32 devices in a mesh: blk: 8 (over y, x, core), head: 4 (over z).
Axes of the slice: x: 2, y: 2, z: 4, core: 2. Of those that a mesh axis runs over, the one named last changes fastest.
Arguments:
- tokens: bfloat16 [2048, 2048], P('blk'), may hold values from -6 to 6
- gain_attn: bfloat16 [2048], replicated, may hold values from 0.25 to 1.75
- w_query: bfloat16 [2048, 256], P(None, 'head'), may hold values from -0.125 to 0.125
- w_key: bfloat16 [2048, 256], P(None, 'head'), may hold values from -0.125 to 0.125
- w_value: bfloat16 [2048, 2048], P(None, 'head'), may hold values from -0.125 to 0.125
- w_out: bfloat16 [2048, 2048], P('head'), may hold values from -1.5 to 1.5
- gain_mlp: bfloat16 [2048], replicated, may hold values from 0.25 to 1.75
- w_gate: bfloat16 [2048, 5504], P(None, 'head'), may hold values from -0.125 to 0.125
- w_up: bfloat16 [2048, 5504], P(None, 'head'), may hold values from -0.125 to 0.125
- w_down: bfloat16 [5504, 2048], P('head'), may hold values from -0.078125 to 0.078125
- doc_lengths: int32 [4], replicated, may hold values from 1 to 1920, 1984 in all
- cotangent: bfloat16 [2048, 2048], P('blk'), may hold values from -6 to 6
Outputs:
- output: bfloat16 [2048, 2048], P('blk')
- input_grad: float32 [2048, 2048], P('blk')
- gain_attn_grad: float32 [2048], replicated
- query_weight_grad: float32 [2048, 256], P(None, 'head')
- key_weight_grad: float32 [2048, 256], P(None, 'head')
- value_weight_grad: float32 [2048, 2048], P(None, 'head')
- out_weight_grad: float32 [2048, 2048], P('head')
- gain_mlp_grad: float32 [2048], replicated
- gate_weight_grad: float32 [2048, 5504], P(None, 'head')
- up_weight_grad: float32 [2048, 5504], P(None, 'head')
- down_weight_grad: float32 [5504, 2048], P('head')
The draws below stay inside these ranges and needn't reach their ends.
Inputs may be any that keep to these rules, and one draw needn't show every extreme that they name: `doc_lengths`: the lengths are positive and sum to 1984; the documents lie end to end from position 0, the last 64 positions are padding, and the longest document has exactly 1920 tokens.
All inputs are finite; a program needn't handle non-finite values.
Results may differ from the reference program's by a relative error of at most 0.015.
Values sent between devices are 32-bit elements; how exact they have to be, the bound alone decides.
No kernel may reach another device: no remote copies, remote signals or barrier semaphores. Data moves between devices by JAX's collectives and lax.ppermute only.
A program may use at most 256 MiB of HBM per device.

```python
import math
import jax
import jax.numpy as jnp
import numpy as np
from jax import lax

D = 2048
HEADS = 16
FEAT = 16
FMAP = 273
VW = 2048
DV = 128
FF = 5504
TOK_DEV = 256
DOCS = 4
TOKENS = 2048
FILLED = 1984
LONG = 1920


def block_scale(key, shape, split, low, high):
    def one(dim, shards_of):
        steps = jax.random.uniform(jax.random.fold_in(jax.random.fold_in(key, 6), dim), (shards_of,), jnp.float32, low / len(split), high / len(split))
        return jnp.repeat(jnp.exp(steps), shape[dim] // shards_of).reshape((-1,) + (1,) * (len(shape) - dim - 1))

    level = one(*split[0])
    for cut in split[1:]:
        level = level * one(*cut)
    return level


def length_profile(number_of, total, limit, skew):
    weights = [(1 << 20) // math.isqrt(grade ** skew) + 1 for grade in range(2, number_of + 1)]
    rest, given = total - limit - (number_of - 1), [1] * (number_of - 1)
    while rest > 0:
        free = [i for i in range(number_of - 1) if given[i] < limit]
        pool, left = sum([weights[i] for i in free]), rest
        for i in free:
            addition = min(limit - given[i], max(1, left * weights[i] // pool), rest)
            given[i] = given[i] + addition
            rest = rest - addition
    return np.array([limit] + given)


def uneven(key, count, total, bound, skew):
    if count == 2:
        one = jax.random.randint(key, (), max(1, total - bound), min(bound, total - 1) + 1)
        return jnp.stack([one, total - one])
    lengths = jnp.asarray(length_profile(count, total, bound, skew), jnp.int32)
    twos = (count - 1) // 2
    source_of, receiver = lengths[1:1 + 2 * twos:2], lengths[2:2 + 2 * twos:2]
    room = jnp.minimum(source_of - 1, bound - receiver)
    passed = jax.random.randint(jax.random.fold_in(key, 1), (twos,), 0, 1 << 20) % (room + 1)
    lengths = lengths.at[1:1 + 2 * twos:2].set(source_of - passed).at[2:2 + 2 * twos:2].set(receiver + passed)
    return lengths[jax.random.permutation(jax.random.fold_in(key, 2), count)]


def noise(own_key, dims, deviation, reach, split=(), kind=jnp.bfloat16):
    drawn = deviation * jax.random.normal(own_key, dims, jnp.float32)
    if split:
        drawn = drawn * block_scale(own_key, dims, split, -0.22, 0.18)
    return jnp.clip(drawn, -reach, reach).astype(kind)


def setup_inputs(seed: int = 0) -> dict:
    arg_keys = jax.random.split(jax.random.key(seed), 13)
    tokens = noise(arg_keys[0], (TOKENS, D), 1.0, 6.0, ((0, 8),))
    gain_attn = jnp.clip(1.0 + 0.15 * jax.random.normal(arg_keys[1], (D,), jnp.float32), 0.25, 1.75).astype(jnp.bfloat16)
    w_query = noise(arg_keys[2], (D, HEADS * FEAT), D ** -0.5, 0.125, ((1, 4),))
    w_key = noise(arg_keys[3], (D, HEADS * FEAT), D ** -0.5, 0.125, ((1, 4),))
    w_value = noise(arg_keys[4], (D, VW), D ** -0.5, 0.125, ((1, 4),))
    w_out = noise(arg_keys[5], (VW, D), 16 ** -0.5, 1.5, ((0, 4),))
    gain_mlp = jnp.clip(1.0 + 0.15 * jax.random.normal(arg_keys[6], (D,), jnp.float32), 0.25, 1.75).astype(jnp.bfloat16)
    w_gate = noise(arg_keys[7], (D, FF), D ** -0.5, 0.125, ((1, 4),))
    w_up = noise(arg_keys[8], (D, FF), D ** -0.5, 0.125, ((1, 4),))
    w_down = noise(arg_keys[9], (FF, D), FF ** -0.5, 0.078125, ((0, 4),))
    doc_lengths = uneven(arg_keys[10], DOCS, FILLED, LONG, 2).astype(jnp.int32)
    cotangent = noise(arg_keys[11], (TOKENS, D), 1.0, 6.0, ((0, 8),))
    return dict(tokens=tokens, gain_attn=gain_attn, w_query=w_query, w_key=w_key, w_value=w_value, w_out=w_out, gain_mlp=gain_mlp, w_gate=w_gate, w_up=w_up, w_down=w_down, doc_lengths=doc_lengths, cotangent=cotangent)


epsilon = 1e-05
highest = lax.Precision.HIGHEST
quad_scale = 1.0 / (4.0 * math.sqrt(2.0))

@jax.custom_vjp
def low(v):
    return lax.optimization_barrier(v.astype(jnp.bfloat16)).astype(jnp.float32)

@jax.custom_vjp
def low_back(v):
    return v

def low_keep(v):
    return (low(v), None)

def low_pass(kept, grad):
    return (grad,)

def back_keep(v):
    return (v, None)

def back_low(kept, grad):
    return (low(grad),)
low.defvjp(low_keep, low_pass)
low_back.defvjp(back_keep, back_low)

def feature_map(vectors):
    width = vectors.shape[-1]
    outer = (vectors[..., :, None] * vectors[..., None, :]).reshape(vectors.shape[:-1] + (width * width,))
    ones_col = jnp.ones(vectors.shape[:-1] + (1,), vectors.dtype)
    return jnp.concatenate([ones_col, 0.5 * vectors, quad_scale * outer], axis=-1)

def normalize(values, gain):
    return values * lax.rsqrt(lax.optimization_barrier(jnp.mean(values * values, axis=-1, keepdims=True)) + epsilon) * gain

def doc_layout(doc_lengths, row_count):
    ends = jnp.cumsum(doc_lengths).astype(jnp.int32)
    positions = jnp.arange(row_count, dtype=jnp.int32)
    doc_ids = lax.optimization_barrier(jnp.sum((positions[:, None] >= ends[None, :-1]).astype(jnp.int32), axis=1)).astype(jnp.int32)
    return (doc_ids, positions < ends[-1])

def attend_block(carry, pieces):
    carry_state, carry_total, prev_doc = carry
    query_block, key_block, value_block, block_docs, block_valid = pieces
    block_rows = block_docs.shape[0]
    positions = jnp.arange(block_rows, dtype=jnp.int32)
    allowed = (block_docs[:, None] == block_docs[None, :]) & (positions[:, None] >= positions[None, :])
    raw_scores = jnp.einsum('thf,shf->hts', query_block, key_block, precision=highest)
    scores = low(low_back(jnp.where(allowed[None], raw_scores, 0.0)))
    carried = (block_docs == prev_doc).astype(query_block.dtype)
    numerator = jnp.einsum('hts,shd->thd', scores, value_block, precision=highest)
    numerator = numerator + carried[:, None, None] * jnp.einsum('thf,hfd->thd', query_block, carry_state, precision=highest)
    denominator = lax.optimization_barrier(jnp.sum(scores, axis=-1)).T + carried[:, None] * jnp.einsum('thf,hf->th', query_block, carry_total, precision=highest)
    result = low_back(numerator) / denominator[:, :, None] * block_valid[:, None, None]
    last_doc = block_docs[block_rows - 1]
    keep_rows = (block_docs == last_doc).astype(query_block.dtype)
    same_doc = (last_doc == prev_doc).astype(query_block.dtype)
    kept_keys = key_block * keep_rows[:, None, None]
    new_state = same_doc * carry_state + jnp.einsum('shf,shd->hfd', kept_keys, value_block, precision=highest)
    new_total = same_doc * carry_total + lax.optimization_barrier(jnp.sum(kept_keys, axis=0))
    return ((new_state, new_total, last_doc), result)

def layer(token_wide, gain_one, query_w, key_w, value_w, out_w, gain_two, gate_w, up_w, down_w, doc_ids, valid_rows):
    row_count = token_wide.shape[0]
    normed_in = low(normalize(token_wide, gain_one))
    query = low_back(jnp.dot(normed_in, query_w, precision=highest)).reshape(row_count, HEADS, FEAT)
    key = low_back(jnp.dot(normed_in, key_w, precision=highest)).reshape(row_count, HEADS, FEAT)
    value = low(low_back(jnp.dot(normed_in, value_w, precision=highest))).reshape(row_count, HEADS, DV)
    query_feat = low(feature_map(query))
    key_feat = low(feature_map(key)) * valid_rows[:, None, None]
    blocks = row_count // TOK_DEV
    pieces = (query_feat.reshape(blocks, TOK_DEV, HEADS, FMAP), key_feat.reshape(blocks, TOK_DEV, HEADS, FMAP), value.reshape(blocks, TOK_DEV, HEADS, DV), doc_ids.reshape(blocks, TOK_DEV), valid_rows.reshape(blocks, TOK_DEV))
    start = (jnp.zeros((HEADS, FMAP, DV), jnp.float32), jnp.zeros((HEADS, FMAP), jnp.float32), jnp.array(-1, jnp.int32))
    unused, attended = lax.scan(jax.checkpoint(attend_block), start, pieces)
    attended = low(attended.reshape(row_count, HEADS * DV))
    resid_mid = token_wide + low_back(jnp.dot(attended, out_w, precision=highest))
    normed_mid = low(normalize(resid_mid, gain_two))
    gate = low_back(jnp.dot(normed_mid, gate_w, precision=highest))
    up_lin = low_back(jnp.dot(normed_mid, up_w, precision=highest))
    hidden = low(jax.nn.silu(gate) * up_lin)
    return resid_mid + low_back(jnp.dot(hidden, down_w, precision=highest))

def reference(tokens, gain_attn, w_query, w_key, w_value, w_out, gain_mlp, w_gate, w_up, w_down, doc_lengths, cotangent):
    doc_ids, valid_mask = doc_layout(doc_lengths, tokens.shape[0])
    valid_rows = valid_mask.astype(jnp.float32)

    def layer_of(*weights):
        return layer(*weights, doc_ids, valid_rows)
    inputs = [item.astype(jnp.float32) for item in (tokens, gain_attn, w_query, w_key, w_value, w_out, gain_mlp, w_gate, w_up, w_down)]
    result, pullback = jax.vjp(layer_of, *inputs)
    gradients = pullback(cotangent.astype(jnp.float32))
    return (result.astype(jnp.bfloat16), gradients[0], gradients[1], gradients[2], gradients[3], gradients[4], gradients[5], gradients[6], gradients[7], gradients[8], gradients[9])
```

```python
import functools

import jax
import jax.numpy as jnp
from jax import lax
from jax.experimental import pallas as pl
from jax.experimental.pallas import tpu as pltpu
from jax.sharding import PartitionSpec as P

FEAT = 16
DV = 128

epsilon = 1e-05
f32, bf16 = jnp.float32, jnp.bfloat16
VMEM_LIMIT = 56 * 1024 * 1024


def hop(value, axis, bit):
    count = lax.axis_size(axis)
    return lax.ppermute(value, axis, [(i, i ^ bit) for i in range(count)])


def gather_blk(value):
    count = lax.axis_size("blk")
    if count != 8:
        slots, bit = [value], 1
        while bit < count:
            slots = slots + [hop(slot, "blk", bit) for slot in slots]
            bit *= 2
        return slots
    half = value.shape[0] // 16 * 8
    from_x, from_y = hop(value, "blk", 2), hop(value, "blk", 4)
    far_low, far_high = hop(from_x[:half], "blk", 4), hop(from_y[half:], "blk", 2)
    own_pair, x_pair, y_pair = (hop(part, "blk", 1) for part in (value, from_x, from_y))
    far = jnp.concatenate([far_low, far_high])
    far_pair = jnp.concatenate([hop(far_low, "blk", 1), hop(far_high, "blk", 1)])
    return [value, own_pair, from_x, x_pair, from_y, y_pair, far, far_pair]


def fold(value, bit):
    low, high = jnp.split(value, 2)
    upper = (lax.axis_index("blk") & bit) != 0
    return jnp.where(upper, high, low) + hop(jnp.where(upper, low, high), "blk", bit)


def unfold(value, bit):
    other = hop(value, "blk", bit)
    upper = (lax.axis_index("blk") & bit) != 0
    return jnp.concatenate([jnp.where(upper, other, value), jnp.where(upper, value, other)])


def sum_blk(value):
    if lax.axis_size("blk") != 8:
        return lax.psum(value, "blk")
    one, two = jnp.split(fold(value, 1), 2)
    one, two = fold(one, 2), fold(two, 4)
    one, two = fold(one, 4), fold(two, 2)
    one, two = unfold(one, 4), unfold(two, 2)
    one, two = unfold(one, 2), unfold(two, 4)
    return unfold(jnp.concatenate([one, two]), 1)


def sum_head(value):
    return lax.psum(value, "head")


def dot_t(left, right):
    return lax.dot_general(left, right, (((1,), (1,)), ((), ())), preferred_element_type=f32)


def dot_n(left, right):
    return lax.dot_general(left, right, (((1,), (0,)), ((), ())), preferred_element_type=f32)


def two_parts(value):
    high = value.astype(bf16)
    return high, (value - high.astype(f32)).astype(bf16)


def quarter_dot(left, right):
    total = dot_t(left[0], right[0]) + (dot_t(left[0], right[1]) + dot_t(left[1], right[0]))
    return 0.25 * total


def head_lanes(rows, width, head):
    lanes = lax.broadcasted_iota(jnp.int32, (rows, width), 1)
    return (lanes >= head * FEAT) & (lanes < (head + 1) * FEAT)


def attend_kernel(heads, slots, col_ref, row_ref, *refs):
    slot_refs, (att_ref, mean_ref, inverse_ref) = refs[:slots], refs[slots:]
    rows = col_ref.shape[0]
    qk = heads * FEAT
    own_pos, own_doc = col_ref[:, 0:1], col_ref[:, 1:2]
    valid = col_ref[:, 2:3].astype(f32)
    query = slot_refs[0][:, :qk]
    numer = [jnp.zeros((rows, DV), f32) for _ in range(heads)]
    denom = [jnp.zeros((rows, 1), f32) for _ in range(heads)]
    queries = [
        two_parts(jnp.where(head_lanes(rows, qk, head), query, 0.0)) for head in range(heads)
    ]
    for slot in range(slots):
        allowed = (row_ref[slot : slot + 1, :] <= own_pos) & (
            row_ref[slots + slot : slots + slot + 1, :] == own_doc
        )
        keys = two_parts(slot_refs[slot][:, qk : 2 * qk])
        for head in range(heads):
            near = quarter_dot(queries[head], keys)
            score = jnp.where(allowed, 1.0 + near + 0.5 * near * near, 0.0).astype(bf16)
            first = 2 * qk + head * DV
            value = slot_refs[slot][:, first : first + DV].astype(bf16)
            numer[head] = numer[head] + dot_n(score, value)
            denom[head] = denom[head] + jnp.sum(score.astype(f32), axis=1, keepdims=True)
    for head in range(heads):
        span = slice(head * DV, (head + 1) * DV)
        mean = numer[head] / denom[head]
        att_ref[:, span] = (valid * mean).astype(bf16)
        mean_ref[:, span] = mean
        inverse_ref[:, span] = jnp.broadcast_to(valid / denom[head], (rows, DV))


def query_kernel(heads, slots, col_ref, row_ref, numer_ref, denom_ref, *refs):
    slot_refs, out_ref = refs[:slots], refs[slots]
    rows = col_ref.shape[0]
    qk = heads * FEAT
    own_pos, own_doc = col_ref[:, 0:1], col_ref[:, 1:2]
    query = slot_refs[0][:, :qk]
    queries = [
        two_parts(jnp.where(head_lanes(rows, qk, head), query, 0.0)) for head in range(heads)
    ]
    sums = [jnp.zeros((rows, qk), f32) for _ in range(heads)]
    for slot in range(slots):
        allowed = (row_ref[slot : slot + 1, :] <= own_pos) & (
            row_ref[slots + slot : slots + slot + 1, :] == own_doc
        )
        keys = two_parts(slot_refs[slot][:, qk : 2 * qk])
        for head in range(heads):
            near = quarter_dot(queries[head], keys)
            first = 2 * qk + head * DV
            value = slot_refs[slot][:, first : first + DV].astype(bf16)
            grad = dot_t(numer_ref[:, head * DV : (head + 1) * DV].astype(bf16), value)
            grad = grad + denom_ref[:, head * DV : head * DV + 1]
            grad = jnp.where(allowed, grad * (1.0 + near), 0.0).astype(bf16)
            sums[head] = sums[head] + dot_n(grad, keys[0])
    total = jnp.zeros((rows, qk), f32)
    for head in range(heads):
        total = jnp.where(head_lanes(rows, qk, head), 0.25 * sums[head], total)
    out_ref[...] = total.astype(bf16)


def key_kernel(heads, slots, col_ref, row_ref, *refs):
    slot_refs, grad_refs, out_ref = refs[:slots], refs[slots : 2 * slots], refs[2 * slots]
    rows = col_ref.shape[0]
    qk = heads * FEAT
    own_pos, own_doc = col_ref[:, 0:1], col_ref[:, 3:4]
    own = slot_refs[0]
    key = own[:, qk : 2 * qk]
    keys = [two_parts(jnp.where(head_lanes(rows, qk, head), key, 0.0)) for head in range(heads)]
    values = [
        own[:, 2 * qk + head * DV : 2 * qk + (head + 1) * DV].astype(bf16) for head in range(heads)
    ]
    key_sums = [jnp.zeros((rows, qk), f32) for _ in range(heads)]
    value_sums = [jnp.zeros((rows, DV), f32) for _ in range(heads)]
    for slot in range(slots):
        allowed = (row_ref[slot : slot + 1, :] >= own_pos) & (
            row_ref[2 * slots + slot : 2 * slots + slot + 1, :] == own_doc
        )
        queries = two_parts(slot_refs[slot][:, :qk])
        for head in range(heads):
            near = quarter_dot(keys[head], queries)
            numer = grad_refs[slot][:rows, head * DV : (head + 1) * DV].astype(bf16)
            lane = (head * rows) % (heads * DV)
            line = rows + (head * rows) // (heads * DV)
            grad = dot_t(values[head], numer) + grad_refs[slot][line : line + 1, lane : lane + rows]
            grad = jnp.where(allowed, grad * (1.0 + near), 0.0).astype(bf16)
            key_sums[head] = key_sums[head] + dot_n(grad, queries[0])
            score = jnp.where(allowed, 1.0 + near + 0.5 * near * near, 0.0).astype(bf16)
            value_sums[head] = value_sums[head] + dot_n(score, numer)
    total = jnp.zeros((rows, qk), f32)
    for head in range(heads):
        total = jnp.where(head_lanes(rows, qk, head), 0.25 * key_sums[head], total)
        out_ref[:, qk + head * DV : qk + (head + 1) * DV] = value_sums[head].astype(bf16)
    out_ref[:, :qk] = total.astype(bf16)


def whole_call(body, outs, *operands, flops=0):
    moved = sum(x.size * x.dtype.itemsize for x in (*operands, *outs))
    return pl.pallas_call(
        body,
        out_shape=outs,
        in_specs=[pl.BlockSpec(memory_space=pltpu.VMEM)] * len(operands),
        out_specs=jax.tree.map(lambda _: pl.BlockSpec(memory_space=pltpu.VMEM), outs),
        compiler_params=pltpu.CompilerParams(vmem_limit_bytes=VMEM_LIMIT),
        cost_estimate=pl.CostEstimate(flops=flops, bytes_accessed=moved, transcendentals=0),
    )(*operands)


def join_kernel(slots, *refs):
    step = pl.program_id(0)
    for slot in range(slots):

        @pl.when(step == slot)
        def _():
            refs[-1][...] = refs[slot][...].astype(bf16)


def join_rounded(parts):
    rows, width = parts[0].shape
    count = len(parts)
    cut = 512
    return pl.pallas_call(
        functools.partial(join_kernel, count),
        grid=(count, width // cut),
        out_shape=jax.ShapeDtypeStruct((count * rows, width), bf16),
        in_specs=[
            pl.BlockSpec(
                (rows, cut),
                functools.partial(
                    lambda slot, i, j: (
                        0,
                        jnp.where(i == slot, j, jnp.where(i < slot, 0, width // cut - 1)),
                    ),
                    slot,
                ),
            )
            for slot in range(count)
        ],
        out_specs=pl.BlockSpec((rows, cut), lambda i, j: (i, j)),
        compiler_params=pltpu.CompilerParams(vmem_limit_bytes=VMEM_LIMIT),
        cost_estimate=pl.CostEstimate(
            flops=0, bytes_accessed=6 * count * rows * width, transcendentals=0
        ),
    )(*parts)


def norm_back(grad_out, values, inverse, gain):
    scaled = grad_out * gain
    return inverse * (
        scaled - values * inverse * inverse * jnp.mean(scaled * values, axis=-1, keepdims=True)
    )


def mm(left, right):
    return jnp.dot(left, right, preferred_element_type=f32)


def mm_t(left, right):
    return jnp.einsum("ac,bc->ab", left, right, preferred_element_type=f32)


def t_mm(left, right):
    return jnp.einsum("ca,cb->ab", left, right, preferred_element_type=f32)


def gated(gate, up_lin, hidden_grad):
    sigmoid = jax.nn.sigmoid(gate)
    silu = gate * sigmoid
    return (
        (silu * up_lin).astype(bf16),
        (hidden_grad * up_lin * sigmoid * (1.0 + gate * (1.0 - sigmoid))).astype(bf16),
        (hidden_grad * silu).astype(bf16),
    )


def per_device(
    tokens,
    gain_attn,
    w_query,
    w_key,
    w_value,
    w_out,
    gain_mlp,
    w_gate,
    w_up,
    w_down,
    doc_lengths,
    cotangent,
):
    rows, width = tokens.shape
    heads = w_query.shape[1] // FEAT
    qk, vw = heads * FEAT, heads * DV
    blk_index, blk_count = lax.axis_index("blk"), lax.axis_size("blk")

    ends = [doc_lengths[0]]
    for doc in range(1, doc_lengths.shape[0]):
        ends.append(ends[-1] + doc_lengths[doc])

    def layout(positions):
        docs = sum((positions >= end).astype(jnp.int32) for end in ends[:-1])
        valid = positions < ends[-1]
        return docs, valid, jnp.where(valid, docs, -1)

    own_pos = blk_index * rows + jnp.arange(rows, dtype=jnp.int32)
    own_docs, own_valid, own_key_docs = layout(own_pos)
    columns = jnp.stack([own_pos, own_docs, own_valid.astype(jnp.int32), own_key_docs], axis=1)
    slot_blocks = blk_index ^ jnp.arange(blk_count, dtype=jnp.int32)
    slot_pos = slot_blocks[:, None] * rows + jnp.arange(rows, dtype=jnp.int32)[None, :]
    slot_docs, _, slot_key_docs = layout(slot_pos)
    lines = jnp.concatenate([slot_pos, slot_key_docs, slot_docs])

    gain_one, gain_two = gain_attn.astype(f32), gain_mlp.astype(f32)
    token_wide = tokens.astype(f32)
    inv_in = lax.rsqrt(jnp.mean(token_wide * token_wide, axis=-1, keepdims=True) + epsilon)
    normed_in = (token_wide * inv_in * gain_one).astype(bf16)
    w_qkv = jnp.concatenate([w_query, w_key, w_value], axis=1)
    qkv = gather_blk(mm(normed_in, w_qkv))

    cost = 16 * rows * rows * blk_count * vw
    attended, mean, inverse = whole_call(
        functools.partial(attend_kernel, heads, blk_count),
        (
            jax.ShapeDtypeStruct((rows, vw), bf16),
            jax.ShapeDtypeStruct((rows, vw), f32),
            jax.ShapeDtypeStruct((rows, vw), f32),
        ),
        columns,
        lines,
        *qkv,
        flops=cost,
    )
    resid_mid = token_wide + sum_head(mm(attended, w_out))
    inv_mid = lax.rsqrt(jnp.mean(resid_mid * resid_mid, axis=-1, keepdims=True) + epsilon)
    scaled_mid = resid_mid * inv_mid

    normed_mid = (scaled_mid * gain_two).astype(bf16)
    hidden, gate_lin_grad, up_lin_grad = gated(
        mm(normed_mid, w_gate), mm(normed_mid, w_up), mm_t(cotangent, w_down)
    )
    mid_part = mm_t(gate_lin_grad, w_gate) + mm_t(up_lin_grad, w_up)
    mlp_part = mm(hidden, w_down)
    mid_grad = sum_head(mid_part)
    output = (resid_mid + sum_head(mlp_part)).astype(bf16)

    all_cot = join_rounded(gather_blk(cotangent.astype(f32)))
    all_mid = join_rounded([part * gain_two for part in gather_blk(scaled_mid)])
    all_hidden, all_gate_grad, all_up_grad = gated(
        mm(all_mid, w_gate), mm(all_mid, w_up), mm_t(all_cot, w_down)
    )
    down_w_grad = t_mm(all_hidden, all_cot)
    gate_w_grad = t_mm(all_mid, all_gate_grad)
    up_w_grad = t_mm(all_mid, all_up_grad)

    resid_grad = cotangent.astype(f32) + norm_back(mid_grad, resid_mid, inv_mid, gain_two)
    out_lin_grad = resid_grad.astype(bf16)
    out_w_grad = sum_blk(t_mm(attended, out_lin_grad))
    attended_grad = mm_t(out_lin_grad, w_out)
    numer_grad = attended_grad * inverse
    denom_grad = -jnp.sum((numer_grad * mean).reshape(rows, heads, DV), axis=-1)
    denom_lines = denom_grad.T.reshape(rows // DV, vw)
    denom_lines = jnp.pad(denom_lines, ((0, -denom_lines.shape[0] % 8), (0, 0)))
    grads = gather_blk(jnp.concatenate([numer_grad, denom_lines]))
    (query_lin_grad,) = whole_call(
        functools.partial(query_kernel, heads, blk_count),
        (jax.ShapeDtypeStruct((rows, qk), bf16),),
        columns,
        lines,
        numer_grad,
        jnp.repeat(denom_grad, DV, axis=1),
        *qkv,
        flops=cost,
    )
    (key_value_grad,) = whole_call(
        functools.partial(key_kernel, heads, blk_count),
        (jax.ShapeDtypeStruct((rows, qk + vw), bf16),),
        columns,
        lines,
        *qkv,
        *grads,
        flops=2 * cost,
    )
    lin_grads = jnp.concatenate([query_lin_grad, key_value_grad], axis=1)
    in_part = mm_t(lin_grads, w_qkv)
    qkv_w_grad = sum_blk(t_mm(normed_in, lin_grads))
    in_grad = sum_head(in_part)
    input_grad = resid_grad + norm_back(in_grad, token_wide, inv_in, gain_one)
    gain_grads = lax.psum(
        jnp.stack(
            [
                jnp.sum(in_part * token_wide * inv_in, axis=0),
                jnp.sum(mid_part * scaled_mid, axis=0),
            ]
        ),
        ("blk", "head"),
    )
    return (
        output,
        input_grad,
        gain_grads[0],
        qkv_w_grad[:, :qk],
        qkv_w_grad[:, qk : 2 * qk],
        qkv_w_grad[:, 2 * qk :],
        out_w_grad,
        gain_grads[1],
        gate_w_grad,
        up_w_grad,
        down_w_grad,
    )


def solution(mesh):
    in_specs = (
        P("blk", None),
        P(),
        P(None, "head"),
        P(None, "head"),
        P(None, "head"),
        P("head", None),
        P(),
        P(None, "head"),
        P(None, "head"),
        P("head", None),
        P(),
        P("blk", None),
    )
    out_specs = (
        P("blk", None),
        P("blk", None),
        P(),
        P(None, "head"),
        P(None, "head"),
        P(None, "head"),
        P("head", None),
        P(),
        P(None, "head"),
        P(None, "head"),
        P("head", None),
    )
    return jax.shard_map(
        per_device, mesh=mesh, in_specs=in_specs, out_specs=out_specs, check_vma=False
    )
```

```python
import functools

import jax
import jax.numpy as jnp
from jax import lax
from jax.experimental import pallas as pl
from jax.experimental.pallas import tpu as pltpu
from jax.sharding import PartitionSpec as P

FEAT = 16
DV = 128

epsilon = 1e-05
f32, bf16 = jnp.float32, jnp.bfloat16
VMEM_LIMIT = 56 * 1024 * 1024


def hop(value, axis, way):
    if isinstance(way, int):
        way = [(i, i ^ way) for i in range(lax.axis_size(axis))]
    return lax.ppermute(value, axis, way)


def after(value, *others):
    return lax.optimization_barrier((value, others))[0]


def gather_blk(value):
    count = lax.axis_size("blk")
    if count != 8:
        slots, bit = [value], 1
        while bit < count:
            slots = slots + [hop(slot, "blk", bit) for slot in slots]
            bit *= 2
        return [[slot] for slot in slots]
    half = value.shape[0] // 16 * 8
    low, high = value[:half], value[half:]
    x_low, y_high = hop(low, "blk", 2), hop(high, "blk", 4)
    x_high, y_low = hop(high, "blk", 2), hop(low, "blk", 4)
    own_pair = hop(value, "blk", 1)
    far_low, far_high = hop(x_low, "blk", 4), hop(y_high, "blk", 2)
    slots = [[value], [own_pair]]
    for slot in ([x_low, x_high], [y_low, y_high], [far_low, far_high]):
        slots += [slot, [hop(part, "blk", 1) for part in slot]]
    return slots


class Chain:
    def __init__(self, steps):
        self.steps, self.result = steps, None
        self.advance(None)

    def advance(self, values):
        try:
            self.due = self.steps.send(values)
        except StopIteration as end:
            self.due, self.result = [], end.value


class Convoy:
    def __init__(self):
        self.landed = ()

    def wave(self, chains, work=None, *operands):
        chains = [chain for chain in chains if chain.due]
        values = [after([value for value, _, _ in chain.due], self.landed) for chain in chains]
        flying = [
            [hop(value, axis, way) for value, (_, axis, way) in zip(sent, chain.due)]
            for sent, chain in zip(values, chains)
        ]
        result = None if work is None else work(*after(operands, values, self.landed))
        flying = after(flying, values if result is None else result)
        for chain, came in zip(chains, flying):
            chain.advance(came)
        self.landed = (flying, result)
        return result


def gather_steps(value, slots, even=False):
    count = lax.axis_size("blk")
    slots[0] = [value]
    if count != 8:
        bit = 1
        while bit < count:
            got = yield [(slots[slot][0], "blk", bit) for slot in range(bit)]
            slots.update({bit + slot: [part] for slot, part in enumerate(got)})
            bit *= 2
        return
    half = value.shape[0] // 16 * 8
    low, high = value[:half], value[half:]
    if even:
        x_low, y_high, own_pair = yield [(low, "blk", 2), (high, "blk", 4), (value, "blk", 1)]
        slots[1] = [own_pair]
        x_high, y_low = yield [(high, "blk", 2), (low, "blk", 4)]
        slots[2], slots[4] = [x_low, x_high], [y_low, y_high]
        slots[6] = yield [(x_low, "blk", 4), (y_high, "blk", 2)]
        first = yield [(x_low, "blk", 1), (y_high, "blk", 1)]
        second = yield [(x_high, "blk", 1), (y_low, "blk", 1)]
        slots[3], slots[5] = [first[0], second[0]], [second[1], first[1]]
    else:
        x_all, y_all, own_pair = yield [(value, "blk", way) for way in (2, 4, 1)]
        slots[1], slots[2], slots[4] = [own_pair], [x_all], [y_all]
        *slots[6], x_pair, y_pair = yield [
            (x_all[:half], "blk", 4),
            (y_all[half:], "blk", 2),
            (x_all, "blk", 1),
            (y_all, "blk", 1),
        ]
        slots[3], slots[5] = [x_pair], [y_pair]
    slots[7] = yield [(part, "blk", 1) for part in slots[6]]


def halves(value, bit):
    low, high = jnp.split(value, 2)
    upper = (lax.axis_index("blk") & bit) != 0
    return jnp.where(upper, high, low), jnp.where(upper, low, high)


def paired(value, other, bit):
    upper = (lax.axis_index("blk") & bit) != 0
    return jnp.concatenate([jnp.where(upper, other, value), jnp.where(upper, value, other)])


def sum_steps(value):
    count = lax.axis_size("blk")
    bits = [1 << place for place in range(count.bit_length() - 1)]
    for bit in bits:
        keep, send = halves(value, bit)
        (got,) = yield [(send, "blk", bit)]
        value = keep + got
    for bit in reversed(bits):
        (got,) = yield [(value, "blk", bit)]
        value = paired(value, got, bit)
    return value


def small_steps(value):
    for axis in ("head", "blk"):
        bit = 1
        while bit < lax.axis_size(axis):
            (got,) = yield [(value, axis, bit)]
            value = value + got
            bit *= 2
    return value


def head_steps(value):
    count, mine = lax.axis_size("head"), lax.axis_index("head")
    rows = value.shape[0] // count

    def share(step):
        return lax.dynamic_slice_in_dim(value, (mine ^ step) * rows, rows)

    got = yield [(share(step), "head", step) for step in range(1, count)]
    total = share(0)
    for part in got:
        total = total + part
    got = yield [(total, "head", step) for step in range(1, count)]
    whole = jnp.zeros_like(value)
    for step, part in enumerate([total, *got]):
        whole = lax.dynamic_update_slice_in_dim(whole, part, (mine ^ step) * rows, 0)
    return whole


def line_steps(value, pieces):
    if lax.axis_size("head") != 4:
        return (yield from head_steps(value))
    mine = lax.axis_index("head")
    inner = (mine == 1) | (mine == 2)
    parts = jnp.split(value, pieces)
    pairs, whole, done = {}, {}, {}
    for wave in range(pieces + 2):
        sends, takes = [], []
        if wave < pieces:
            sends.append((parts[wave], "head", [(0, 1), (3, 2)]))
            takes.append((pairs, wave, parts))
        if 0 <= wave - 1 < pieces:
            sends.append((pairs[wave - 1], "head", [(1, 2), (2, 1)]))
            takes.append((whole, wave - 1, pairs))
        if 0 <= wave - 2:
            sends.append((whole[wave - 2], "head", [(1, 0), (2, 3)]))
            takes.append((done, wave - 2, whole))
        got = yield sends
        for part, (into, piece, own) in zip(got, takes):
            if into is done:
                into[piece] = jnp.where(inner, own[piece], part)
            else:
                into[piece] = own[piece] + part
    return jnp.concatenate([done[piece] for piece in range(pieces)])


def sum_head(value):
    return lax.psum(value, "head")


def dot_t(left, right):
    return lax.dot_general(left, right, (((1,), (1,)), ((), ())), preferred_element_type=f32)


def dot_n(left, right):
    return lax.dot_general(left, right, (((1,), (0,)), ((), ())), preferred_element_type=f32)


def head_lanes(rows, width, first):
    lanes = lax.broadcasted_iota(jnp.int32, (rows, width), 1)
    return (lanes >= first) & (lanes < first + FEAT)


def read(slot, lines, lanes):
    parts = [ref[:, lanes] for ref in slot]
    whole = parts[0] if len(parts) == 1 else jnp.concatenate(parts)
    return whole if lines is None else whole[lines]


def split_refs(refs, shape):
    slots, at = [], 0
    for pieces in shape:
        slots.append(refs[at : at + pieces])
        at += pieces
    return slots, refs[at:]


def turned(tile, heads, use_key):
    rows, width = tile.shape
    moved = jnp.concatenate([tile[:, width // 2 :], tile[:, : width // 2]], axis=1)
    base = 0 if use_key else width // 2
    scaled = moved * 0.25
    return [
        jnp.where(head_lanes(rows, width, base + head * FEAT), scaled, 0.0).astype(bf16)
        for head in range(heads)
    ]


def attend_kernel(heads, shape, col_ref, row_ref, *refs):
    slots, (att_ref, mean_ref, inverse_ref) = split_refs(refs, shape)
    count = len(slots)
    rows = col_ref.shape[0]
    qk = heads * FEAT
    own_pos, own_doc = col_ref[:, 0:1], col_ref[:, 1:2]
    valid = col_ref[:, 2:3].astype(f32)
    numer = [jnp.zeros((rows, DV), f32) for _ in range(heads)]
    denom = [jnp.zeros((rows, 1), f32) for _ in range(heads)]
    queries = turned(read(slots[0], None, slice(0, 2 * qk)), heads, False)
    for slot in range(count):
        allowed = (row_ref[slot : slot + 1, :] <= own_pos) & (
            row_ref[count + slot : count + slot + 1, :] == own_doc
        )
        keys = read(slots[slot], None, slice(0, 2 * qk)).astype(bf16)
        for head in range(heads):
            near = 1.0 + dot_t(queries[head], keys)
            score = jnp.where(allowed, 0.5 * near * near + 0.5, 0.0)
            first = 2 * qk + head * DV
            value = read(slots[slot], None, slice(first, first + DV)).astype(bf16)
            numer[head] = numer[head] + dot_n(score.astype(bf16), value)
            denom[head] = denom[head] + jnp.sum(score, axis=1, keepdims=True)
    for head in range(heads):
        span = slice(head * DV, (head + 1) * DV)
        mean = numer[head] / denom[head]
        att_ref[:, span] = (valid * mean).astype(bf16)
        mean_ref[:, span] = mean
        inverse_ref[:, span] = jnp.broadcast_to(valid / denom[head], (rows, DV))


def query_kernel(heads, shape, col_ref, row_ref, numer_ref, denom_ref, *refs):
    slots, (out_ref,) = split_refs(refs, shape)
    count = len(slots)
    rows = col_ref.shape[0]
    qk = heads * FEAT
    own_pos, own_doc = col_ref[:, 0:1], col_ref[:, 1:2]
    queries = turned(read(slots[0], None, slice(0, 2 * qk)), heads, False)
    sums = [jnp.zeros((rows, 2 * qk), f32) for _ in range(heads)]
    for slot in range(count):
        allowed = (row_ref[slot : slot + 1, :] <= own_pos) & (
            row_ref[count + slot : count + slot + 1, :] == own_doc
        )
        keys = read(slots[slot], None, slice(0, 2 * qk)).astype(bf16)
        for head in range(heads):
            near = 1.0 + dot_t(queries[head], keys)
            first = 2 * qk + head * DV
            value = read(slots[slot], None, slice(first, first + DV)).astype(bf16)
            grad = dot_t(numer_ref[:, head * DV : (head + 1) * DV].astype(bf16), value)
            grad = grad + denom_ref[:, head * DV : head * DV + 1]
            grad = jnp.where(allowed, grad * near, 0.0).astype(bf16)
            sums[head] = sums[head] + dot_n(grad, keys)
    total = jnp.zeros((rows, 2 * qk), f32)
    for head in range(heads):
        total = jnp.where(head_lanes(rows, 2 * qk, qk + head * FEAT), 0.25 * sums[head], total)
    out_ref[...] = total[:, qk:].astype(bf16)


def key_kernel(heads, shape, grad_shape, col_ref, row_ref, *refs):
    slots, rest = split_refs(refs, shape)
    grads, (key_ref, value_ref) = split_refs(rest, grad_shape)
    count = len(slots)
    rows = col_ref.shape[0]
    qk, vw = heads * FEAT, heads * DV
    own_pos, own_doc = col_ref[:, 0:1], col_ref[:, 3:4]
    keys = turned(read(slots[0], None, slice(0, 2 * qk)), heads, True)
    values = [
        read(slots[0], None, slice(2 * qk + head * DV, 2 * qk + (head + 1) * DV)).astype(bf16)
        for head in range(heads)
    ]
    key_sums = [jnp.zeros((rows, 2 * qk), f32) for _ in range(heads)]
    value_sums = [jnp.zeros((rows, DV), f32) for _ in range(heads)]
    for slot in range(count):
        allowed = (row_ref[slot : slot + 1, :] >= own_pos) & (
            row_ref[2 * count + slot : 2 * count + slot + 1, :] == own_doc
        )
        queries = read(slots[slot], None, slice(0, 2 * qk)).astype(bf16)
        last = grads[slot][-1]
        extra = last.shape[0] - (rows - sum(ref.shape[0] for ref in grads[slot][:-1]))
        base = last.shape[0] - extra
        for head in range(heads):
            near = 1.0 + dot_t(keys[head], queries)
            span = slice(head * DV, (head + 1) * DV)
            numer = read(grads[slot], slice(0, rows), span).astype(bf16)
            line, lane = base + (head * rows) // vw, (head * rows) % vw
            grad = dot_t(values[head], numer) + last[line : line + 1, lane : lane + rows]
            grad = jnp.where(allowed, grad * near, 0.0).astype(bf16)
            key_sums[head] = key_sums[head] + dot_n(grad, queries)
            score = jnp.where(allowed, 0.5 * near * near + 0.5, 0.0).astype(bf16)
            value_sums[head] = value_sums[head] + dot_n(score, numer)
    total = jnp.zeros((rows, 2 * qk), f32)
    for head in range(heads):
        total = jnp.where(head_lanes(rows, 2 * qk, head * FEAT), 0.25 * key_sums[head], total)
        value_ref[:, head * DV : (head + 1) * DV] = value_sums[head].astype(bf16)
    key_ref[...] = total[:, :qk].astype(bf16)


def whole_call(body, outs, *operands, flops=0):
    moved = sum(x.size * x.dtype.itemsize for x in (*operands, *outs))
    return pl.pallas_call(
        body,
        out_shape=outs,
        in_specs=[pl.BlockSpec(memory_space=pltpu.VMEM)] * len(operands),
        out_specs=jax.tree.map(lambda _: pl.BlockSpec(memory_space=pltpu.VMEM), outs),
        compiler_params=pltpu.CompilerParams(vmem_limit_bytes=VMEM_LIMIT),
        cost_estimate=pl.CostEstimate(flops=flops, bytes_accessed=moved, transcendentals=0),
    )(*operands)


def join_kernel(shape, scale_ref, *refs):
    slots, (out_ref,) = split_refs(refs, shape)
    step = pl.program_id(0)
    for slot in range(len(slots)):

        @pl.when(step == slot)
        def _():
            at = 0
            for ref in slots[slot]:
                out_ref[at : at + ref.shape[0], :] = (ref[...] * scale_ref[...]).astype(bf16)
                at += ref.shape[0]


def join_rounded(slots, scale):
    parts = [part for slot in slots for part in slot]
    rows, width = sum(part.shape[0] for part in slots[0]), parts[0].shape[1]
    count = len(slots)
    return pl.pallas_call(
        functools.partial(join_kernel, tuple(len(slot) for slot in slots)),
        grid=(count,),
        out_shape=jax.ShapeDtypeStruct((count * rows, width), bf16),
        in_specs=[pl.BlockSpec((1, width), lambda i: (0, 0))]
        + [
            pl.BlockSpec(part.shape, lambda i: (0, 0), pipeline_mode=pl.Buffered(1))
            for part in parts
        ],
        out_specs=pl.BlockSpec((rows, width), lambda i: (i, 0)),
        compiler_params=pltpu.CompilerParams(vmem_limit_bytes=VMEM_LIMIT),
        cost_estimate=pl.CostEstimate(
            flops=0, bytes_accessed=6 * count * rows * width, transcendentals=0
        ),
    )(scale[None, :], *parts)


def norm_back(grad_out, values, inverse, gain):
    scaled = grad_out * gain
    return inverse * (
        scaled - values * inverse * inverse * jnp.mean(scaled * values, axis=-1, keepdims=True)
    )


def mm(left, right):
    return jnp.dot(left, right, preferred_element_type=f32)


def mm_t(left, right):
    return jnp.einsum("ac,bc->ab", left, right, preferred_element_type=f32)


def t_mm(left, right):
    return jnp.einsum("ca,cb->ab", left, right, preferred_element_type=f32)


def gated(gate, up_lin, hidden_grad):
    sigmoid = 0.5 + 0.5 * jnp.tanh(0.5 * gate)
    silu = gate * sigmoid
    return (
        (silu * up_lin).astype(bf16),
        (hidden_grad * up_lin * sigmoid * (1.0 + gate * (1.0 - sigmoid))).astype(bf16),
        (hidden_grad * silu).astype(bf16),
    )


def per_device(
    tokens,
    gain_attn,
    w_query,
    w_key,
    w_value,
    w_out,
    gain_mlp,
    w_gate,
    w_up,
    w_down,
    doc_lengths,
    cotangent,
):
    rows, width = tokens.shape
    heads = w_query.shape[1] // FEAT
    qk, vw = heads * FEAT, heads * DV
    blk_index, blk_count = lax.axis_index("blk"), lax.axis_size("blk")

    ends = [doc_lengths[0]]
    for doc in range(1, doc_lengths.shape[0]):
        ends.append(ends[-1] + doc_lengths[doc])

    def layout(positions):
        docs = sum((positions >= end).astype(jnp.int32) for end in ends[:-1])
        valid = positions < ends[-1]
        return docs, valid, jnp.where(valid, docs, -1)

    own_pos = blk_index * rows + jnp.arange(rows, dtype=jnp.int32)
    own_docs, own_valid, own_key_docs = layout(own_pos)
    columns = jnp.stack([own_pos, own_docs, own_valid.astype(jnp.int32), own_key_docs], axis=1)
    slot_blocks = blk_index ^ jnp.arange(blk_count, dtype=jnp.int32)
    slot_pos = slot_blocks[:, None] * rows + jnp.arange(rows, dtype=jnp.int32)[None, :]
    slot_docs, _, slot_key_docs = layout(slot_pos)
    lines = jnp.concatenate([slot_pos, slot_key_docs, slot_docs])

    gain_one, gain_two = gain_attn.astype(f32), gain_mlp.astype(f32)
    token_wide, cot_wide = tokens.astype(f32), cotangent.astype(f32)
    inv_in = lax.rsqrt(jnp.mean(token_wide * token_wide, axis=-1, keepdims=True) + epsilon)
    normed_in = (token_wide * inv_in * gain_one).astype(bf16)
    qkv_own = jnp.concatenate(
        [mm(normed_in, w_query), mm(normed_in, w_key), mm(normed_in, w_value)], axis=1
    )
    qkv = gather_blk(qkv_own)
    shape = tuple(len(slot) for slot in qkv)
    qkv_parts = [part for slot in qkv for part in slot]

    cost = 8 * rows * rows * blk_count * vw
    attended, mean, inverse = whole_call(
        functools.partial(attend_kernel, heads, shape),
        (
            jax.ShapeDtypeStruct((rows, vw), bf16),
            jax.ShapeDtypeStruct((rows, vw), f32),
            jax.ShapeDtypeStruct((rows, vw), f32),
        ),
        columns,
        lines,
        *qkv_parts,
        flops=cost,
    )
    attn_part = mm(attended, w_out)
    attn_sum = sum_head(attn_part)
    convoy = Convoy()
    cot_slots = {}
    cot = Chain(gather_steps(after(cot_wide, qkv[-2]), cot_slots))
    own_hidden_grad = convoy.wave(
        [cot], lambda left, _: mm_t(left, w_down), cotangent, attn_part
    )
    token_sum = after(token_wide, convoy.landed) + attn_sum

    def middle(resid_mid):
        inv_mid = lax.rsqrt(jnp.mean(resid_mid * resid_mid, axis=-1, keepdims=True) + epsilon)
        scaled_mid = resid_mid * inv_mid
        normed_mid = (scaled_mid * gain_two).astype(bf16)
        hidden, gate_lin_grad, up_lin_grad = gated(
            mm(normed_mid, w_gate), mm(normed_mid, w_up), own_hidden_grad
        )
        mid_part = mm_t(gate_lin_grad, w_gate) + mm_t(up_lin_grad, w_up)
        return resid_mid, inv_mid, scaled_mid, hidden, mid_part

    resid_mid, inv_mid, scaled_mid, hidden, mid_part = convoy.wave([cot], middle, token_sum)

    def ready(chain, slots, wanted):
        while not all(slot in slots for slot in wanted):
            convoy.wave([chain])
        return [slots[slot] for slot in wanted]

    order = [0, 1, 2, 4, 3, 5, 6, 7] if blk_count == 8 else list(range(blk_count))
    early, late = order[: blk_count // 2], order[blk_count // 2 :]
    ones = jnp.ones_like(gain_two)
    mid_slots = {}
    mid_sum = Chain(line_steps(mid_part, 2))
    mid = Chain(gather_steps(scaled_mid, mid_slots, even=True))
    cot_early, cot_late = ready(cot, cot_slots, early), ready(cot, cot_slots, late)

    def share_work(hidden, *slots):
        mlp_part = mm(hidden, w_down)
        cot_a = join_rounded(after(slots[: len(early)], mlp_part), ones)
        return mlp_part, cot_a, join_rounded(after(slots[len(early) :], cot_a), ones)

    mlp_part, cot_a, cot_b = convoy.wave([mid_sum, mid], share_work, hidden, *cot_early, *cot_late)
    hidden_grad_a, hidden_grad_b = convoy.wave(
        [mid_sum, mid], lambda a, b: (mm_t(a, w_down), mm_t(b, w_down)), cot_a, cot_b
    )
    mlp = Chain(line_steps(mlp_part, 2))

    def gate_work(*slots):
        rows_of = join_rounded(slots, gain_two)
        return rows_of, mm(rows_of, w_gate)

    def up_work(rows_of, gate, hidden_grad):
        return gated(gate, mm(rows_of, w_up), hidden_grad)

    mid_a, gate_a = convoy.wave([mid_sum, mid, mlp], gate_work, *ready(mid, mid_slots, early))
    hidden_a, gate_grad_a, up_grad_a = convoy.wave(
        [mid_sum, mid, mlp], up_work, mid_a, gate_a, hidden_grad_a
    )
    while mid_sum.due:
        convoy.wave([mid_sum])
    mid_grad = mid_sum.result

    resid_grad = cot_wide + norm_back(mid_grad, resid_mid, inv_mid, gain_two)
    out_lin_grad = resid_grad.astype(bf16)
    attended_grad = mm_t(out_lin_grad, w_out)
    numer_grad = attended_grad * inverse
    denom_grad = -jnp.sum((numer_grad * mean).reshape(rows, heads, DV), axis=-1)
    denom_lines = denom_grad.T.reshape(rows // DV, vw)
    denom_lines = jnp.pad(denom_lines, ((0, -denom_lines.shape[0] % 8), (0, 0)))
    grad_slots = {}
    grads = Chain(gather_steps(jnp.concatenate([numer_grad, denom_lines]), grad_slots))

    def query_work(numer_grad, denom_grad, out_lin_grad):
        (query_lin_grad,) = whole_call(
            functools.partial(query_kernel, heads, shape),
            (jax.ShapeDtypeStruct((rows, qk), bf16),),
            columns,
            lines,
            numer_grad,
            jnp.repeat(denom_grad, DV, axis=1),
            *qkv_parts,
            flops=cost,
        )
        return query_lin_grad, t_mm(attended, after(out_lin_grad, query_lin_grad))

    query_lin_grad, out_part = convoy.wave(
        [grads, mid], query_work, numer_grad, denom_grad, out_lin_grad
    )
    out = Chain(sum_steps(out_part))
    down_a = convoy.wave([grads, out], t_mm, hidden_a, cot_a)
    convoy.wave([grads, mid])
    grad_slots = ready(grads, grad_slots, range(blk_count))
    grad_shape = tuple(len(slot) for slot in grad_slots)

    def key_work(query_lin_grad, grad_parts):
        key_lin_grad, value_grad = whole_call(
            functools.partial(key_kernel, heads, shape, grad_shape),
            (jax.ShapeDtypeStruct((rows, qk), bf16), jax.ShapeDtypeStruct((rows, vw), bf16)),
            columns,
            lines,
            *qkv_parts,
            *grad_parts,
            flops=2 * cost,
        )
        in_part = mm_t(query_lin_grad, w_query) + mm_t(key_lin_grad, w_key)
        in_part = in_part + mm_t(value_grad, w_value)
        return in_part, query_lin_grad, key_lin_grad, value_grad

    grad_parts = [part for slot in grad_slots for part in slot]
    in_part, *lin_grads = convoy.wave([], key_work, query_lin_grad, grad_parts)
    late_in = after(normed_in, in_part)
    parts = [t_mm(late_in, grad) for grad in lin_grads]
    gain_parts = jnp.stack(
        [
            jnp.sum(after(in_part, parts) * token_wide * inv_in, axis=0),
            jnp.sum(mid_part * scaled_mid, axis=0),
        ]
    )
    qkv_w_grads = lax.psum(tuple(parts), "blk")
    gains = Chain(small_steps(gain_parts))

    in_sum = Chain(line_steps(in_part, 2))
    mid_late = ready(mid, mid_slots, late)

    def third_work(hidden_b, down_a, gate_grad_a):
        down_w_grad = down_a + t_mm(hidden_b, cot_b)
        return down_w_grad, t_mm(mid_a, after(gate_grad_a, down_w_grad))

    def second_work(mid_b, gate_b, hidden_grad_b, up_grad_a):
        parts = up_work(mid_b, gate_b, hidden_grad_b)
        return (*parts, t_mm(mid_a, after(up_grad_a, parts)))

    def last_work(gate_grad_b, gate_part, up_grad_b, up_part, mlp_sum):
        gate_w_grad = gate_part + t_mm(mid_b, gate_grad_b)
        output = (resid_mid + after(mlp_sum, gate_w_grad)).astype(bf16)
        late_grad = after(up_grad_b, gate_w_grad, output, qkv_w_grads)
        return gate_w_grad, up_part + t_mm(mid_b, late_grad), output

    chains = [in_sum, out, gains, mlp]
    mid_b, gate_b = convoy.wave(chains, gate_work, *after(mid_late, parts))
    hidden_b, gate_grad_b, up_grad_b, up_part = convoy.wave(
        chains, second_work, mid_b, gate_b, hidden_grad_b, up_grad_a
    )
    down_w_grad, gate_part = convoy.wave(chains, third_work, hidden_b, down_a, gate_grad_a)
    while mlp.due:
        convoy.wave([mlp])
    gate_w_grad, up_w_grad, output = convoy.wave(
        chains, last_work, gate_grad_b, gate_part, up_grad_b, up_part, mlp.result
    )
    while any(chain.due for chain in chains):
        convoy.wave(chains)
    in_grad, out_w_grad, gain_grads = (chain.result for chain in chains[:3])
    input_grad = resid_grad + norm_back(in_grad, token_wide, inv_in, gain_one)
    return (
        output,
        input_grad,
        gain_grads[0],
        *qkv_w_grads,
        out_w_grad,
        gain_grads[1],
        gate_w_grad,
        up_w_grad,
        down_w_grad,
    )


def solution(mesh):
    in_specs = (
        P("blk", None),
        P(),
        P(None, "head"),
        P(None, "head"),
        P(None, "head"),
        P("head", None),
        P(),
        P(None, "head"),
        P(None, "head"),
        P("head", None),
        P(),
        P("blk", None),
    )
    out_specs = (
        P("blk", None),
        P("blk", None),
        P(),
        P(None, "head"),
        P(None, "head"),
        P(None, "head"),
        P("head", None),
        P(),
        P(None, "head"),
        P(None, "head"),
        P("head", None),
    )
    return jax.shard_map(
        per_device, mesh=mesh, in_specs=in_specs, out_specs=out_specs, check_vma=False
    )
```

```python
import functools

import jax
import jax.numpy as jnp
from jax import lax
from jax.experimental import pallas as pl
from jax.experimental.pallas import tpu as pltpu
from jax.sharding import PartitionSpec as P

FEAT = 16
DV = 128

epsilon = 1e-05
f32, bf16 = jnp.float32, jnp.bfloat16
VMEM_LIMIT = 56 * 1024 * 1024


def hop(value, axis, way):
    if isinstance(way, int):
        way = [(i, i ^ way) for i in range(lax.axis_size(axis))]
    return lax.ppermute(value, axis, way)


def after(value, *others):
    return lax.optimization_barrier((value, others))[0]


def gather_blk(value):
    count = lax.axis_size("blk")
    if count != 8:
        slots, bit = [value], 1
        while bit < count:
            slots = slots + [hop(slot, "blk", bit) for slot in slots]
            bit *= 2
        return [[slot] for slot in slots]
    half = value.shape[0] // 16 * 8
    low, high = value[:half], value[half:]
    x_low, y_high = hop(low, "blk", 2), hop(high, "blk", 4)
    x_high, y_low = hop(high, "blk", 2), hop(low, "blk", 4)
    own_pair = hop(value, "blk", 1)
    far_low, far_high = hop(x_low, "blk", 4), hop(y_high, "blk", 2)
    slots = [[value], [own_pair]]
    for slot in ([x_low, x_high], [y_low, y_high], [far_low, far_high]):
        slots += [slot, [hop(part, "blk", 1) for part in slot]]
    return slots


class Chain:
    def __init__(self, steps):
        self.steps, self.result, self.flying = steps, None, None
        self.advance(None)

    def advance(self, values):
        try:
            self.due = self.steps.send(values)
        except StopIteration as end:
            self.due, self.result = [], end.value


class Convoy:
    def __init__(self):
        self.landed, self.sent, self.done = (), (), ()

    def launch(self, *chains):
        for chain in chains:
            if chain.due:
                values = after([value for value, _, _ in chain.due], self.landed, self.sent)
                chain.flying = [
                    hop(value, axis, way) for value, (_, axis, way) in zip(values, chain.due)
                ]
                self.sent = (self.sent, values)

    def work(self, work, *operands):
        self.done = work(*after(operands, self.sent, self.landed))
        return self.done

    def land(self, *chains):
        chains = [chain for chain in chains if chain.flying is not None]
        came = after([chain.flying for chain in chains], self.done)
        self.landed, self.sent = (came, self.done), ()
        for chain, values in zip(chains, came):
            chain.flying = None
            chain.advance(values)

    def wave(self, chains, work=None, *operands):
        self.launch(*chains)
        result = None if work is None else self.work(work, *operands)
        self.land(*chains)
        return result

    def finish(self, chain):
        while chain.due:
            self.wave([chain])


def gather_steps(value, slots):
    count = lax.axis_size("blk")
    slots[0] = [value]
    if count != 8:
        bit = 1
        while bit < count:
            got = yield [(slots[slot][0], "blk", bit) for slot in range(bit)]
            slots.update({bit + slot: [part] for slot, part in enumerate(got)})
            bit *= 2
        return
    half = value.shape[0] // 16 * 8
    x_all, y_all, own_pair = yield [(value, "blk", way) for way in (2, 4, 1)]
    slots[1], slots[2], slots[4] = [own_pair], [x_all], [y_all]
    *slots[6], x_pair, y_pair = yield [
        (x_all[:half], "blk", 4),
        (y_all[half:], "blk", 2),
        (x_all, "blk", 1),
        (y_all, "blk", 1),
    ]
    slots[3], slots[5] = [x_pair], [y_pair]
    slots[7] = yield [(part, "blk", 1) for part in slots[6]]


def small_steps(value):
    for axis in ("head", "blk"):
        bit = 1
        while bit < lax.axis_size(axis):
            ways = [bit]
            if axis == "blk" and bit == 2 and lax.axis_size(axis) == 8:
                ways = [2, 4, 6]
            for got in (yield [(value, axis, way) for way in ways]):
                value = value + got
            bit *= 2 * len(ways)
    return value


def head_share(value, step=0):
    rows = value.shape[0] // lax.axis_size("head")
    return lax.dynamic_slice_in_dim(value, (lax.axis_index("head") ^ step) * rows, rows)


def head_steps(value, finish=None):
    count, mine = lax.axis_size("head"), lax.axis_index("head")
    got = yield [(head_share(value, step), "head", step) for step in range(1, count)]
    total = head_share(value)
    for part in got:
        total = total + part
    total = total if finish is None else finish(total)
    got = yield [(total, "head", step) for step in range(1, count)]
    whole = jnp.zeros_like(value)
    for step, part in enumerate([total, *got]):
        whole = lax.dynamic_update_slice_in_dim(whole, part, (mine ^ step) * part.shape[0], 0)
    return whole


def line_steps(value, pieces):
    if lax.axis_size("head") != 4:
        return (yield from head_steps(value))
    mine = lax.axis_index("head")
    inner = (mine == 1) | (mine == 2)
    parts = jnp.split(value, pieces)
    pairs, whole, done = {}, {}, {}
    for wave in range(pieces + 2):
        sends, takes = [], []
        if wave < pieces:
            sends.append((parts[wave], "head", [(0, 1), (3, 2)]))
            takes.append((pairs, wave, parts))
        if 0 <= wave - 1 < pieces:
            sends.append((pairs[wave - 1], "head", [(1, 2), (2, 1)]))
            takes.append((whole, wave - 1, pairs))
        if 0 <= wave - 2:
            sends.append((whole[wave - 2], "head", [(1, 0), (2, 3)]))
            takes.append((done, wave - 2, whole))
        got = yield sends
        for part, (into, piece, own) in zip(got, takes):
            if into is done:
                into[piece] = jnp.where(inner, own[piece], part)
            else:
                into[piece] = own[piece] + part
    return jnp.concatenate([done[piece] for piece in range(pieces)])


def sum_head(value):
    return lax.psum(value, "head")


def dot_t(left, right):
    return lax.dot_general(left, right, (((1,), (1,)), ((), ())), preferred_element_type=f32)


def dot_n(left, right):
    return lax.dot_general(left, right, (((1,), (0,)), ((), ())), preferred_element_type=f32)


def head_lanes(rows, width, first):
    lanes = lax.broadcasted_iota(jnp.int32, (rows, width), 1)
    return (lanes >= first) & (lanes < first + FEAT)


def read(slot, lines, lanes):
    parts = [ref[:, lanes] for ref in slot]
    whole = parts[0] if len(parts) == 1 else jnp.concatenate(parts)
    return whole if lines is None else whole[lines]


def split_refs(refs, shape):
    slots, at = [], 0
    for pieces in shape:
        slots.append(refs[at : at + pieces])
        at += pieces
    return slots, refs[at:]


def turned(tile, heads, use_key):
    rows, width = tile.shape
    moved = jnp.concatenate([tile[:, width // 2 :], tile[:, : width // 2]], axis=1)
    base = 0 if use_key else width // 2
    scaled = moved * 0.25
    return [
        jnp.where(head_lanes(rows, width, base + head * FEAT), scaled, 0.0).astype(bf16)
        for head in range(heads)
    ]


def attend_kernel(heads, shape, col_ref, row_ref, *refs):
    slots, (att_ref, mean_ref, inverse_ref) = split_refs(refs, shape)
    count = len(slots)
    rows = col_ref.shape[0]
    qk = heads * FEAT
    own_pos, own_doc = col_ref[:, 0:1], col_ref[:, 1:2]
    valid = col_ref[:, 2:3].astype(f32)
    numer = [jnp.zeros((rows, DV), f32) for _ in range(heads)]
    denom = [jnp.zeros((rows, 1), f32) for _ in range(heads)]
    queries = turned(read(slots[0], None, slice(0, 2 * qk)), heads, False)
    for slot in range(count):
        allowed = (row_ref[slot : slot + 1, :] <= own_pos) & (
            row_ref[count + slot : count + slot + 1, :] == own_doc
        )
        keys = read(slots[slot], None, slice(0, 2 * qk)).astype(bf16)
        for head in range(heads):
            near = 1.0 + dot_t(queries[head], keys)
            score = jnp.where(allowed, 0.5 * near * near + 0.5, 0.0)
            first = 2 * qk + head * DV
            value = read(slots[slot], None, slice(first, first + DV)).astype(bf16)
            numer[head] = numer[head] + dot_n(score.astype(bf16), value)
            denom[head] = denom[head] + jnp.sum(score, axis=1, keepdims=True)
    for head in range(heads):
        span = slice(head * DV, (head + 1) * DV)
        mean = numer[head] / denom[head]
        att_ref[:, span] = (valid * mean).astype(bf16)
        mean_ref[:, span] = mean
        inverse_ref[:, span] = jnp.broadcast_to(valid / denom[head], (rows, DV))


def query_kernel(heads, shape, col_ref, row_ref, numer_ref, denom_ref, *refs):
    slots, (out_ref,) = split_refs(refs, shape)
    count = len(slots)
    rows = col_ref.shape[0]
    qk = heads * FEAT
    own_pos, own_doc = col_ref[:, 0:1], col_ref[:, 1:2]
    queries = turned(read(slots[0], None, slice(0, 2 * qk)), heads, False)
    sums = [jnp.zeros((rows, 2 * qk), f32) for _ in range(heads)]
    for slot in range(count):
        allowed = (row_ref[slot : slot + 1, :] <= own_pos) & (
            row_ref[count + slot : count + slot + 1, :] == own_doc
        )
        keys = read(slots[slot], None, slice(0, 2 * qk)).astype(bf16)
        for head in range(heads):
            near = 1.0 + dot_t(queries[head], keys)
            first = 2 * qk + head * DV
            value = read(slots[slot], None, slice(first, first + DV)).astype(bf16)
            grad = dot_t(numer_ref[:, head * DV : (head + 1) * DV].astype(bf16), value)
            grad = grad + denom_ref[:, head * DV : head * DV + 1]
            grad = jnp.where(allowed, grad * near, 0.0).astype(bf16)
            sums[head] = sums[head] + dot_n(grad, keys)
    total = jnp.zeros((rows, 2 * qk), f32)
    for head in range(heads):
        total = jnp.where(head_lanes(rows, 2 * qk, qk + head * FEAT), 0.25 * sums[head], total)
    out_ref[...] = total[:, qk:].astype(bf16)


def key_kernel(heads, shape, grad_shape, col_ref, row_ref, *refs):
    slots, rest = split_refs(refs, shape)
    grads, (key_ref, value_ref) = split_refs(rest, grad_shape)
    count = len(slots)
    rows = col_ref.shape[0]
    qk, vw = heads * FEAT, heads * DV
    own_pos, own_doc = col_ref[:, 0:1], col_ref[:, 3:4]
    keys = turned(read(slots[0], None, slice(0, 2 * qk)), heads, True)
    values = [
        read(slots[0], None, slice(2 * qk + head * DV, 2 * qk + (head + 1) * DV)).astype(bf16)
        for head in range(heads)
    ]
    key_sums = [jnp.zeros((rows, 2 * qk), f32) for _ in range(heads)]
    value_sums = [jnp.zeros((rows, DV), f32) for _ in range(heads)]
    for slot in range(count):
        allowed = (row_ref[slot : slot + 1, :] >= own_pos) & (
            row_ref[2 * count + slot : 2 * count + slot + 1, :] == own_doc
        )
        queries = read(slots[slot], None, slice(0, 2 * qk)).astype(bf16)
        last = grads[slot][-1]
        extra = last.shape[0] - (rows - sum(ref.shape[0] for ref in grads[slot][:-1]))
        base = last.shape[0] - extra
        for head in range(heads):
            near = 1.0 + dot_t(keys[head], queries)
            span = slice(head * DV, (head + 1) * DV)
            numer = read(grads[slot], slice(0, rows), span).astype(bf16)
            line, lane = base + (head * rows) // vw, (head * rows) % vw
            grad = dot_t(values[head], numer) + last[line : line + 1, lane : lane + rows]
            grad = jnp.where(allowed, grad * near, 0.0).astype(bf16)
            key_sums[head] = key_sums[head] + dot_n(grad, queries)
            score = jnp.where(allowed, 0.5 * near * near + 0.5, 0.0).astype(bf16)
            value_sums[head] = value_sums[head] + dot_n(score, numer)
    total = jnp.zeros((rows, 2 * qk), f32)
    for head in range(heads):
        total = jnp.where(head_lanes(rows, 2 * qk, head * FEAT), 0.25 * key_sums[head], total)
        value_ref[:, head * DV : (head + 1) * DV] = value_sums[head].astype(bf16)
    key_ref[...] = total[:, :qk].astype(bf16)


def whole_call(body, outs, *operands, flops=0):
    moved = sum(x.size * x.dtype.itemsize for x in (*operands, *outs))
    return pl.pallas_call(
        body,
        out_shape=outs,
        in_specs=[pl.BlockSpec(memory_space=pltpu.VMEM)] * len(operands),
        out_specs=jax.tree.map(lambda _: pl.BlockSpec(memory_space=pltpu.VMEM), outs),
        compiler_params=pltpu.CompilerParams(vmem_limit_bytes=VMEM_LIMIT),
        cost_estimate=pl.CostEstimate(flops=flops, bytes_accessed=moved, transcendentals=0),
    )(*operands)


def join_kernel(shape, scale_ref, *refs):
    slots, (out_ref,) = split_refs(refs, shape)
    step = pl.program_id(0)
    for slot in range(len(slots)):

        @pl.when(step == slot)
        def _():
            at = 0
            for ref in slots[slot]:
                out_ref[at : at + ref.shape[0], :] = (ref[...] * scale_ref[...]).astype(bf16)
                at += ref.shape[0]


def join_rounded(slots, scale):
    parts = [part for slot in slots for part in slot]
    rows, width = sum(part.shape[0] for part in slots[0]), parts[0].shape[1]
    count = len(slots)
    return pl.pallas_call(
        functools.partial(join_kernel, tuple(len(slot) for slot in slots)),
        grid=(count,),
        out_shape=jax.ShapeDtypeStruct((count * rows, width), bf16),
        in_specs=[pl.BlockSpec((1, width), lambda i: (0, 0))]
        + [
            pl.BlockSpec(part.shape, lambda i: (0, 0), pipeline_mode=pl.Buffered(1))
            for part in parts
        ],
        out_specs=pl.BlockSpec((rows, width), lambda i: (i, 0)),
        compiler_params=pltpu.CompilerParams(vmem_limit_bytes=VMEM_LIMIT),
        cost_estimate=pl.CostEstimate(
            flops=0, bytes_accessed=6 * count * rows * width, transcendentals=0
        ),
    )(scale[None, :], *parts)


def norm_back(grad_out, values, inverse, gain):
    scaled = grad_out * gain
    return inverse * (
        scaled - values * inverse * inverse * jnp.mean(scaled * values, axis=-1, keepdims=True)
    )


def mm(left, right):
    return jnp.dot(left, right, preferred_element_type=f32)


def mm_t(left, right):
    return jnp.einsum("ac,bc->ab", left, right, preferred_element_type=f32)


def t_mm(left, right):
    return jnp.einsum("ca,cb->ab", left, right, preferred_element_type=f32)


def gated(gate, up_lin, hidden_grad):
    sigmoid = 0.5 + 0.5 * jnp.tanh(0.5 * gate)
    silu = gate * sigmoid
    return (
        (silu * up_lin).astype(bf16),
        (hidden_grad * up_lin * sigmoid * (1.0 + gate * (1.0 - sigmoid))).astype(bf16),
        (hidden_grad * silu).astype(bf16),
    )


def per_device(
    tokens,
    gain_attn,
    w_query,
    w_key,
    w_value,
    w_out,
    gain_mlp,
    w_gate,
    w_up,
    w_down,
    doc_lengths,
    cotangent,
):
    rows, width = tokens.shape
    heads = w_query.shape[1] // FEAT
    qk, vw = heads * FEAT, heads * DV
    blk_index, blk_count = lax.axis_index("blk"), lax.axis_size("blk")

    ends = [doc_lengths[0]]
    for doc in range(1, doc_lengths.shape[0]):
        ends.append(ends[-1] + doc_lengths[doc])

    def layout(positions):
        docs = sum((positions >= end).astype(jnp.int32) for end in ends[:-1])
        valid = positions < ends[-1]
        return docs, valid, jnp.where(valid, docs, -1)

    own_pos = blk_index * rows + jnp.arange(rows, dtype=jnp.int32)
    own_docs, own_valid, own_key_docs = layout(own_pos)
    columns = jnp.stack([own_pos, own_docs, own_valid.astype(jnp.int32), own_key_docs], axis=1)
    slot_blocks = blk_index ^ jnp.arange(blk_count, dtype=jnp.int32)
    slot_pos = slot_blocks[:, None] * rows + jnp.arange(rows, dtype=jnp.int32)[None, :]
    slot_docs, _, slot_key_docs = layout(slot_pos)
    lines = jnp.concatenate([slot_pos, slot_key_docs, slot_docs])

    gain_one, gain_two = gain_attn.astype(f32), gain_mlp.astype(f32)
    token_wide, cot_wide = tokens.astype(f32), cotangent.astype(f32)
    inv_in = lax.rsqrt(jnp.mean(token_wide * token_wide, axis=-1, keepdims=True) + epsilon)
    normed_in = (token_wide * inv_in * gain_one).astype(bf16)
    qkv_own = jnp.concatenate(
        [mm(normed_in, w_query), mm(normed_in, w_key), mm(normed_in, w_value)], axis=1
    )
    qkv = gather_blk(qkv_own)
    shape = tuple(len(slot) for slot in qkv)
    qkv_parts = [part for slot in qkv for part in slot]

    cost = 8 * rows * rows * blk_count * vw
    attended, mean, inverse = whole_call(
        functools.partial(attend_kernel, heads, shape),
        (
            jax.ShapeDtypeStruct((rows, vw), bf16),
            jax.ShapeDtypeStruct((rows, vw), f32),
            jax.ShapeDtypeStruct((rows, vw), f32),
        ),
        columns,
        lines,
        *qkv_parts,
        flops=cost,
    )
    attn_part = mm(attended, w_out)
    attn_sum = sum_head(attn_part)
    order = [0, 1, 2, 4, 3, 5, 6, 7] if blk_count == 8 else list(range(blk_count))
    early, late = order[: blk_count // 2], order[blk_count // 2 :]
    ones = jnp.ones_like(gain_two)
    convoy = Convoy()

    def ready(chain, slots, wanted):
        while not all(slot in slots for slot in wanted):
            convoy.wave([chain])
        return [slots[slot] for slot in wanted]

    def cot_work(*slots):
        rows_of = join_rounded(slots, ones)
        return rows_of, mm_t(rows_of, w_down)

    def gate_work(*slots):
        rows_of = join_rounded(slots, gain_two)
        return rows_of, mm(rows_of, w_gate)

    def up_work(rows_of, gate, hidden_grad):
        return gated(gate, mm(rows_of, w_up), hidden_grad)

    cot_slots = {}
    cot = Chain(gather_steps(after(cot_wide, qkv[-2]), cot_slots))
    own_hidden_grad = convoy.wave(
        [cot], lambda left, _: mm_t(left, w_down), cotangent, attn_part
    )
    cot_early = ready(cot, cot_slots, early)
    convoy.launch(cot)
    cot_a, hidden_grad_a = convoy.work(cot_work, *cot_early)
    resid_mid = after(token_wide, convoy.done) + attn_sum
    inv_mid = lax.rsqrt(jnp.mean(resid_mid * resid_mid, axis=-1, keepdims=True) + epsilon)
    scaled_mid = resid_mid * inv_mid
    convoy.done = scaled_mid
    convoy.land(cot)
    mid_slots = {}
    mid = Chain(gather_steps(scaled_mid, mid_slots))

    def middle(scaled_mid):
        normed_mid = (scaled_mid * gain_two).astype(bf16)
        hidden, gate_lin_grad, up_lin_grad = gated(
            mm(normed_mid, w_gate), mm(normed_mid, w_up), own_hidden_grad
        )
        return hidden, mm_t(gate_lin_grad, w_gate) + mm_t(up_lin_grad, w_up)

    convoy.launch(mid, cot)
    hidden, mid_part = convoy.work(middle, scaled_mid)
    convoy.land(cot)
    mid_sum = sum_head(mid_part)

    def share_work(hidden, *slots):
        mlp_part = mm(hidden, w_down)
        return mlp_part, *cot_work(*after(slots, mlp_part))

    mlp_part, cot_b, hidden_grad_b = convoy.work(
        share_work, hidden, *ready(cot, cot_slots, late)
    )
    mlp = Chain(line_steps(mlp_part, 2))
    convoy.land(mid)
    mid_early = ready(mid, mid_slots, early)
    convoy.launch(mid)
    mid_a, gate_a = convoy.work(gate_work, *mid_early)
    hidden_a, gate_grad_a, up_grad_a = convoy.work(
        up_work, after(mid_a, convoy.done), gate_a, hidden_grad_a
    )
    down_a = convoy.work(t_mm, after(hidden_a, convoy.done), cot_a)
    mid_grad = after(mid_sum, down_a)

    resid_grad = cot_wide + norm_back(mid_grad, resid_mid, inv_mid, gain_two)
    out_lin_grad = resid_grad.astype(bf16)
    attended_grad = mm_t(out_lin_grad, w_out)
    numer_grad = attended_grad * inverse
    denom_grad = -jnp.sum((numer_grad * mean).reshape(rows, heads, DV), axis=-1)
    denom_lines = denom_grad.T.reshape(rows // DV, vw)
    denom_lines = jnp.pad(denom_lines, ((0, -denom_lines.shape[0] % 8), (0, 0)))
    sent = jnp.concatenate([numer_grad, denom_lines])
    convoy.done = sent
    convoy.land(mid)
    grad_slots = {}
    grads = Chain(gather_steps(sent, grad_slots))

    def query_work(numer_grad, denom_grad, out_lin_grad):
        (query_lin_grad,) = whole_call(
            functools.partial(query_kernel, heads, shape),
            (jax.ShapeDtypeStruct((rows, qk), bf16),),
            columns,
            lines,
            numer_grad,
            jnp.repeat(denom_grad, DV, axis=1),
            *qkv_parts,
            flops=cost,
        )
        return query_lin_grad, t_mm(attended, after(out_lin_grad, query_lin_grad))

    convoy.launch(grads, mlp)
    query_lin_grad, out_part = convoy.work(query_work, numer_grad, denom_grad, out_lin_grad)
    convoy.land(grads)
    gate_part = convoy.wave([grads], t_mm, mid_a, gate_grad_a)
    convoy.launch(grads)
    convoy.land(grads, mlp)
    convoy.finish(grads)
    grad_slots = [grad_slots[slot] for slot in range(blk_count)]
    grad_shape = tuple(len(slot) for slot in grad_slots)

    def key_work(query_lin_grad, grad_parts):
        key_lin_grad, value_grad = whole_call(
            functools.partial(key_kernel, heads, shape, grad_shape),
            (jax.ShapeDtypeStruct((rows, qk), bf16), jax.ShapeDtypeStruct((rows, vw), bf16)),
            columns,
            lines,
            *qkv_parts,
            *grad_parts,
            flops=2 * cost,
        )
        in_part = mm_t(query_lin_grad, w_query) + mm_t(key_lin_grad, w_key)
        in_part = in_part + mm_t(value_grad, w_value)
        return in_part, query_lin_grad, key_lin_grad, value_grad

    grad_parts = [part for slot in grad_slots for part in slot]
    convoy.launch(mid, mlp)
    in_part, *lin_grads = convoy.work(key_work, query_lin_grad, grad_parts)
    convoy.land(mid)
    mid_late = ready(mid, mid_slots, late)

    in_sum = Chain(line_steps(in_part, 2))
    convoy.launch(in_sum)
    late_in = after(normed_in, convoy.sent)
    parts = [t_mm(late_in, grad) for grad in lin_grads]
    gain_parts = jnp.stack(
        [
            jnp.sum(after(in_part, parts) * token_wide * inv_in, axis=0),
            jnp.sum(mid_part * scaled_mid, axis=0),
        ]
    )
    *qkv_w_grads, out_w_grad = lax.psum((*parts, out_part), "blk")
    gains = Chain(small_steps(gain_parts))
    convoy.launch(gains)
    chains = [in_sum, gains, mlp]
    mid_b, gate_b = convoy.work(gate_work, *after(mid_late, gain_parts))
    convoy.land(*chains)

    def second_work(mid_b, gate_b, hidden_grad_b):
        parts = up_work(mid_b, gate_b, hidden_grad_b)
        return (*parts, t_mm(mid_a, after(up_grad_a, parts)))

    hidden_b, gate_grad_b, up_grad_b, up_part = convoy.wave(
        chains, second_work, mid_b, gate_b, hidden_grad_b
    )
    down_w_grad = convoy.wave(chains, lambda x, y: down_a + t_mm(x, y), hidden_b, cot_b)
    convoy.finish(mlp)

    def gate_last(gate_grad_b, mlp_sum):
        output = (resid_mid + mlp_sum).astype(bf16)
        return gate_part + t_mm(mid_b, after(gate_grad_b, output)), output

    chains = [in_sum, gains]
    convoy.launch(*chains)
    gate_w_grad, output = convoy.work(gate_last, gate_grad_b, mlp.result)
    up_w_grad = convoy.work(
        lambda x: up_part + t_mm(mid_b, x), after(up_grad_b, gate_w_grad)
    )
    convoy.land(*chains)
    while any(chain.due for chain in chains):
        convoy.wave(chains)
    in_grad, gain_grads = (chain.result for chain in chains)
    in_grad = after(in_grad, qkv_w_grads, out_w_grad)
    input_grad = resid_grad + norm_back(in_grad, token_wide, inv_in, gain_one)
    return (
        output,
        input_grad,
        gain_grads[0],
        *qkv_w_grads,
        out_w_grad,
        gain_grads[1],
        gate_w_grad,
        up_w_grad,
        down_w_grad,
    )


def solution(mesh):
    in_specs = (
        P("blk", None),
        P(),
        P(None, "head"),
        P(None, "head"),
        P(None, "head"),
        P("head", None),
        P(),
        P(None, "head"),
        P(None, "head"),
        P("head", None),
        P(),
        P("blk", None),
    )
    out_specs = (
        P("blk", None),
        P("blk", None),
        P(),
        P(None, "head"),
        P(None, "head"),
        P(None, "head"),
        P("head", None),
        P(),
        P(None, "head"),
        P(None, "head"),
        P("head", None),
    )
    return jax.shard_map(
        per_device, mesh=mesh, in_specs=in_specs, out_specs=out_specs, check_vma=False
    )
```

```python
import functools

import jax
import jax.numpy as jnp
from jax import lax
from jax.experimental import pallas as pl
from jax.experimental.pallas import tpu as pltpu
from jax.sharding import PartitionSpec as P

FEAT = 16
DV = 128

epsilon = 1e-05
f32, bf16 = jnp.float32, jnp.bfloat16
VMEM_LIMIT = 56 * 1024 * 1024


def hop(value, axis, way):
    if isinstance(way, int):
        way = [(i, i ^ way) for i in range(lax.axis_size(axis))]
    return lax.ppermute(value, axis, way)


def after(value, *others):
    return lax.optimization_barrier((value, others))[0]


def gather_blk(value):
    count = lax.axis_size("blk")
    if count != 8:
        slots, bit = [value], 1
        while bit < count:
            slots = slots + [hop(slot, "blk", bit) for slot in slots]
            bit *= 2
        return [[slot] for slot in slots]
    half = value.shape[0] // 16 * 8
    low, high = value[:half], value[half:]
    x_low, y_high = hop(low, "blk", 2), hop(high, "blk", 4)
    x_high, y_low = hop(high, "blk", 2), hop(low, "blk", 4)
    own_pair = hop(value, "blk", 1)
    far_low, far_high = hop(x_low, "blk", 4), hop(y_high, "blk", 2)
    slots = [[value], [own_pair]]
    for slot in ([x_low, x_high], [y_low, y_high], [far_low, far_high]):
        slots += [slot, [hop(part, "blk", 1) for part in slot]]
    return slots


class Chain:
    def __init__(self, steps):
        self.steps, self.result, self.flying = steps, None, None
        self.advance(None)

    def advance(self, values):
        try:
            self.due = self.steps.send(values)
        except StopIteration as end:
            self.due, self.result = [], end.value


class Convoy:
    def __init__(self):
        self.landed, self.sent, self.done = (), (), ()

    def launch(self, *chains):
        for chain in chains:
            if chain.due:
                values = after([value for value, _, _ in chain.due], self.landed, self.sent)
                chain.flying = [
                    hop(value, axis, way) for value, (_, axis, way) in zip(values, chain.due)
                ]
                self.sent = (self.sent, values)

    def work(self, work, *operands):
        self.done = work(*after(operands, self.sent, self.landed))
        return self.done

    def land(self, *chains):
        chains = [chain for chain in chains if chain.flying is not None]
        came = after([chain.flying for chain in chains], self.done)
        self.landed, self.sent = (came, self.done), ()
        for chain, values in zip(chains, came):
            chain.flying = None
            chain.advance(values)

    def wave(self, chains, work=None, *operands):
        self.launch(*chains)
        result = None if work is None else self.work(work, *operands)
        self.land(*chains)
        return result

    def finish(self, chain):
        while chain.due:
            self.wave([chain])


def gather_steps(value, slots):
    count = lax.axis_size("blk")
    slots[0] = [value]
    if count != 8:
        bit = 1
        while bit < count:
            got = yield [(slots[slot][0], "blk", bit) for slot in range(bit)]
            slots.update({bit + slot: [part] for slot, part in enumerate(got)})
            bit *= 2
        return
    half = value.shape[0] // 16 * 8
    x_all, y_all, own_pair = yield [(value, "blk", way) for way in (2, 4, 1)]
    slots[1], slots[2], slots[4] = [own_pair], [x_all], [y_all]
    *slots[6], x_pair, y_pair = yield [
        (x_all[:half], "blk", 4),
        (y_all[half:], "blk", 2),
        (x_all, "blk", 1),
        (y_all, "blk", 1),
    ]
    slots[3], slots[5] = [x_pair], [y_pair]
    slots[7] = yield [(part, "blk", 1) for part in slots[6]]


def small_steps(value):
    for axis in ("head", "blk"):
        bit = 1
        while bit < lax.axis_size(axis):
            ways = [bit]
            if axis == "blk" and bit == 2 and lax.axis_size(axis) == 8:
                ways = [2, 4, 6]
            for got in (yield [(value, axis, way) for way in ways]):
                value = value + got
            bit *= 2 * len(ways)
    return value


def head_share(value, step=0):
    rows = value.shape[0] // lax.axis_size("head")
    return lax.dynamic_slice_in_dim(value, (lax.axis_index("head") ^ step) * rows, rows)


def head_steps(value, finish=None):
    count, mine = lax.axis_size("head"), lax.axis_index("head")
    got = yield [(head_share(value, step), "head", step) for step in range(1, count)]
    total = head_share(value)
    for part in got:
        total = total + part
    total = total if finish is None else finish(total)
    got = yield [(total, "head", step) for step in range(1, count)]
    whole = jnp.zeros_like(value)
    for step, part in enumerate([total, *got]):
        whole = lax.dynamic_update_slice_in_dim(whole, part, (mine ^ step) * part.shape[0], 0)
    return whole


def line_steps(value, pieces):
    if lax.axis_size("head") != 4:
        return (yield from head_steps(value))
    mine = lax.axis_index("head")
    inner = (mine == 1) | (mine == 2)
    parts = jnp.split(value, pieces)
    pairs, whole, done = {}, {}, {}
    for wave in range(pieces + 2):
        sends, takes = [], []
        if wave < pieces:
            sends.append((parts[wave], "head", [(0, 1), (3, 2)]))
            takes.append((pairs, wave, parts))
        if 0 <= wave - 1 < pieces:
            sends.append((pairs[wave - 1], "head", [(1, 2), (2, 1)]))
            takes.append((whole, wave - 1, pairs))
        if 0 <= wave - 2:
            sends.append((whole[wave - 2], "head", [(1, 0), (2, 3)]))
            takes.append((done, wave - 2, whole))
        got = yield sends
        for part, (into, piece, own) in zip(got, takes):
            if into is done:
                into[piece] = jnp.where(inner, own[piece], part)
            else:
                into[piece] = own[piece] + part
    return jnp.concatenate([done[piece] for piece in range(pieces)])


def sum_head(value):
    return lax.psum(value, "head")


def dot_t(left, right):
    return lax.dot_general(left, right, (((1,), (1,)), ((), ())), preferred_element_type=f32)


def dot_n(left, right):
    return lax.dot_general(left, right, (((1,), (0,)), ((), ())), preferred_element_type=f32)


def head_lanes(rows, width, first):
    lanes = lax.broadcasted_iota(jnp.int32, (rows, width), 1)
    return (lanes >= first) & (lanes < first + FEAT)


def read(slot, lines, lanes):
    parts = [ref[:, lanes] for ref in slot]
    whole = parts[0] if len(parts) == 1 else jnp.concatenate(parts)
    return whole if lines is None else whole[lines]


def split_refs(refs, shape):
    slots, at = [], 0
    for pieces in shape:
        slots.append(refs[at : at + pieces])
        at += pieces
    return slots, refs[at:]


def turned(tile, heads, use_key):
    rows, width = tile.shape
    moved = jnp.concatenate([tile[:, width // 2 :], tile[:, : width // 2]], axis=1)
    base = 0 if use_key else width // 2
    scaled = moved * 0.25
    return [
        jnp.where(head_lanes(rows, width, base + head * FEAT), scaled, 0.0).astype(bf16)
        for head in range(heads)
    ]


def attend_kernel(heads, shape, col_ref, row_ref, *refs):
    slots, (att_ref, mean_ref, inverse_ref) = split_refs(refs, shape)
    count = len(slots)
    rows = col_ref.shape[0]
    qk = heads * FEAT
    own_pos, own_doc = col_ref[:, 0:1], col_ref[:, 1:2]
    valid = col_ref[:, 2:3].astype(f32)
    numer = [jnp.zeros((rows, DV), f32) for _ in range(heads)]
    denom = [jnp.zeros((rows, 1), f32) for _ in range(heads)]
    queries = turned(read(slots[0], None, slice(0, 2 * qk)), heads, False)
    for slot in range(count):
        allowed = (row_ref[slot : slot + 1, :] <= own_pos) & (
            row_ref[count + slot : count + slot + 1, :] == own_doc
        )
        keys = read(slots[slot], None, slice(0, 2 * qk)).astype(bf16)
        for head in range(heads):
            near = 1.0 + dot_t(queries[head], keys)
            score = jnp.where(allowed, 0.5 * near * near + 0.5, 0.0)
            first = 2 * qk + head * DV
            value = read(slots[slot], None, slice(first, first + DV)).astype(bf16)
            numer[head] = numer[head] + dot_n(score.astype(bf16), value)
            denom[head] = denom[head] + jnp.sum(score, axis=1, keepdims=True)
    for head in range(heads):
        span = slice(head * DV, (head + 1) * DV)
        mean = numer[head] / denom[head]
        att_ref[:, span] = (valid * mean).astype(bf16)
        mean_ref[:, span] = mean
        inverse_ref[:, span] = jnp.broadcast_to(valid / denom[head], (rows, DV))


def query_kernel(heads, shape, col_ref, row_ref, numer_ref, denom_ref, *refs):
    slots, (out_ref,) = split_refs(refs, shape)
    count = len(slots)
    rows = col_ref.shape[0]
    qk = heads * FEAT
    own_pos, own_doc = col_ref[:, 0:1], col_ref[:, 1:2]
    queries = turned(read(slots[0], None, slice(0, 2 * qk)), heads, False)
    sums = [jnp.zeros((rows, 2 * qk), f32) for _ in range(heads)]
    for slot in range(count):
        allowed = (row_ref[slot : slot + 1, :] <= own_pos) & (
            row_ref[count + slot : count + slot + 1, :] == own_doc
        )
        keys = read(slots[slot], None, slice(0, 2 * qk)).astype(bf16)
        for head in range(heads):
            near = 1.0 + dot_t(queries[head], keys)
            first = 2 * qk + head * DV
            value = read(slots[slot], None, slice(first, first + DV)).astype(bf16)
            grad = dot_t(numer_ref[:, head * DV : (head + 1) * DV].astype(bf16), value)
            grad = grad + denom_ref[:, head * DV : head * DV + 1]
            grad = jnp.where(allowed, grad * near, 0.0).astype(bf16)
            sums[head] = sums[head] + dot_n(grad, keys)
    total = jnp.zeros((rows, 2 * qk), f32)
    for head in range(heads):
        total = jnp.where(head_lanes(rows, 2 * qk, qk + head * FEAT), 0.25 * sums[head], total)
    out_ref[...] = total[:, qk:].astype(bf16)


def key_kernel(heads, shape, grad_shape, col_ref, row_ref, *refs):
    slots, rest = split_refs(refs, shape)
    grads, (key_ref, value_ref) = split_refs(rest, grad_shape)
    count = len(slots)
    rows = col_ref.shape[0]
    qk, vw = heads * FEAT, heads * DV
    own_pos, own_doc = col_ref[:, 0:1], col_ref[:, 3:4]
    keys = turned(read(slots[0], None, slice(0, 2 * qk)), heads, True)
    values = [
        read(slots[0], None, slice(2 * qk + head * DV, 2 * qk + (head + 1) * DV)).astype(bf16)
        for head in range(heads)
    ]
    key_sums = [jnp.zeros((rows, 2 * qk), f32) for _ in range(heads)]
    value_sums = [jnp.zeros((rows, DV), f32) for _ in range(heads)]
    for slot in range(count):
        allowed = (row_ref[slot : slot + 1, :] >= own_pos) & (
            row_ref[2 * count + slot : 2 * count + slot + 1, :] == own_doc
        )
        queries = read(slots[slot], None, slice(0, 2 * qk)).astype(bf16)
        last = grads[slot][-1]
        extra = last.shape[0] - (rows - sum(ref.shape[0] for ref in grads[slot][:-1]))
        base = last.shape[0] - extra
        for head in range(heads):
            near = 1.0 + dot_t(keys[head], queries)
            span = slice(head * DV, (head + 1) * DV)
            numer = read(grads[slot], slice(0, rows), span).astype(bf16)
            line, lane = base + (head * rows) // vw, (head * rows) % vw
            grad = dot_t(values[head], numer) + last[line : line + 1, lane : lane + rows]
            grad = jnp.where(allowed, grad * near, 0.0).astype(bf16)
            key_sums[head] = key_sums[head] + dot_n(grad, queries)
            score = jnp.where(allowed, 0.5 * near * near + 0.5, 0.0).astype(bf16)
            value_sums[head] = value_sums[head] + dot_n(score, numer)
    total = jnp.zeros((rows, 2 * qk), f32)
    for head in range(heads):
        total = jnp.where(head_lanes(rows, 2 * qk, head * FEAT), 0.25 * key_sums[head], total)
        value_ref[:, head * DV : (head + 1) * DV] = value_sums[head].astype(bf16)
    key_ref[...] = total[:, :qk].astype(bf16)


def whole_call(body, outs, *operands, flops=0):
    moved = sum(x.size * x.dtype.itemsize for x in (*operands, *outs))
    return pl.pallas_call(
        body,
        out_shape=outs,
        in_specs=[pl.BlockSpec(memory_space=pltpu.VMEM)] * len(operands),
        out_specs=jax.tree.map(lambda _: pl.BlockSpec(memory_space=pltpu.VMEM), outs),
        compiler_params=pltpu.CompilerParams(vmem_limit_bytes=VMEM_LIMIT),
        cost_estimate=pl.CostEstimate(flops=flops, bytes_accessed=moved, transcendentals=0),
    )(*operands)


def join_kernel(shape, scale_ref, *refs):
    slots, (out_ref,) = split_refs(refs, shape)
    step = pl.program_id(0)
    for slot in range(len(slots)):

        @pl.when(step == slot)
        def _():
            at = 0
            for ref in slots[slot]:
                out_ref[at : at + ref.shape[0], :] = (ref[...] * scale_ref[...]).astype(bf16)
                at += ref.shape[0]


def join_rounded(slots, scale):
    parts = [part for slot in slots for part in slot]
    rows, width = sum(part.shape[0] for part in slots[0]), parts[0].shape[1]
    count = len(slots)
    return pl.pallas_call(
        functools.partial(join_kernel, tuple(len(slot) for slot in slots)),
        grid=(count,),
        out_shape=jax.ShapeDtypeStruct((count * rows, width), bf16),
        in_specs=[pl.BlockSpec((1, width), lambda i: (0, 0))]
        + [
            pl.BlockSpec(part.shape, lambda i: (0, 0), pipeline_mode=pl.Buffered(1))
            for part in parts
        ],
        out_specs=pl.BlockSpec((rows, width), lambda i: (i, 0)),
        compiler_params=pltpu.CompilerParams(vmem_limit_bytes=VMEM_LIMIT),
        cost_estimate=pl.CostEstimate(
            flops=0, bytes_accessed=6 * count * rows * width, transcendentals=0
        ),
    )(scale[None, :], *parts)


def norm_back(grad_out, values, inverse, gain):
    scaled = grad_out * gain
    return inverse * (
        scaled - values * inverse * inverse * jnp.mean(scaled * values, axis=-1, keepdims=True)
    )


def mm(left, right):
    return jnp.dot(left, right, preferred_element_type=f32)


def mm_t(left, right):
    return jnp.einsum("ac,bc->ab", left, right, preferred_element_type=f32)


def t_mm(left, right):
    return jnp.einsum("ca,cb->ab", left, right, preferred_element_type=f32)


def gated(gate, up_lin, hidden_grad):
    sigmoid = 0.5 + 0.5 * jnp.tanh(0.5 * gate)
    silu = gate * sigmoid
    return (
        (silu * up_lin).astype(bf16),
        (hidden_grad * up_lin * sigmoid * (1.0 + gate * (1.0 - sigmoid))).astype(bf16),
        (hidden_grad * silu).astype(bf16),
    )


def per_device(
    tokens,
    gain_attn,
    w_query,
    w_key,
    w_value,
    w_out,
    gain_mlp,
    w_gate,
    w_up,
    w_down,
    doc_lengths,
    cotangent,
):
    rows, width = tokens.shape
    heads = w_query.shape[1] // FEAT
    qk, vw = heads * FEAT, heads * DV
    blk_index, blk_count = lax.axis_index("blk"), lax.axis_size("blk")

    ends = [doc_lengths[0]]
    for doc in range(1, doc_lengths.shape[0]):
        ends.append(ends[-1] + doc_lengths[doc])

    def layout(positions):
        docs = sum((positions >= end).astype(jnp.int32) for end in ends[:-1])
        valid = positions < ends[-1]
        return docs, valid, jnp.where(valid, docs, -1)

    own_pos = blk_index * rows + jnp.arange(rows, dtype=jnp.int32)
    own_docs, own_valid, own_key_docs = layout(own_pos)
    columns = jnp.stack([own_pos, own_docs, own_valid.astype(jnp.int32), own_key_docs], axis=1)
    slot_blocks = blk_index ^ jnp.arange(blk_count, dtype=jnp.int32)
    slot_pos = slot_blocks[:, None] * rows + jnp.arange(rows, dtype=jnp.int32)[None, :]
    slot_docs, _, slot_key_docs = layout(slot_pos)
    lines = jnp.concatenate([slot_pos, slot_key_docs, slot_docs])

    gain_one, gain_two = gain_attn.astype(f32), gain_mlp.astype(f32)
    token_wide, cot_wide = tokens.astype(f32), cotangent.astype(f32)
    inv_in = lax.rsqrt(jnp.mean(token_wide * token_wide, axis=-1, keepdims=True) + epsilon)
    normed_in = (token_wide * inv_in * gain_one).astype(bf16)
    qkv_own = jnp.concatenate(
        [mm(normed_in, w_query), mm(normed_in, w_key), mm(normed_in, w_value)], axis=1
    )
    qkv = gather_blk(qkv_own)
    shape = tuple(len(slot) for slot in qkv)
    qkv_parts = [part for slot in qkv for part in slot]

    cost = 8 * rows * rows * blk_count * vw
    attended, mean, inverse = whole_call(
        functools.partial(attend_kernel, heads, shape),
        (
            jax.ShapeDtypeStruct((rows, vw), bf16),
            jax.ShapeDtypeStruct((rows, vw), f32),
            jax.ShapeDtypeStruct((rows, vw), f32),
        ),
        columns,
        lines,
        *qkv_parts,
        flops=cost,
    )
    attn_part = mm(attended, w_out)
    attn_sum = sum_head(attn_part)
    order = [0, 1, 2, 4, 3, 5, 6, 7] if blk_count == 8 else list(range(blk_count))
    early, late = order[: blk_count // 2], order[blk_count // 2 :]
    ones = jnp.ones_like(gain_two)
    convoy = Convoy()

    def ready(chain, slots, wanted):
        while not all(slot in slots for slot in wanted):
            convoy.wave([chain])
        return [slots[slot] for slot in wanted]

    def cot_work(*slots):
        rows_of = join_rounded(slots, ones)
        return rows_of, mm_t(rows_of, w_down)

    def gate_work(*slots):
        rows_of = join_rounded(slots, gain_two)
        return rows_of, mm(rows_of, w_gate)

    def up_work(rows_of, gate, hidden_grad):
        return gated(gate, mm(rows_of, w_up), hidden_grad)

    cot_slots = {}
    cot = Chain(gather_steps(after(cot_wide, qkv[-2]), cot_slots))
    own_hidden_grad = convoy.wave(
        [cot], lambda left, _: mm_t(left, w_down), cotangent, attn_part
    )
    cot_early = ready(cot, cot_slots, early)
    convoy.launch(cot)
    cot_a, hidden_grad_a = convoy.work(cot_work, *cot_early)
    resid_mid = after(token_wide, convoy.done) + attn_sum
    inv_mid = lax.rsqrt(jnp.mean(resid_mid * resid_mid, axis=-1, keepdims=True) + epsilon)
    scaled_mid = resid_mid * inv_mid
    convoy.done = scaled_mid
    convoy.land(cot)
    mid_slots = {}
    mid = Chain(gather_steps(scaled_mid, mid_slots))

    def middle(scaled_mid):
        normed_mid = (scaled_mid * gain_two).astype(bf16)
        hidden, gate_lin_grad, up_lin_grad = gated(
            mm(normed_mid, w_gate), mm(normed_mid, w_up), own_hidden_grad
        )
        return hidden, mm_t(gate_lin_grad, w_gate) + mm_t(up_lin_grad, w_up)

    convoy.launch(mid, cot)
    hidden, mid_part = convoy.work(middle, scaled_mid)
    convoy.land(cot)
    mid_sum = sum_head(mid_part)

    def share_work(hidden, *slots):
        mlp_part = mm(hidden, w_down)
        return mlp_part, *cot_work(*after(slots, mlp_part))

    mlp_part, cot_b, hidden_grad_b = convoy.work(
        share_work, hidden, *ready(cot, cot_slots, late)
    )
    mlp = Chain(line_steps(mlp_part, 2))
    convoy.land(mid)
    mid_early = ready(mid, mid_slots, early)
    convoy.launch(mid)
    mid_a, gate_a = convoy.work(gate_work, *mid_early)
    hidden_a, gate_grad_a, up_grad_a = convoy.work(
        up_work, after(mid_a, convoy.done), gate_a, hidden_grad_a
    )
    down_a = convoy.work(t_mm, after(hidden_a, convoy.done), cot_a)
    mid_grad = after(mid_sum, down_a)

    resid_grad = cot_wide + norm_back(mid_grad, resid_mid, inv_mid, gain_two)
    out_lin_grad = resid_grad.astype(bf16)
    attended_grad = mm_t(out_lin_grad, w_out)
    numer_grad = attended_grad * inverse
    denom_grad = -jnp.sum((numer_grad * mean).reshape(rows, heads, DV), axis=-1)
    denom_lines = denom_grad.T.reshape(rows // DV, vw)
    denom_lines = jnp.pad(denom_lines, ((0, -denom_lines.shape[0] % 8), (0, 0)))
    sent = jnp.concatenate([numer_grad, denom_lines])
    convoy.done = sent
    convoy.land(mid)
    grad_slots = {}
    grads = Chain(gather_steps(sent, grad_slots))

    def query_work(numer_grad, denom_grad, out_lin_grad):
        (query_lin_grad,) = whole_call(
            functools.partial(query_kernel, heads, shape),
            (jax.ShapeDtypeStruct((rows, qk), bf16),),
            columns,
            lines,
            numer_grad,
            jnp.repeat(denom_grad, DV, axis=1),
            *qkv_parts,
            flops=cost,
        )
        return query_lin_grad, t_mm(attended, after(out_lin_grad, query_lin_grad))

    convoy.launch(grads, mlp)
    query_lin_grad, out_part = convoy.work(query_work, numer_grad, denom_grad, out_lin_grad)
    convoy.land(grads)
    gate_part = convoy.wave([grads], t_mm, mid_a, gate_grad_a)
    convoy.launch(grads)
    convoy.land(grads, mlp)
    convoy.finish(grads)
    grad_slots = [grad_slots[slot] for slot in range(blk_count)]
    grad_shape = tuple(len(slot) for slot in grad_slots)

    def key_work(query_lin_grad, grad_parts):
        key_lin_grad, value_grad = whole_call(
            functools.partial(key_kernel, heads, shape, grad_shape),
            (jax.ShapeDtypeStruct((rows, qk), bf16), jax.ShapeDtypeStruct((rows, vw), bf16)),
            columns,
            lines,
            *qkv_parts,
            *grad_parts,
            flops=2 * cost,
        )
        in_part = mm_t(query_lin_grad, w_query) + mm_t(key_lin_grad, w_key)
        in_part = in_part + mm_t(value_grad, w_value)
        return in_part, query_lin_grad, key_lin_grad, value_grad

    grad_parts = [part for slot in grad_slots for part in slot]
    convoy.launch(mid, mlp)
    in_part, *lin_grads = convoy.work(key_work, query_lin_grad, grad_parts)
    convoy.land(mid)
    mid_late = ready(mid, mid_slots, late)

    in_sum = Chain(line_steps(in_part, 2))
    convoy.launch(in_sum)

    def parts_work(normed_in, *lin_grads):
        return [t_mm(normed_in, grad) for grad in lin_grads]

    parts = convoy.work(parts_work, normed_in, *lin_grads)
    *qkv_w_grads, out_w_grad = lax.psum((*parts, out_part), "blk")
    gain_parts = jnp.stack(
        [
            jnp.sum(after(in_part, parts) * token_wide * inv_in, axis=0),
            jnp.sum(mid_part * scaled_mid, axis=0),
        ]
    )
    convoy.done = gain_parts
    convoy.land(mlp)
    gains = Chain(small_steps(gain_parts))
    convoy.launch(mlp, gains)
    chains = [in_sum, gains, mlp]
    mid_b, gate_b = convoy.work(gate_work, *mid_late)
    convoy.land(*chains)

    def second_work(mid_b, gate_b, hidden_grad_b):
        parts = up_work(mid_b, gate_b, hidden_grad_b)
        return (*parts, t_mm(mid_a, after(up_grad_a, parts)))

    hidden_b, gate_grad_b, up_grad_b, up_part = convoy.wave(
        chains, second_work, mid_b, gate_b, hidden_grad_b
    )
    down_w_grad = convoy.wave(chains, lambda x, y: down_a + t_mm(x, y), hidden_b, cot_b)
    convoy.finish(mlp)

    def gate_last(gate_grad_b, mlp_sum):
        output = (resid_mid + mlp_sum).astype(bf16)
        return gate_part + t_mm(mid_b, after(gate_grad_b, output)), output

    chains = [in_sum, gains]
    convoy.launch(*chains)
    gate_w_grad, output = convoy.work(gate_last, gate_grad_b, mlp.result)
    up_w_grad = convoy.work(
        lambda x: up_part + t_mm(mid_b, x), after(up_grad_b, gate_w_grad)
    )
    convoy.land(*chains)
    while any(chain.due for chain in chains):
        convoy.wave(chains)
    in_grad, gain_grads = (chain.result for chain in chains)
    in_grad = after(in_grad, qkv_w_grads, out_w_grad)
    input_grad = resid_grad + norm_back(in_grad, token_wide, inv_in, gain_one)
    return (
        output,
        input_grad,
        gain_grads[0],
        *qkv_w_grads,
        out_w_grad,
        gain_grads[1],
        gate_w_grad,
        up_w_grad,
        down_w_grad,
    )


def solution(mesh):
    in_specs = (
        P("blk", None),
        P(),
        P(None, "head"),
        P(None, "head"),
        P(None, "head"),
        P("head", None),
        P(),
        P(None, "head"),
        P(None, "head"),
        P("head", None),
        P(),
        P("blk", None),
    )
    out_specs = (
        P("blk", None),
        P("blk", None),
        P(),
        P(None, "head"),
        P(None, "head"),
        P(None, "head"),
        P("head", None),
        P(),
        P(None, "head"),
        P(None, "head"),
        P("head", None),
    )
    return jax.shard_map(
        per_device, mesh=mesh, in_specs=in_specs, out_specs=out_specs, check_vma=False
    )
```

```python
import functools

import jax
import jax.numpy as jnp
from jax import lax
from jax.experimental import pallas as pl
from jax.experimental.layout import Layout, with_layout_constraint
from jax.experimental.pallas import tpu as pltpu
from jax.sharding import PartitionSpec as P

FEAT = 16
DV = 128

epsilon = 1e-05
f32, bf16 = jnp.float32, jnp.bfloat16
VMEM_LIMIT = 56 * 1024 * 1024


def hop(value, axis, way):
    if isinstance(way, int):
        way = [(i, i ^ way) for i in range(lax.axis_size(axis))]
    return lax.ppermute(value, axis, way)


def after(value, *others):
    return lax.optimization_barrier((value, others))[0]


class Chain:
    def __init__(self, steps):
        self.steps, self.result, self.flying = steps, None, None
        self.advance(None)

    def advance(self, values):
        try:
            self.due = self.steps.send(values)
        except StopIteration as end:
            self.due, self.result = [], end.value


class Convoy:
    def __init__(self):
        self.landed, self.sent, self.done = (), (), ()

    def launch(self, *chains):
        for chain in chains:
            if chain.due:
                values = after([value for value, _, _ in chain.due], self.landed, self.sent)
                chain.flying = [
                    hop(value, axis, way) for value, (_, axis, way) in zip(values, chain.due)
                ]
                self.sent = (self.sent, values)

    def work(self, work, *operands):
        self.done = work(*after(operands, self.sent, self.landed))
        return self.done

    def land(self, *chains):
        chains = [chain for chain in chains if chain.flying is not None]
        came = after([chain.flying for chain in chains], self.done)
        self.landed, self.sent = (came, self.done), ()
        for chain, values in zip(chains, came):
            chain.flying = None
            chain.advance(values)

    def wave(self, chains, work=None, *operands):
        self.launch(*chains)
        result = None if work is None else self.work(work, *operands)
        self.land(*chains)
        return result

    def finish(self, chain):
        while chain.due:
            self.wave([chain])


def gather_steps(value, slots):
    count = lax.axis_size("blk")
    slots[0] = [value]
    if count != 8:
        bit = 1
        while bit < count:
            got = yield [(slots[slot][0], "blk", bit) for slot in range(bit)]
            slots.update({bit + slot: [part] for slot, part in enumerate(got)})
            bit *= 2
        return
    half = value.shape[0] // 16 * 8
    x_all, y_all, own_pair = yield [(value, "blk", way) for way in (2, 4, 1)]
    slots[1], slots[2], slots[4] = [own_pair], [x_all], [y_all]
    *slots[6], x_pair, y_pair = yield [
        (x_all[:half], "blk", 4),
        (y_all[half:], "blk", 2),
        (x_all, "blk", 1),
        (y_all, "blk", 1),
    ]
    slots[3], slots[5] = [x_pair], [y_pair]
    slots[7] = yield [(part, "blk", 1) for part in slots[6]]


def small_steps(value):
    for axis in ("head", "blk"):
        bit = 1
        while bit < lax.axis_size(axis):
            ways = [bit]
            if axis == "blk" and bit == 2 and lax.axis_size(axis) == 8:
                ways = [2, 4, 6]
            for got in (yield [(value, axis, way) for way in ways]):
                value = value + got
            bit *= 2 * len(ways)
    return value


def head_share(value, step=0):
    rows = value.shape[0] // lax.axis_size("head")
    return lax.dynamic_slice_in_dim(value, (lax.axis_index("head") ^ step) * rows, rows)


def head_steps(value, finish=None):
    count, mine = lax.axis_size("head"), lax.axis_index("head")
    got = yield [(head_share(value, step), "head", step) for step in range(1, count)]
    total = head_share(value)
    for part in got:
        total = total + part
    total = total if finish is None else finish(total)
    got = yield [(total, "head", step) for step in range(1, count)]
    whole = jnp.zeros_like(value)
    for step, part in enumerate([total, *got]):
        whole = lax.dynamic_update_slice_in_dim(whole, part, (mine ^ step) * part.shape[0], 0)
    return whole


def line_steps(value, pieces):
    if lax.axis_size("head") != 4:
        return (yield from head_steps(value))
    mine = lax.axis_index("head")
    inner = (mine == 1) | (mine == 2)
    parts = jnp.split(value, pieces)
    pairs, whole, done = {}, {}, {}
    for wave in range(pieces + 2):
        sends, takes = [], []
        if wave < pieces:
            sends.append((parts[wave], "head", [(0, 1), (3, 2)]))
            takes.append((pairs, wave, parts))
        if 0 <= wave - 1 < pieces:
            sends.append((pairs[wave - 1], "head", [(1, 2), (2, 1)]))
            takes.append((whole, wave - 1, pairs))
        if 0 <= wave - 2:
            sends.append((whole[wave - 2], "head", [(1, 0), (2, 3)]))
            takes.append((done, wave - 2, whole))
        got = yield sends
        for part, (into, piece, own) in zip(got, takes):
            if into is done:
                into[piece] = jnp.where(inner, own[piece], part)
            else:
                into[piece] = own[piece] + part
    return jnp.concatenate([done[piece] for piece in range(pieces)])


def sum_head(value):
    return lax.psum(value, "head")


def dot_t(left, right):
    return lax.dot_general(left, right, (((1,), (1,)), ((), ())), preferred_element_type=f32)


def dot_n(left, right):
    return lax.dot_general(left, right, (((1,), (0,)), ((), ())), preferred_element_type=f32)


def head_lanes(rows, width, first):
    lanes = lax.broadcasted_iota(jnp.int32, (rows, width), 1)
    return (lanes >= first) & (lanes < first + FEAT)


def read(slot, lines, lanes):
    parts = [ref[:, lanes] for ref in slot]
    whole = parts[0] if len(parts) == 1 else jnp.concatenate(parts)
    return whole if lines is None else whole[lines]


def split_refs(refs, shape):
    slots, at = [], 0
    for pieces in shape:
        slots.append(refs[at : at + pieces])
        at += pieces
    return slots, refs[at:]


def turned(tile, heads, use_key):
    rows, width = tile.shape
    moved = jnp.concatenate([tile[:, width // 2 :], tile[:, : width // 2]], axis=1)
    base = 0 if use_key else width // 2
    scaled = moved * 0.25
    return [
        jnp.where(head_lanes(rows, width, base + head * FEAT), scaled, 0.0).astype(bf16)
        for head in range(heads)
    ]


def attend_kernel(heads, shape, col_ref, row_ref, *refs):
    slots, (att_ref, mean_ref, inverse_ref) = split_refs(refs, shape)
    count = len(slots)
    rows = col_ref.shape[0]
    qk = heads * FEAT
    own_pos, own_doc = col_ref[:, 0:1], col_ref[:, 1:2]
    valid = col_ref[:, 2:3].astype(f32)
    numer = [jnp.zeros((rows, DV), f32) for _ in range(heads)]
    denom = [jnp.zeros((rows, 1), f32) for _ in range(heads)]
    queries = turned(read(slots[0], None, slice(0, 2 * qk)), heads, False)
    for slot in range(count):
        allowed = (row_ref[slot : slot + 1, :] <= own_pos) & (
            row_ref[count + slot : count + slot + 1, :] == own_doc
        )
        keys = read(slots[slot], None, slice(0, 2 * qk)).astype(bf16)
        for head in range(heads):
            near = 1.0 + dot_t(queries[head], keys)
            score = jnp.where(allowed, 0.5 * near * near + 0.5, 0.0)
            first = 2 * qk + head * DV
            value = read(slots[slot], None, slice(first, first + DV)).astype(bf16)
            numer[head] = numer[head] + dot_n(score.astype(bf16), value)
            denom[head] = denom[head] + jnp.sum(score, axis=1, keepdims=True)
    for head in range(heads):
        span = slice(head * DV, (head + 1) * DV)
        mean = numer[head] / denom[head]
        att_ref[:, span] = (valid * mean).astype(bf16)
        mean_ref[:, span] = mean
        inverse_ref[:, span] = jnp.broadcast_to(valid / denom[head], (rows, DV))


def query_kernel(heads, shape, col_ref, row_ref, numer_ref, denom_ref, *refs):
    slots, (out_ref,) = split_refs(refs, shape)
    count = len(slots)
    rows = col_ref.shape[0]
    qk = heads * FEAT
    own_pos, own_doc = col_ref[:, 0:1], col_ref[:, 1:2]
    queries = turned(read(slots[0], None, slice(0, 2 * qk)), heads, False)
    sums = [jnp.zeros((rows, 2 * qk), f32) for _ in range(heads)]
    for slot in range(count):
        allowed = (row_ref[slot : slot + 1, :] <= own_pos) & (
            row_ref[count + slot : count + slot + 1, :] == own_doc
        )
        keys = read(slots[slot], None, slice(0, 2 * qk)).astype(bf16)
        for head in range(heads):
            near = 1.0 + dot_t(queries[head], keys)
            first = 2 * qk + head * DV
            value = read(slots[slot], None, slice(first, first + DV)).astype(bf16)
            grad = dot_t(numer_ref[:, head * DV : (head + 1) * DV].astype(bf16), value)
            grad = grad + denom_ref[:, head * DV : head * DV + 1]
            grad = jnp.where(allowed, grad * near, 0.0).astype(bf16)
            sums[head] = sums[head] + dot_n(grad, keys)
    total = jnp.zeros((rows, 2 * qk), f32)
    for head in range(heads):
        total = jnp.where(head_lanes(rows, 2 * qk, qk + head * FEAT), 0.25 * sums[head], total)
    out_ref[...] = total[:, qk:].astype(bf16)


def key_kernel(heads, shape, grad_shape, col_ref, row_ref, *refs):
    slots, rest = split_refs(refs, shape)
    grads, (key_ref, value_ref) = split_refs(rest, grad_shape)
    count = len(slots)
    rows = col_ref.shape[0]
    qk, vw = heads * FEAT, heads * DV
    own_pos, own_doc = col_ref[:, 0:1], col_ref[:, 3:4]
    keys = turned(read(slots[0], None, slice(0, 2 * qk)), heads, True)
    values = [
        read(slots[0], None, slice(2 * qk + head * DV, 2 * qk + (head + 1) * DV)).astype(bf16)
        for head in range(heads)
    ]
    key_sums = [jnp.zeros((rows, 2 * qk), f32) for _ in range(heads)]
    value_sums = [jnp.zeros((rows, DV), f32) for _ in range(heads)]
    for slot in range(count):
        allowed = (row_ref[slot : slot + 1, :] >= own_pos) & (
            row_ref[2 * count + slot : 2 * count + slot + 1, :] == own_doc
        )
        queries = read(slots[slot], None, slice(0, 2 * qk)).astype(bf16)
        last = grads[slot][-1]
        extra = last.shape[0] - (rows - sum(ref.shape[0] for ref in grads[slot][:-1]))
        base = last.shape[0] - extra
        for head in range(heads):
            near = 1.0 + dot_t(keys[head], queries)
            span = slice(head * DV, (head + 1) * DV)
            numer = read(grads[slot], slice(0, rows), span).astype(bf16)
            line, lane = base + (head * rows) // vw, (head * rows) % vw
            grad = dot_t(values[head], numer) + last[line : line + 1, lane : lane + rows]
            grad = jnp.where(allowed, grad * near, 0.0).astype(bf16)
            key_sums[head] = key_sums[head] + dot_n(grad, queries)
            score = jnp.where(allowed, 0.5 * near * near + 0.5, 0.0).astype(bf16)
            value_sums[head] = value_sums[head] + dot_n(score, numer)
    total = jnp.zeros((rows, 2 * qk), f32)
    for head in range(heads):
        total = jnp.where(head_lanes(rows, 2 * qk, head * FEAT), 0.25 * key_sums[head], total)
        value_ref[:, head * DV : (head + 1) * DV] = value_sums[head].astype(bf16)
    key_ref[...] = total[:, :qk].astype(bf16)


def whole_call(body, outs, *operands, flops=0):
    moved = sum(x.size * x.dtype.itemsize for x in (*operands, *outs))
    return pl.pallas_call(
        body,
        out_shape=outs,
        in_specs=[pl.BlockSpec(memory_space=pltpu.VMEM)] * len(operands),
        out_specs=jax.tree.map(lambda _: pl.BlockSpec(memory_space=pltpu.VMEM), outs),
        compiler_params=pltpu.CompilerParams(vmem_limit_bytes=VMEM_LIMIT),
        cost_estimate=pl.CostEstimate(flops=flops, bytes_accessed=moved, transcendentals=0),
    )(*operands)


def join_kernel(shape, scale_ref, *refs):
    slots, (out_ref,) = split_refs(refs, shape)
    step = pl.program_id(0)
    for slot in range(len(slots)):

        @pl.when(step == slot)
        def _():
            at = 0
            for ref in slots[slot]:
                out_ref[at : at + ref.shape[0], :] = (ref[...] * scale_ref[...]).astype(bf16)
                at += ref.shape[0]


def join_rounded(slots, scale):
    parts = [part for slot in slots for part in slot]
    rows, width = sum(part.shape[0] for part in slots[0]), parts[0].shape[1]
    count = len(slots)
    return pl.pallas_call(
        functools.partial(join_kernel, tuple(len(slot) for slot in slots)),
        grid=(count,),
        out_shape=jax.ShapeDtypeStruct((count * rows, width), bf16),
        in_specs=[pl.BlockSpec((1, width), lambda i: (0, 0))]
        + [
            pl.BlockSpec(part.shape, lambda i: (0, 0), pipeline_mode=pl.Buffered(1))
            for part in parts
        ],
        out_specs=pl.BlockSpec((rows, width), lambda i: (i, 0)),
        compiler_params=pltpu.CompilerParams(vmem_limit_bytes=VMEM_LIMIT),
        cost_estimate=pl.CostEstimate(
            flops=0, bytes_accessed=6 * count * rows * width, transcendentals=0
        ),
    )(scale[None, :], *parts)


def norm_back(grad_out, values, inverse, gain):
    scaled = grad_out * gain
    return inverse * (
        scaled - values * inverse * inverse * jnp.mean(scaled * values, axis=-1, keepdims=True)
    )


def mm(left, right):
    return jnp.dot(left, right, preferred_element_type=f32)


def mm_t(left, right):
    return jnp.einsum("ac,bc->ab", left, right, preferred_element_type=f32)


def t_mm(left, right):
    return jnp.einsum("ca,cb->ab", left, right, preferred_element_type=f32)


def gated(gate, up_lin, hidden_grad):
    sigmoid = 0.5 + 0.5 * jnp.tanh(0.5 * gate)
    silu = gate * sigmoid
    return (
        (silu * up_lin).astype(bf16),
        (hidden_grad * up_lin * sigmoid * (1.0 + gate * (1.0 - sigmoid))).astype(bf16),
        (hidden_grad * silu).astype(bf16),
    )


def per_device(
    tokens,
    gain_attn,
    w_query,
    w_key,
    w_value,
    w_out,
    gain_mlp,
    w_gate,
    w_up,
    w_down,
    doc_lengths,
    cotangent,
):
    rows, width = tokens.shape
    heads = w_query.shape[1] // FEAT
    qk, vw = heads * FEAT, heads * DV
    blk_index, blk_count = lax.axis_index("blk"), lax.axis_size("blk")

    ends = [doc_lengths[0]]
    for doc in range(1, doc_lengths.shape[0]):
        ends.append(ends[-1] + doc_lengths[doc])

    def layout(positions):
        docs = sum((positions >= end).astype(jnp.int32) for end in ends[:-1])
        valid = positions < ends[-1]
        return docs, valid, jnp.where(valid, docs, -1)

    own_pos = blk_index * rows + jnp.arange(rows, dtype=jnp.int32)
    own_docs, own_valid, own_key_docs = layout(own_pos)
    columns = jnp.stack([own_pos, own_docs, own_valid.astype(jnp.int32), own_key_docs], axis=1)
    slot_blocks = blk_index ^ jnp.arange(blk_count, dtype=jnp.int32)
    slot_pos = slot_blocks[:, None] * rows + jnp.arange(rows, dtype=jnp.int32)[None, :]
    slot_docs, _, slot_key_docs = layout(slot_pos)
    lines = jnp.concatenate([slot_pos, slot_key_docs, slot_docs])

    gain_one, gain_two = gain_attn.astype(f32), gain_mlp.astype(f32)
    token_wide, cot_wide = tokens.astype(f32), cotangent.astype(f32)
    inv_in = lax.rsqrt(jnp.mean(token_wide * token_wide, axis=-1, keepdims=True) + epsilon)
    normed_in = (token_wide * inv_in * gain_one).astype(bf16)
    qkv_own = jnp.concatenate(
        [mm(normed_in, w_query), mm(normed_in, w_key), mm(normed_in, w_value)], axis=1
    )
    convoy = Convoy()
    qkv_slots = {}
    convoy.finish(Chain(gather_steps(qkv_own, qkv_slots)))
    qkv = [qkv_slots[slot] for slot in range(blk_count)]
    shape = tuple(len(slot) for slot in qkv)
    qkv_parts = [part for slot in qkv for part in slot]

    cost = 8 * rows * rows * blk_count * vw
    attended, mean, inverse = whole_call(
        functools.partial(attend_kernel, heads, shape),
        (
            jax.ShapeDtypeStruct((rows, vw), bf16),
            jax.ShapeDtypeStruct((rows, vw), f32),
            jax.ShapeDtypeStruct((rows, vw), f32),
        ),
        columns,
        lines,
        *qkv_parts,
        flops=cost,
    )
    attn_part = mm(attended, w_out)
    attn_sum = sum_head(attn_part)
    order = [0, 1, 2, 4, 3, 5, 6, 7] if blk_count == 8 else list(range(blk_count))
    early, late = order[: blk_count // 2], order[blk_count // 2 :]
    ones = jnp.ones_like(gain_two)

    def ready(chain, slots, wanted):
        while not all(slot in slots for slot in wanted):
            convoy.wave([chain])
        return [slots[slot] for slot in wanted]

    def cot_work(*slots):
        rows_of = join_rounded(slots, ones)
        return rows_of, mm_t(rows_of, w_down)

    def gate_work(*slots):
        rows_of = join_rounded(slots, gain_two)
        return rows_of, mm(rows_of, w_gate)

    def up_work(rows_of, gate, hidden_grad):
        return gated(gate, mm(rows_of, w_up), hidden_grad)

    cot_slots = {}
    cot = Chain(gather_steps(cot_wide, cot_slots))
    own_hidden_grad = convoy.wave(
        [cot], lambda left, _: mm_t(left, w_down), cotangent, attn_part
    )
    cot_early = ready(cot, cot_slots, early)
    convoy.launch(cot)
    cot_a, hidden_grad_a = convoy.work(cot_work, *cot_early)
    resid_mid = after(token_wide, convoy.done) + attn_sum
    inv_mid = lax.rsqrt(jnp.mean(resid_mid * resid_mid, axis=-1, keepdims=True) + epsilon)
    scaled_mid = resid_mid * inv_mid
    convoy.done = scaled_mid
    convoy.land(cot)
    mid_slots = {}
    mid = Chain(gather_steps(scaled_mid, mid_slots))

    def middle(scaled_mid):
        normed_mid = (scaled_mid * gain_two).astype(bf16)
        hidden, gate_lin_grad, up_lin_grad = gated(
            mm(normed_mid, w_gate), mm(normed_mid, w_up), own_hidden_grad
        )
        return hidden, mm_t(gate_lin_grad, w_gate) + mm_t(up_lin_grad, w_up)

    convoy.launch(mid, cot)
    hidden, mid_part = convoy.work(middle, scaled_mid)
    convoy.land(cot)
    mid_sum = sum_head(mid_part)

    def share_work(hidden, *slots):
        mlp_part = mm(hidden, w_down)
        return mlp_part, *cot_work(*after(slots, mlp_part))

    mlp_part, cot_b, hidden_grad_b = convoy.work(
        share_work, hidden, *ready(cot, cot_slots, late)
    )
    mlp = Chain(line_steps(mlp_part, 2))
    convoy.land(mid)
    mid_early = ready(mid, mid_slots, early)
    convoy.launch(mid)
    mid_a, gate_a = convoy.work(gate_work, *mid_early)
    hidden_a, gate_grad_a, up_grad_a = convoy.work(
        up_work, after(mid_a, convoy.done), gate_a, hidden_grad_a
    )
    down_a = convoy.work(t_mm, after(hidden_a, convoy.done), cot_a)
    mid_grad = after(mid_sum, down_a)

    resid_grad = cot_wide + norm_back(mid_grad, resid_mid, inv_mid, gain_two)
    out_lin_grad = resid_grad.astype(bf16)
    attended_grad = mm_t(out_lin_grad, w_out)
    numer_grad = attended_grad * inverse
    denom_grad = -jnp.sum((numer_grad * mean).reshape(rows, heads, DV), axis=-1)
    denom_lines = denom_grad.T.reshape(rows // DV, vw)
    denom_lines = jnp.pad(denom_lines, ((0, -denom_lines.shape[0] % 8), (0, 0)))
    sent = jnp.concatenate([numer_grad, denom_lines])
    convoy.done = sent
    convoy.land(mid)
    grad_slots = {}
    grads = Chain(gather_steps(sent, grad_slots))

    def query_work(numer_grad, denom_grad, out_lin_grad):
        (query_lin_grad,) = whole_call(
            functools.partial(query_kernel, heads, shape),
            (jax.ShapeDtypeStruct((rows, qk), bf16),),
            columns,
            lines,
            numer_grad,
            jnp.repeat(denom_grad, DV, axis=1),
            *qkv_parts,
            flops=cost,
        )
        return query_lin_grad, t_mm(attended, after(out_lin_grad, query_lin_grad))

    convoy.launch(grads, mlp)
    query_lin_grad, out_part = convoy.work(query_work, numer_grad, denom_grad, out_lin_grad)
    convoy.land(grads)
    gate_part = convoy.wave([grads], t_mm, mid_a, gate_grad_a)
    convoy.launch(grads)
    convoy.land(grads, mlp)
    convoy.finish(grads)
    grad_slots = [grad_slots[slot] for slot in range(blk_count)]
    grad_shape = tuple(len(slot) for slot in grad_slots)

    def key_work(query_lin_grad, grad_parts):
        key_lin_grad, value_grad = whole_call(
            functools.partial(key_kernel, heads, shape, grad_shape),
            (jax.ShapeDtypeStruct((rows, qk), bf16), jax.ShapeDtypeStruct((rows, vw), bf16)),
            columns,
            lines,
            *qkv_parts,
            *grad_parts,
            flops=2 * cost,
        )
        lin_grads = (query_lin_grad, key_lin_grad, value_grad)
        parts = [t_mm(normed_in, grad) for grad in lin_grads]
        parts[2] = with_layout_constraint(parts[2], Layout(major_to_minor=(0, 1)))
        query_lin_grad, key_lin_grad, value_grad = after(lin_grads, parts)
        in_part = mm_t(query_lin_grad, w_query) + mm_t(key_lin_grad, w_key)
        return in_part + mm_t(value_grad, w_value), parts

    grad_parts = [part for slot in grad_slots for part in slot]
    convoy.launch(mid, mlp)
    in_part, parts = convoy.work(key_work, query_lin_grad, grad_parts)
    *qkv_w_grads, out_w_grad = lax.psum((*parts, out_part), "blk")
    convoy.land(mid)
    mid_late = ready(mid, mid_slots, late)

    in_sum = Chain(line_steps(in_part, 2))
    convoy.launch(in_sum)

    gain_parts = jnp.stack(
        [
            jnp.sum(after(in_part, convoy.sent) * token_wide * inv_in, axis=0),
            jnp.sum(mid_part * scaled_mid, axis=0),
        ]
    )
    convoy.done = gain_parts
    convoy.land(mlp)
    gains = Chain(small_steps(gain_parts))
    convoy.launch(mlp, gains)
    chains = [in_sum, gains, mlp]
    mid_b, gate_b = convoy.work(gate_work, *mid_late)
    convoy.land(*chains)

    def second_work(mid_b, gate_b, hidden_grad_b):
        parts = up_work(mid_b, gate_b, hidden_grad_b)
        return (*parts, t_mm(mid_a, after(up_grad_a, parts)))

    hidden_b, gate_grad_b, up_grad_b, up_part = convoy.wave(
        chains, second_work, mid_b, gate_b, hidden_grad_b
    )
    down_w_grad = convoy.wave(chains, lambda x, y: down_a + t_mm(x, y), hidden_b, cot_b)
    convoy.finish(mlp)

    def gate_last(gate_grad_b, mlp_sum):
        output = (resid_mid + mlp_sum).astype(bf16)
        return gate_part + t_mm(mid_b, after(gate_grad_b, output)), output

    chains = [in_sum, gains]
    convoy.launch(*chains)
    gate_w_grad, output = convoy.work(gate_last, gate_grad_b, mlp.result)
    up_w_grad = convoy.work(
        lambda x: up_part + t_mm(mid_b, x), after(up_grad_b, gate_w_grad)
    )
    convoy.land(*chains)
    while any(chain.due for chain in chains):
        convoy.wave(chains)
    in_grad, gain_grads = (chain.result for chain in chains)
    gain_grads = after(gain_grads, qkv_w_grads, out_w_grad)
    input_grad = resid_grad + norm_back(in_grad, token_wide, inv_in, gain_one)
    return (
        output,
        input_grad,
        gain_grads[0],
        *qkv_w_grads,
        out_w_grad,
        gain_grads[1],
        gate_w_grad,
        up_w_grad,
        down_w_grad,
    )


def solution(mesh):
    in_specs = (
        P("blk", None),
        P(),
        P(None, "head"),
        P(None, "head"),
        P(None, "head"),
        P("head", None),
        P(),
        P(None, "head"),
        P(None, "head"),
        P("head", None),
        P(),
        P("blk", None),
    )
    out_specs = (
        P("blk", None),
        P("blk", None),
        P(),
        P(None, "head"),
        P(None, "head"),
        P(None, "head"),
        P("head", None),
        P(),
        P(None, "head"),
        P(None, "head"),
        P("head", None),
    )
    return jax.shard_map(
        per_device, mesh=mesh, in_specs=in_specs, out_specs=out_specs, check_vma=False
    )
```

```python
import functools

import jax
import jax.numpy as jnp
from jax import lax
from jax.experimental import pallas as pl
from jax.experimental.pallas import tpu as pltpu
from jax.sharding import PartitionSpec as P

FEAT = 16
DV = 128

epsilon = 1e-05
f32, bf16 = jnp.float32, jnp.bfloat16
VMEM_LIMIT = 56 * 1024 * 1024


def hop(value, axis, way):
    if isinstance(way, int):
        way = [(i, i ^ way) for i in range(lax.axis_size(axis))]
    return lax.ppermute(value, axis, way)


def after(value, *others):
    return lax.optimization_barrier((value, others))[0]


class Chain:
    def __init__(self, steps):
        self.steps, self.result, self.flying = steps, None, None
        self.advance(None)

    def advance(self, values):
        try:
            self.due = self.steps.send(values)
        except StopIteration as end:
            self.due, self.result = [], end.value


class Convoy:
    def __init__(self):
        self.landed, self.sent, self.done = (), (), ()

    def launch(self, *chains):
        for chain in chains:
            if chain.due:
                values = after([value for value, _, _ in chain.due], self.landed, self.sent)
                chain.flying = [
                    hop(value, axis, way) for value, (_, axis, way) in zip(values, chain.due)
                ]
                self.sent = (self.sent, values)

    def work(self, work, *operands):
        self.done = work(*after(operands, self.sent, self.landed))
        return self.done

    def land(self, *chains):
        chains = [chain for chain in chains if chain.flying is not None]
        came = after([chain.flying for chain in chains], self.done)
        self.landed, self.sent = (came, self.done), ()
        for chain, values in zip(chains, came):
            chain.flying = None
            chain.advance(values)

    def wave(self, chains, work=None, *operands):
        self.launch(*chains)
        result = None if work is None else self.work(work, *operands)
        self.land(*chains)
        return result

    def finish(self, chain):
        while chain.due:
            self.wave([chain])


def gather_steps(value, slots):
    count = lax.axis_size("blk")
    slots[0] = [value]
    if count != 8:
        bit = 1
        while bit < count:
            got = yield [(slots[slot][0], "blk", bit) for slot in range(bit)]
            slots.update({bit + slot: [part] for slot, part in enumerate(got)})
            bit *= 2
        return
    half = value.shape[0] // 16 * 8
    x_all, y_all, own_pair = yield [(value, "blk", way) for way in (2, 4, 1)]
    slots[1], slots[2], slots[4] = [own_pair], [x_all], [y_all]
    *slots[6], x_pair, y_pair = yield [
        (x_all[:half], "blk", 4),
        (y_all[half:], "blk", 2),
        (x_all, "blk", 1),
        (y_all, "blk", 1),
    ]
    slots[3], slots[5] = [x_pair], [y_pair]
    slots[7] = yield [(part, "blk", 1) for part in slots[6]]


def small_steps(value):
    for axis in ("head", "blk"):
        bit = 1
        while bit < lax.axis_size(axis):
            ways = [bit]
            if axis == "blk" and bit == 2 and lax.axis_size(axis) == 8:
                ways = [2, 4, 6]
            for got in (yield [(value, axis, way) for way in ways]):
                value = value + got
            bit *= 2 * len(ways)
    return value


def head_share(value, step=0):
    rows = value.shape[0] // lax.axis_size("head")
    return lax.dynamic_slice_in_dim(value, (lax.axis_index("head") ^ step) * rows, rows)


def head_steps(value, finish=None):
    count, mine = lax.axis_size("head"), lax.axis_index("head")
    got = yield [(head_share(value, step), "head", step) for step in range(1, count)]
    total = head_share(value)
    for part in got:
        total = total + part
    total = total if finish is None else finish(total)
    got = yield [(total, "head", step) for step in range(1, count)]
    whole = jnp.zeros_like(value)
    for step, part in enumerate([total, *got]):
        whole = lax.dynamic_update_slice_in_dim(whole, part, (mine ^ step) * part.shape[0], 0)
    return whole


def line_steps(value, pieces):
    if lax.axis_size("head") != 4:
        return (yield from head_steps(value))
    mine = lax.axis_index("head")
    inner = (mine == 1) | (mine == 2)
    parts = jnp.split(value, pieces)
    pairs, whole, done = {}, {}, {}
    for wave in range(pieces + 2):
        sends, takes = [], []
        if wave < pieces:
            sends.append((parts[wave], "head", [(0, 1), (3, 2)]))
            takes.append((pairs, wave, parts))
        if 0 <= wave - 1 < pieces:
            sends.append((pairs[wave - 1], "head", [(1, 2), (2, 1)]))
            takes.append((whole, wave - 1, pairs))
        if 0 <= wave - 2:
            sends.append((whole[wave - 2], "head", [(1, 0), (2, 3)]))
            takes.append((done, wave - 2, whole))
        got = yield sends
        for part, (into, piece, own) in zip(got, takes):
            if into is done:
                into[piece] = jnp.where(inner, own[piece], part)
            else:
                into[piece] = own[piece] + part
    return jnp.concatenate([done[piece] for piece in range(pieces)])


def sum_head(value):
    return lax.psum(value, "head")


def dot_t(left, right):
    return lax.dot_general(left, right, (((1,), (1,)), ((), ())), preferred_element_type=f32)


def dot_n(left, right):
    return lax.dot_general(left, right, (((1,), (0,)), ((), ())), preferred_element_type=f32)


def head_lanes(rows, width, first):
    lanes = lax.broadcasted_iota(jnp.int32, (rows, width), 1)
    return (lanes >= first) & (lanes < first + FEAT)


def read(slot, lines, lanes):
    parts = [ref[:, lanes] for ref in slot]
    whole = parts[0] if len(parts) == 1 else jnp.concatenate(parts)
    return whole if lines is None else whole[lines]


def split_refs(refs, shape):
    slots, at = [], 0
    for pieces in shape:
        slots.append(refs[at : at + pieces])
        at += pieces
    return slots, refs[at:]


def turned(tile, heads, use_key):
    rows, width = tile.shape
    moved = jnp.concatenate([tile[:, width // 2 :], tile[:, : width // 2]], axis=1)
    base = 0 if use_key else width // 2
    scaled = moved * 0.25
    return [
        jnp.where(head_lanes(rows, width, base + head * FEAT), scaled, 0.0).astype(bf16)
        for head in range(heads)
    ]


def attend_kernel(heads, shape, col_ref, row_ref, *refs):
    slots, (att_ref, mean_ref, inverse_ref) = split_refs(refs, shape)
    count = len(slots)
    rows = col_ref.shape[0]
    qk = heads * FEAT
    own_pos, own_doc = col_ref[:, 0:1], col_ref[:, 1:2]
    valid = col_ref[:, 2:3].astype(f32)
    numer = [jnp.zeros((rows, DV), f32) for _ in range(heads)]
    denom = [jnp.zeros((rows, 1), f32) for _ in range(heads)]
    queries = turned(read(slots[0], None, slice(0, 2 * qk)), heads, False)
    for slot in range(count):
        allowed = (row_ref[slot : slot + 1, :] <= own_pos) & (
            row_ref[count + slot : count + slot + 1, :] == own_doc
        )
        keys = read(slots[slot], None, slice(0, 2 * qk)).astype(bf16)
        for head in range(heads):
            near = 1.0 + dot_t(queries[head], keys)
            score = jnp.where(allowed, 0.5 * near * near + 0.5, 0.0)
            first = 2 * qk + head * DV
            value = read(slots[slot], None, slice(first, first + DV)).astype(bf16)
            numer[head] = numer[head] + dot_n(score.astype(bf16), value)
            denom[head] = denom[head] + jnp.sum(score, axis=1, keepdims=True)
    for head in range(heads):
        span = slice(head * DV, (head + 1) * DV)
        mean = numer[head] / denom[head]
        att_ref[:, span] = (valid * mean).astype(bf16)
        mean_ref[:, span] = mean
        inverse_ref[:, span] = jnp.broadcast_to(valid / denom[head], (rows, DV))


def query_kernel(heads, shape, col_ref, row_ref, numer_ref, denom_ref, *refs):
    slots, (out_ref,) = split_refs(refs, shape)
    count = len(slots)
    rows = col_ref.shape[0]
    qk = heads * FEAT
    own_pos, own_doc = col_ref[:, 0:1], col_ref[:, 1:2]
    queries = turned(read(slots[0], None, slice(0, 2 * qk)), heads, False)
    sums = [jnp.zeros((rows, 2 * qk), f32) for _ in range(heads)]
    for slot in range(count):
        allowed = (row_ref[slot : slot + 1, :] <= own_pos) & (
            row_ref[count + slot : count + slot + 1, :] == own_doc
        )
        keys = read(slots[slot], None, slice(0, 2 * qk)).astype(bf16)
        for head in range(heads):
            near = 1.0 + dot_t(queries[head], keys)
            first = 2 * qk + head * DV
            value = read(slots[slot], None, slice(first, first + DV)).astype(bf16)
            grad = dot_t(numer_ref[:, head * DV : (head + 1) * DV].astype(bf16), value)
            grad = grad + denom_ref[:, head : head + 1]
            grad = jnp.where(allowed, grad * near, 0.0).astype(bf16)
            sums[head] = sums[head] + dot_n(grad, keys)
    total = jnp.zeros((rows, 2 * qk), f32)
    for head in range(heads):
        total = jnp.where(head_lanes(rows, 2 * qk, qk + head * FEAT), 0.25 * sums[head], total)
    out_ref[...] = total[:, qk:].astype(bf16)


def key_kernel(heads, shape, grad_shape, col_ref, row_ref, *refs):
    slots, rest = split_refs(refs, shape)
    grads, (key_ref, value_ref) = split_refs(rest, grad_shape)
    count = len(slots)
    rows = col_ref.shape[0]
    qk, vw = heads * FEAT, heads * DV
    own_pos, own_doc = col_ref[:, 0:1], col_ref[:, 3:4]
    keys = turned(read(slots[0], None, slice(0, 2 * qk)), heads, True)
    values = [
        read(slots[0], None, slice(2 * qk + head * DV, 2 * qk + (head + 1) * DV)).astype(bf16)
        for head in range(heads)
    ]
    key_sums = [jnp.zeros((rows, 2 * qk), f32) for _ in range(heads)]
    value_sums = [jnp.zeros((rows, DV), f32) for _ in range(heads)]
    for slot in range(count):
        allowed = (row_ref[slot : slot + 1, :] >= own_pos) & (
            row_ref[2 * count + slot : 2 * count + slot + 1, :] == own_doc
        )
        queries = read(slots[slot], None, slice(0, 2 * qk)).astype(bf16)
        last = grads[slot][-1]
        extra = last.shape[0] - (rows - sum(ref.shape[0] for ref in grads[slot][:-1]))
        base = last.shape[0] - extra
        for head in range(heads):
            near = 1.0 + dot_t(keys[head], queries)
            span = slice(head * DV, (head + 1) * DV)
            numer = read(grads[slot], slice(0, rows), span).astype(bf16)
            line, lane = base + (head * rows) // vw, (head * rows) % vw
            grad = dot_t(values[head], numer) + last[line : line + 1, lane : lane + rows]
            grad = jnp.where(allowed, grad * near, 0.0).astype(bf16)
            key_sums[head] = key_sums[head] + dot_n(grad, queries)
            score = jnp.where(allowed, 0.5 * near * near + 0.5, 0.0).astype(bf16)
            value_sums[head] = value_sums[head] + dot_n(score, numer)
    total = jnp.zeros((rows, 2 * qk), f32)
    for head in range(heads):
        total = jnp.where(head_lanes(rows, 2 * qk, head * FEAT), 0.25 * key_sums[head], total)
        value_ref[:, head * DV : (head + 1) * DV] = value_sums[head].astype(bf16)
    key_ref[...] = total[:, :qk].astype(bf16)


def whole_call(body, outs, *operands, flops=0):
    moved = sum(x.size * x.dtype.itemsize for x in (*operands, *outs))
    return pl.pallas_call(
        body,
        out_shape=outs,
        in_specs=[pl.BlockSpec(memory_space=pltpu.VMEM)] * len(operands),
        out_specs=jax.tree.map(lambda _: pl.BlockSpec(memory_space=pltpu.VMEM), outs),
        compiler_params=pltpu.CompilerParams(vmem_limit_bytes=VMEM_LIMIT),
        cost_estimate=pl.CostEstimate(flops=flops, bytes_accessed=moved, transcendentals=0),
    )(*operands)


def join_kernel(shape, scale_ref, *refs):
    slots, (out_ref,) = split_refs(refs, shape)
    step = pl.program_id(0)
    for slot in range(len(slots)):

        @pl.when(step == slot)
        def _():
            at = 0
            for ref in slots[slot]:
                out_ref[at : at + ref.shape[0], :] = (ref[...] * scale_ref[...]).astype(bf16)
                at += ref.shape[0]


def join_rounded(slots, scale):
    parts = [part for slot in slots for part in slot]
    rows, width = sum(part.shape[0] for part in slots[0]), parts[0].shape[1]
    count = len(slots)
    return pl.pallas_call(
        functools.partial(join_kernel, tuple(len(slot) for slot in slots)),
        grid=(count,),
        out_shape=jax.ShapeDtypeStruct((count * rows, width), bf16),
        in_specs=[pl.BlockSpec((1, width), lambda i: (0, 0))]
        + [
            pl.BlockSpec(part.shape, lambda i: (0, 0), pipeline_mode=pl.Buffered(1))
            for part in parts
        ],
        out_specs=pl.BlockSpec((rows, width), lambda i: (i, 0)),
        compiler_params=pltpu.CompilerParams(vmem_limit_bytes=VMEM_LIMIT),
        cost_estimate=pl.CostEstimate(
            flops=0, bytes_accessed=6 * count * rows * width, transcendentals=0
        ),
    )(scale[None, :], *parts)


def norm_back(grad_out, values, inverse, gain):
    scaled = grad_out * gain
    return inverse * (
        scaled - values * inverse * inverse * jnp.mean(scaled * values, axis=-1, keepdims=True)
    )


def mm(left, right):
    return jnp.dot(left, right, preferred_element_type=f32)


def mm_t(left, right):
    return jnp.einsum("ac,bc->ab", left, right, preferred_element_type=f32)


def t_mm(left, right):
    return jnp.einsum("ca,cb->ab", left, right, preferred_element_type=f32)


def gated(gate, up_lin, hidden_grad):
    sigmoid = 0.5 + 0.5 * jnp.tanh(0.5 * gate)
    silu = gate * sigmoid
    return (
        (silu * up_lin).astype(bf16),
        (hidden_grad * up_lin * sigmoid * (1.0 + gate * (1.0 - sigmoid))).astype(bf16),
        (hidden_grad * silu).astype(bf16),
    )


def per_device(
    tokens,
    gain_attn,
    w_query,
    w_key,
    w_value,
    w_out,
    gain_mlp,
    w_gate,
    w_up,
    w_down,
    doc_lengths,
    cotangent,
):
    rows, width = tokens.shape
    heads = w_query.shape[1] // FEAT
    qk, vw = heads * FEAT, heads * DV
    blk_index, blk_count = lax.axis_index("blk"), lax.axis_size("blk")

    def layout(doc_lengths, cotangent):
        ends = [doc_lengths[0]]
        for doc in range(1, doc_lengths.shape[0]):
            ends.append(ends[-1] + doc_lengths[doc])

        def documents(positions):
            docs = sum((positions >= end).astype(jnp.int32) for end in ends[:-1])
            valid = positions < ends[-1]
            return docs, valid, jnp.where(valid, docs, -1)

        own_pos = blk_index * rows + jnp.arange(rows, dtype=jnp.int32)
        own_docs, own_valid, own_key_docs = documents(own_pos)
        columns = [own_pos, own_docs, own_valid.astype(jnp.int32), own_key_docs]
        slot_blocks = blk_index ^ jnp.arange(blk_count, dtype=jnp.int32)
        slot_pos = slot_blocks[:, None] * rows + jnp.arange(rows, dtype=jnp.int32)[None, :]
        slot_docs, _, slot_key_docs = documents(slot_pos)
        lines = jnp.concatenate([slot_pos, slot_key_docs, slot_docs])
        return jnp.stack(columns, axis=1), lines, cotangent.astype(f32)

    gain_one, gain_two = gain_attn.astype(f32), gain_mlp.astype(f32)
    token_wide = tokens.astype(f32)
    inv_in = lax.rsqrt(jnp.mean(token_wide * token_wide, axis=-1, keepdims=True) + epsilon)
    normed_in = (token_wide * inv_in * gain_one).astype(bf16)
    qkv_own = jnp.concatenate(
        [mm(normed_in, w_query), mm(normed_in, w_key), mm(normed_in, w_value)], axis=1
    )
    convoy = Convoy()
    qkv_slots = {}
    qkv_chain = Chain(gather_steps(qkv_own, qkv_slots))
    columns, lines, cot_wide = convoy.wave([qkv_chain], layout, doc_lengths, cotangent)
    convoy.finish(qkv_chain)
    qkv = [qkv_slots[slot] for slot in range(blk_count)]
    shape = tuple(len(slot) for slot in qkv)
    qkv_parts = [part for slot in qkv for part in slot]

    cost = 8 * rows * rows * blk_count * vw
    attended, mean, inverse = whole_call(
        functools.partial(attend_kernel, heads, shape),
        (
            jax.ShapeDtypeStruct((rows, vw), bf16),
            jax.ShapeDtypeStruct((rows, vw), f32),
            jax.ShapeDtypeStruct((rows, vw), f32),
        ),
        columns,
        lines,
        *qkv_parts,
        flops=cost,
    )
    attn_part = mm(attended, w_out)
    attn_sum = sum_head(attn_part)
    order = [0, 1, 2, 4, 3, 5, 6, 7] if blk_count == 8 else list(range(blk_count))
    early, late = order[: blk_count // 2], order[blk_count // 2 :]
    ones = jnp.ones_like(gain_two)

    def ready(chain, slots, wanted):
        while not all(slot in slots for slot in wanted):
            convoy.wave([chain])
        return [slots[slot] for slot in wanted]

    def cot_work(*slots):
        rows_of = join_rounded(slots, ones)
        return rows_of, mm_t(rows_of, w_down)

    def gate_work(*slots):
        rows_of = join_rounded(slots, gain_two)
        return rows_of, mm(rows_of, w_gate)

    def up_work(rows_of, gate, hidden_grad):
        return gated(gate, mm(rows_of, w_up), hidden_grad)

    cot_slots = {}
    cot = Chain(gather_steps(cot_wide, cot_slots))
    own_hidden_grad = convoy.wave(
        [cot], lambda left, _: mm_t(left, w_down), cotangent, attn_part
    )
    cot_early = ready(cot, cot_slots, early)
    convoy.launch(cot)
    cot_a, hidden_grad_a = convoy.work(cot_work, *cot_early)
    resid_mid = after(token_wide, convoy.done) + attn_sum
    inv_mid = lax.rsqrt(jnp.mean(resid_mid * resid_mid, axis=-1, keepdims=True) + epsilon)
    scaled_mid = resid_mid * inv_mid
    convoy.done = scaled_mid
    convoy.land(cot)
    mid_slots = {}
    mid = Chain(gather_steps(scaled_mid, mid_slots))

    def middle(scaled_mid):
        normed_mid = (scaled_mid * gain_two).astype(bf16)
        hidden, gate_lin_grad, up_lin_grad = gated(
            mm(normed_mid, w_gate), mm(normed_mid, w_up), own_hidden_grad
        )
        return hidden, mm_t(gate_lin_grad, w_gate) + mm_t(up_lin_grad, w_up)

    convoy.launch(mid, cot)
    hidden, mid_part = convoy.work(middle, scaled_mid)
    convoy.land(cot)
    mid_sum = sum_head(mid_part)

    def share_work(hidden, *slots):
        mlp_part = mm(hidden, w_down)
        return mlp_part, *cot_work(*after(slots, mlp_part))

    mlp_part, cot_b, hidden_grad_b = convoy.work(
        share_work, hidden, *ready(cot, cot_slots, late)
    )
    mlp = Chain(line_steps(mlp_part, 2))
    convoy.land(mid)
    mid_early = ready(mid, mid_slots, early)
    convoy.launch(mid)
    mid_a, gate_a = convoy.work(gate_work, *mid_early)
    hidden_a, gate_grad_a, up_grad_a = convoy.work(
        up_work, after(mid_a, convoy.done), gate_a, hidden_grad_a
    )
    down_a = convoy.work(t_mm, after(hidden_a, convoy.done), cot_a)
    mid_grad = after(mid_sum, down_a)

    resid_grad = cot_wide + norm_back(mid_grad, resid_mid, inv_mid, gain_two)
    out_lin_grad = resid_grad.astype(bf16)
    attended_grad = mm_t(out_lin_grad, w_out)
    numer_grad = attended_grad * inverse
    denom_grad = -jnp.sum((numer_grad * mean).reshape(rows, heads, DV), axis=-1)
    denom_lines = denom_grad.T.reshape(rows // DV, vw)
    denom_lines = jnp.pad(denom_lines, ((0, -denom_lines.shape[0] % 8), (0, 0)))
    sent = jnp.concatenate([numer_grad, denom_lines])
    convoy.done = sent
    convoy.land(mid)
    grad_slots = {}
    grads = Chain(gather_steps(sent, grad_slots))

    def query_work(numer_grad, denom_grad):
        (query_lin_grad,) = whole_call(
            functools.partial(query_kernel, heads, shape),
            (jax.ShapeDtypeStruct((rows, qk), bf16),),
            columns,
            lines,
            numer_grad,
            denom_grad,
            *qkv_parts,
            flops=cost,
        )
        return query_lin_grad

    convoy.launch(grads, mlp)
    query_lin_grad = convoy.work(query_work, numer_grad, denom_grad)
    convoy.land(grads)
    out_part = convoy.wave([grads], t_mm, attended, out_lin_grad)
    convoy.launch(grads)
    convoy.land(grads, mlp)
    convoy.finish(grads)
    grad_slots = [grad_slots[slot] for slot in range(blk_count)]
    grad_shape = tuple(len(slot) for slot in grad_slots)

    def key_work(query_lin_grad, grad_parts):
        key_lin_grad, value_grad = whole_call(
            functools.partial(key_kernel, heads, shape, grad_shape),
            (jax.ShapeDtypeStruct((rows, qk), bf16), jax.ShapeDtypeStruct((rows, vw), bf16)),
            columns,
            lines,
            *qkv_parts,
            *grad_parts,
            flops=2 * cost,
        )
        lin_grads = (query_lin_grad, key_lin_grad, value_grad)
        parts = [t_mm(normed_in, grad) for grad in lin_grads]
        query_lin_grad, key_lin_grad, value_grad = after(lin_grads, parts)
        in_part = mm_t(query_lin_grad, w_query) + mm_t(key_lin_grad, w_key)
        return in_part + mm_t(value_grad, w_value), parts

    grad_parts = [part for slot in grad_slots for part in slot]
    convoy.launch(mid, mlp)
    in_part, parts = convoy.work(key_work, query_lin_grad, grad_parts)
    *qkv_w_grads, out_w_grad = lax.psum((*parts, out_part), "blk")
    convoy.land(mid)
    mid_late = ready(mid, mid_slots, late)

    in_sum = Chain(line_steps(in_part, 2))
    convoy.launch(in_sum)

    gain_parts = jnp.stack(
        [
            jnp.sum(after(in_part, convoy.sent) * token_wide * inv_in, axis=0),
            jnp.sum(mid_part * scaled_mid, axis=0),
        ]
    )
    convoy.done = gain_parts
    convoy.land(mlp)
    gains = Chain(small_steps(gain_parts))
    convoy.launch(mlp, gains)
    chains = [in_sum, gains, mlp]
    mid_b, gate_b = convoy.work(gate_work, *mid_late)
    convoy.land(*chains)

    def second_work(mid_b, gate_b, hidden_grad_b):
        parts = up_work(mid_b, gate_b, hidden_grad_b)
        return (*parts, t_mm(mid_a, after(up_grad_a, parts)))

    hidden_b, gate_grad_b, up_grad_b, up_part = convoy.wave(
        chains, second_work, mid_b, gate_b, hidden_grad_b
    )

    def third_work(hidden_b, gate_grad_a):
        down_w_grad = down_a + t_mm(hidden_b, cot_b)
        return down_w_grad, t_mm(mid_a, after(gate_grad_a, down_w_grad))

    down_w_grad, gate_part = convoy.wave(chains, third_work, hidden_b, gate_grad_a)
    convoy.finish(mlp)

    def gate_last(gate_grad_b, mlp_sum):
        output = (resid_mid + mlp_sum).astype(bf16)
        return gate_part + t_mm(mid_b, after(gate_grad_b, output)), output

    chains = [in_sum, gains]
    convoy.launch(*chains)
    gate_w_grad, output = convoy.work(gate_last, gate_grad_b, mlp.result)
    up_w_grad = convoy.work(
        lambda x: up_part + t_mm(mid_b, x), after(up_grad_b, gate_w_grad)
    )
    convoy.land(*chains)
    while any(chain.due for chain in chains):
        convoy.wave(chains)
    in_grad, gain_grads = (chain.result for chain in chains)
    gain_grads = after(gain_grads, qkv_w_grads, out_w_grad)
    input_grad = resid_grad + norm_back(in_grad, token_wide, inv_in, gain_one)
    return (
        output,
        input_grad,
        gain_grads[0],
        *qkv_w_grads,
        out_w_grad,
        gain_grads[1],
        gate_w_grad,
        up_w_grad,
        down_w_grad,
    )


def solution(mesh):
    in_specs = (
        P("blk", None),
        P(),
        P(None, "head"),
        P(None, "head"),
        P(None, "head"),
        P("head", None),
        P(),
        P(None, "head"),
        P(None, "head"),
        P("head", None),
        P(),
        P("blk", None),
    )
    out_specs = (
        P("blk", None),
        P("blk", None),
        P(),
        P(None, "head"),
        P(None, "head"),
        P(None, "head"),
        P("head", None),
        P(),
        P(None, "head"),
        P(None, "head"),
        P("head", None),
    )
    return jax.shard_map(
        per_device, mesh=mesh, in_specs=in_specs, out_specs=out_specs, check_vma=False
    )
```

```python
import functools

import jax
import jax.numpy as jnp
from jax import lax
from jax.experimental import pallas as pl
from jax.experimental.pallas import tpu as pltpu
from jax.sharding import PartitionSpec as P

FEAT = 16
DV = 128

epsilon = 1e-05
f32, bf16 = jnp.float32, jnp.bfloat16
VMEM_LIMIT = 56 * 1024 * 1024


def hop(value, axis, way):
    if isinstance(way, int):
        way = [(i, i ^ way) for i in range(lax.axis_size(axis))]
    return lax.ppermute(value, axis, way)


def after(value, *others):
    return lax.optimization_barrier((value, others))[0]


class Chain:
    def __init__(self, steps):
        self.steps, self.result, self.flying = steps, None, None
        self.advance(None)

    def advance(self, values):
        try:
            self.due = self.steps.send(values)
        except StopIteration as end:
            self.due, self.result = [], end.value


class Convoy:
    def __init__(self):
        self.landed, self.sent, self.done = (), (), ()

    def launch(self, *chains):
        for chain in chains:
            if chain.due:
                values = after([value for value, _, _ in chain.due], self.landed, self.sent)
                chain.flying = [
                    hop(value, axis, way) for value, (_, axis, way) in zip(values, chain.due)
                ]
                self.sent = (self.sent, values)

    def work(self, work, *operands):
        self.done = work(*after(operands, self.sent, self.landed))
        return self.done

    def land(self, *chains):
        chains = [chain for chain in chains if chain.flying is not None]
        came = after([chain.flying for chain in chains], self.done)
        self.landed, self.sent = (came, self.done), ()
        for chain, values in zip(chains, came):
            chain.flying = None
            chain.advance(values)

    def wave(self, chains, work=None, *operands):
        self.launch(*chains)
        result = None if work is None else self.work(work, *operands)
        self.land(*chains)
        return result

    def finish(self, chain):
        while chain.due:
            self.wave([chain])


def gather_steps(value, slots):
    count = lax.axis_size("blk")
    slots[0] = [value]
    if count != 8:
        bit = 1
        while bit < count:
            got = yield [(slots[slot][0], "blk", bit) for slot in range(bit)]
            slots.update({bit + slot: [part] for slot, part in enumerate(got)})
            bit *= 2
        return
    half = value.shape[0] // 16 * 8
    x_all, y_all, own_pair = yield [(value, "blk", way) for way in (2, 4, 1)]
    slots[1], slots[2], slots[4] = [own_pair], [x_all], [y_all]
    *slots[6], x_pair, y_pair = yield [
        (x_all[:half], "blk", 4),
        (y_all[half:], "blk", 2),
        (x_all, "blk", 1),
        (y_all, "blk", 1),
    ]
    slots[3], slots[5] = [x_pair], [y_pair]
    slots[7] = yield [(part, "blk", 1) for part in slots[6]]


def small_steps(value):
    for axis in ("head", "blk"):
        bit = 1
        while bit < lax.axis_size(axis):
            ways = [bit]
            if axis == "blk" and bit == 2 and lax.axis_size(axis) == 8:
                ways = [2, 4, 6]
            for got in (yield [(value, axis, way) for way in ways]):
                value = value + got
            bit *= 2 * len(ways)
    return value


def head_share(value, step=0):
    rows = value.shape[0] // lax.axis_size("head")
    return lax.dynamic_slice_in_dim(value, (lax.axis_index("head") ^ step) * rows, rows)


def head_steps(value, finish=None):
    count, mine = lax.axis_size("head"), lax.axis_index("head")
    got = yield [(head_share(value, step), "head", step) for step in range(1, count)]
    total = head_share(value)
    for part in got:
        total = total + part
    total = total if finish is None else finish(total)
    got = yield [(total, "head", step) for step in range(1, count)]
    whole = jnp.zeros_like(value)
    for step, part in enumerate([total, *got]):
        whole = lax.dynamic_update_slice_in_dim(whole, part, (mine ^ step) * part.shape[0], 0)
    return whole


def line_steps(value, pieces):
    if lax.axis_size("head") != 4:
        return (yield from head_steps(value))
    mine = lax.axis_index("head")
    inner = (mine == 1) | (mine == 2)
    parts = jnp.split(value, pieces)
    pairs, whole, done = {}, {}, {}
    for wave in range(pieces + 2):
        sends, takes = [], []
        if wave < pieces:
            sends.append((parts[wave], "head", [(0, 1), (3, 2)]))
            takes.append((pairs, wave, parts))
        if 0 <= wave - 1 < pieces:
            sends.append((pairs[wave - 1], "head", [(1, 2), (2, 1)]))
            takes.append((whole, wave - 1, pairs))
        if 0 <= wave - 2:
            sends.append((whole[wave - 2], "head", [(1, 0), (2, 3)]))
            takes.append((done, wave - 2, whole))
        got = yield sends
        for part, (into, piece, own) in zip(got, takes):
            if into is done:
                into[piece] = jnp.where(inner, own[piece], part)
            else:
                into[piece] = own[piece] + part
    return jnp.concatenate([done[piece] for piece in range(pieces)])


def sum_head(value):
    return lax.psum(value, "head")


def dot_t(left, right):
    return lax.dot_general(left, right, (((1,), (1,)), ((), ())), preferred_element_type=f32)


def dot_n(left, right):
    return lax.dot_general(left, right, (((1,), (0,)), ((), ())), preferred_element_type=f32)


def head_lanes(rows, width, first):
    lanes = lax.broadcasted_iota(jnp.int32, (rows, width), 1)
    return (lanes >= first) & (lanes < first + FEAT)


def read(slot, lines, lanes):
    parts = [ref[:, lanes] for ref in slot]
    whole = parts[0] if len(parts) == 1 else jnp.concatenate(parts)
    return whole if lines is None else whole[lines]


def split_refs(refs, shape):
    slots, at = [], 0
    for pieces in shape:
        slots.append(refs[at : at + pieces])
        at += pieces
    return slots, refs[at:]


def turned(tile, heads, use_key):
    rows, width = tile.shape
    moved = jnp.concatenate([tile[:, width // 2 :], tile[:, : width // 2]], axis=1)
    base = 0 if use_key else width // 2
    scaled = moved * 0.25
    return [
        jnp.where(head_lanes(rows, width, base + head * FEAT), scaled, 0.0).astype(bf16)
        for head in range(heads)
    ]


def attend_kernel(heads, shape, col_ref, row_ref, *refs):
    slots, (att_ref, mean_ref, inverse_ref) = split_refs(refs, shape)
    count = len(slots)
    rows = col_ref.shape[0]
    qk = heads * FEAT
    own_pos, own_doc = col_ref[:, 0:1], col_ref[:, 1:2]
    valid = col_ref[:, 2:3].astype(f32)
    numer = [jnp.zeros((rows, DV), f32) for _ in range(heads)]
    denom = [jnp.zeros((rows, 1), f32) for _ in range(heads)]
    queries = turned(read(slots[0], None, slice(0, 2 * qk)), heads, False)
    for slot in range(count):
        allowed = (row_ref[slot : slot + 1, :] <= own_pos) & (
            row_ref[count + slot : count + slot + 1, :] == own_doc
        )
        keys = read(slots[slot], None, slice(0, 2 * qk)).astype(bf16)
        for head in range(heads):
            near = 1.0 + dot_t(queries[head], keys)
            score = jnp.where(allowed, 0.5 * near * near + 0.5, 0.0)
            first = 2 * qk + head * DV
            value = read(slots[slot], None, slice(first, first + DV)).astype(bf16)
            numer[head] = numer[head] + dot_n(score.astype(bf16), value)
            denom[head] = denom[head] + jnp.sum(score, axis=1, keepdims=True)
    for head in range(heads):
        span = slice(head * DV, (head + 1) * DV)
        mean = numer[head] / denom[head]
        att_ref[:, span] = (valid * mean).astype(bf16)
        mean_ref[:, span] = mean
        inverse_ref[:, span] = jnp.broadcast_to(valid / denom[head], (rows, DV))


def query_kernel(heads, shape, col_ref, row_ref, numer_ref, denom_ref, *refs):
    slots, (out_ref,) = split_refs(refs, shape)
    count = len(slots)
    rows = col_ref.shape[0]
    qk = heads * FEAT
    own_pos, own_doc = col_ref[:, 0:1], col_ref[:, 1:2]
    queries = turned(read(slots[0], None, slice(0, 2 * qk)), heads, False)
    sums = [jnp.zeros((rows, 2 * qk), f32) for _ in range(heads)]
    for slot in range(count):
        allowed = (row_ref[slot : slot + 1, :] <= own_pos) & (
            row_ref[count + slot : count + slot + 1, :] == own_doc
        )
        keys = read(slots[slot], None, slice(0, 2 * qk)).astype(bf16)
        for head in range(heads):
            near = 1.0 + dot_t(queries[head], keys)
            first = 2 * qk + head * DV
            value = read(slots[slot], None, slice(first, first + DV)).astype(bf16)
            grad = dot_t(numer_ref[:, head * DV : (head + 1) * DV].astype(bf16), value)
            grad = grad + denom_ref[:, head * DV : head * DV + 1]
            grad = jnp.where(allowed, grad * near, 0.0).astype(bf16)
            sums[head] = sums[head] + dot_n(grad, keys)
    total = jnp.zeros((rows, 2 * qk), f32)
    for head in range(heads):
        total = jnp.where(head_lanes(rows, 2 * qk, qk + head * FEAT), 0.25 * sums[head], total)
    out_ref[...] = total[:, qk:].astype(bf16)


def key_kernel(heads, shape, grad_shape, col_ref, row_ref, *refs):
    slots, rest = split_refs(refs, shape)
    grads, (key_ref, value_ref) = split_refs(rest, grad_shape)
    count = len(slots)
    rows = col_ref.shape[0]
    qk, vw = heads * FEAT, heads * DV
    own_pos, own_doc = col_ref[:, 0:1], col_ref[:, 3:4]
    keys = turned(read(slots[0], None, slice(0, 2 * qk)), heads, True)
    values = [
        read(slots[0], None, slice(2 * qk + head * DV, 2 * qk + (head + 1) * DV)).astype(bf16)
        for head in range(heads)
    ]
    key_sums = [jnp.zeros((rows, 2 * qk), f32) for _ in range(heads)]
    value_sums = [jnp.zeros((rows, DV), f32) for _ in range(heads)]
    for slot in range(count):
        allowed = (row_ref[slot : slot + 1, :] >= own_pos) & (
            row_ref[2 * count + slot : 2 * count + slot + 1, :] == own_doc
        )
        queries = read(slots[slot], None, slice(0, 2 * qk)).astype(bf16)
        last = grads[slot][-1]
        extra = last.shape[0] - (rows - sum(ref.shape[0] for ref in grads[slot][:-1]))
        base = last.shape[0] - extra
        for head in range(heads):
            near = 1.0 + dot_t(keys[head], queries)
            span = slice(head * DV, (head + 1) * DV)
            numer = read(grads[slot], slice(0, rows), span).astype(bf16)
            line, lane = base + (head * rows) // vw, (head * rows) % vw
            grad = dot_t(values[head], numer) + last[line : line + 1, lane : lane + rows]
            grad = jnp.where(allowed, grad * near, 0.0).astype(bf16)
            key_sums[head] = key_sums[head] + dot_n(grad, queries)
            score = jnp.where(allowed, 0.5 * near * near + 0.5, 0.0).astype(bf16)
            value_sums[head] = value_sums[head] + dot_n(score, numer)
    total = jnp.zeros((rows, 2 * qk), f32)
    for head in range(heads):
        total = jnp.where(head_lanes(rows, 2 * qk, head * FEAT), 0.25 * key_sums[head], total)
        value_ref[:, head * DV : (head + 1) * DV] = value_sums[head].astype(bf16)
    key_ref[...] = total[:, :qk].astype(bf16)


def whole_call(body, outs, *operands, flops=0):
    moved = sum(x.size * x.dtype.itemsize for x in (*operands, *outs))
    return pl.pallas_call(
        body,
        out_shape=outs,
        in_specs=[pl.BlockSpec(memory_space=pltpu.VMEM)] * len(operands),
        out_specs=jax.tree.map(lambda _: pl.BlockSpec(memory_space=pltpu.VMEM), outs),
        compiler_params=pltpu.CompilerParams(vmem_limit_bytes=VMEM_LIMIT),
        cost_estimate=pl.CostEstimate(flops=flops, bytes_accessed=moved, transcendentals=0),
    )(*operands)


def join_kernel(shape, scale_ref, *refs):
    slots, (out_ref,) = split_refs(refs, shape)
    step = pl.program_id(0)
    for slot in range(len(slots)):

        @pl.when(step == slot)
        def _():
            at = 0
            for ref in slots[slot]:
                out_ref[at : at + ref.shape[0], :] = (ref[...] * scale_ref[...]).astype(bf16)
                at += ref.shape[0]


def join_rounded(slots, scale):
    parts = [part for slot in slots for part in slot]
    rows, width = sum(part.shape[0] for part in slots[0]), parts[0].shape[1]
    count = len(slots)
    return pl.pallas_call(
        functools.partial(join_kernel, tuple(len(slot) for slot in slots)),
        grid=(count,),
        out_shape=jax.ShapeDtypeStruct((count * rows, width), bf16),
        in_specs=[pl.BlockSpec((1, width), lambda i: (0, 0))]
        + [
            pl.BlockSpec(part.shape, lambda i: (0, 0), pipeline_mode=pl.Buffered(1))
            for part in parts
        ],
        out_specs=pl.BlockSpec((rows, width), lambda i: (i, 0)),
        compiler_params=pltpu.CompilerParams(vmem_limit_bytes=VMEM_LIMIT),
        cost_estimate=pl.CostEstimate(
            flops=0, bytes_accessed=6 * count * rows * width, transcendentals=0
        ),
    )(scale[None, :], *parts)


def norm_back(grad_out, values, inverse, gain):
    scaled = grad_out * gain
    return inverse * (
        scaled - values * inverse * inverse * jnp.mean(scaled * values, axis=-1, keepdims=True)
    )


def mm(left, right):
    return jnp.dot(left, right, preferred_element_type=f32)


def mm_t(left, right):
    return jnp.einsum("ac,bc->ab", left, right, preferred_element_type=f32)


def t_mm(left, right):
    return jnp.einsum("ca,cb->ab", left, right, preferred_element_type=f32)


def gated(gate, up_lin, hidden_grad):
    sigmoid = 0.5 + 0.5 * jnp.tanh(0.5 * gate)
    silu = gate * sigmoid
    return (
        (silu * up_lin).astype(bf16),
        (hidden_grad * up_lin * sigmoid * (1.0 + gate * (1.0 - sigmoid))).astype(bf16),
        (hidden_grad * silu).astype(bf16),
    )


def per_device(
    tokens,
    gain_attn,
    w_query,
    w_key,
    w_value,
    w_out,
    gain_mlp,
    w_gate,
    w_up,
    w_down,
    doc_lengths,
    cotangent,
):
    rows, width = tokens.shape
    heads = w_query.shape[1] // FEAT
    qk, vw = heads * FEAT, heads * DV
    blk_index, blk_count = lax.axis_index("blk"), lax.axis_size("blk")

    def layout(doc_lengths, cotangent):
        ends = [doc_lengths[0]]
        for doc in range(1, doc_lengths.shape[0]):
            ends.append(ends[-1] + doc_lengths[doc])

        def documents(positions):
            docs = sum((positions >= end).astype(jnp.int32) for end in ends[:-1])
            valid = positions < ends[-1]
            return docs, valid, jnp.where(valid, docs, -1)

        own_pos = blk_index * rows + jnp.arange(rows, dtype=jnp.int32)
        own_docs, own_valid, own_key_docs = documents(own_pos)
        columns = [own_pos, own_docs, own_valid.astype(jnp.int32), own_key_docs]
        slot_blocks = blk_index ^ jnp.arange(blk_count, dtype=jnp.int32)
        slot_pos = slot_blocks[:, None] * rows + jnp.arange(rows, dtype=jnp.int32)[None, :]
        slot_docs, _, slot_key_docs = documents(slot_pos)
        lines = jnp.concatenate([slot_pos, slot_key_docs, slot_docs])
        return jnp.stack(columns, axis=1), lines, cotangent.astype(f32)

    gain_one, gain_two = gain_attn.astype(f32), gain_mlp.astype(f32)
    token_wide = tokens.astype(f32)
    inv_in = lax.rsqrt(jnp.mean(token_wide * token_wide, axis=-1, keepdims=True) + epsilon)
    normed_in = (token_wide * inv_in * gain_one).astype(bf16)
    qkv_own = jnp.concatenate(
        [mm(normed_in, w_query), mm(normed_in, w_key), mm(normed_in, w_value)], axis=1
    )
    convoy = Convoy()
    qkv_slots = {}
    qkv_chain = Chain(gather_steps(qkv_own, qkv_slots))
    columns, lines, cot_wide = convoy.wave([qkv_chain], layout, doc_lengths, cotangent)
    convoy.finish(qkv_chain)
    qkv = [qkv_slots[slot] for slot in range(blk_count)]
    shape = tuple(len(slot) for slot in qkv)
    qkv_parts = [part for slot in qkv for part in slot]

    cost = 8 * rows * rows * blk_count * vw
    attended, mean, inverse = whole_call(
        functools.partial(attend_kernel, heads, shape),
        (
            jax.ShapeDtypeStruct((rows, vw), bf16),
            jax.ShapeDtypeStruct((rows, vw), f32),
            jax.ShapeDtypeStruct((rows, vw), f32),
        ),
        columns,
        lines,
        *qkv_parts,
        flops=cost,
    )
    attn_part = mm(attended, w_out)
    attn_sum = sum_head(attn_part)
    order = [0, 1, 2, 4, 3, 5, 6, 7] if blk_count == 8 else list(range(blk_count))
    early, late = order[: blk_count // 2], order[blk_count // 2 :]
    ones = jnp.ones_like(gain_two)

    def ready(chain, slots, wanted):
        while not all(slot in slots for slot in wanted):
            convoy.wave([chain])
        return [slots[slot] for slot in wanted]

    def cot_work(*slots):
        rows_of = join_rounded(slots, ones)
        return rows_of, mm_t(rows_of, w_down)

    def gate_work(*slots):
        rows_of = join_rounded(slots, gain_two)
        return rows_of, mm(rows_of, w_gate)

    def up_work(rows_of, gate, hidden_grad):
        return gated(gate, mm(rows_of, w_up), hidden_grad)

    cot_slots = {}
    cot = Chain(gather_steps(cot_wide, cot_slots))
    own_hidden_grad = convoy.wave(
        [cot], lambda left, _: mm_t(left, w_down), cotangent, attn_part
    )
    cot_early = ready(cot, cot_slots, early)
    convoy.launch(cot)
    cot_a, hidden_grad_a = convoy.work(cot_work, *cot_early)
    token_wide = after(tokens, attn_part).astype(f32)
    resid_mid = after(token_wide, convoy.done) + attn_sum
    inv_mid = lax.rsqrt(jnp.mean(resid_mid * resid_mid, axis=-1, keepdims=True) + epsilon)
    scaled_mid = resid_mid * inv_mid
    convoy.done = scaled_mid
    convoy.land(cot)
    mid_slots = {}
    mid = Chain(gather_steps(scaled_mid, mid_slots))

    def middle(scaled_mid):
        normed_mid = (scaled_mid * gain_two).astype(bf16)
        hidden, gate_lin_grad, up_lin_grad = gated(
            mm(normed_mid, w_gate), mm(normed_mid, w_up), own_hidden_grad
        )
        return hidden, mm_t(gate_lin_grad, w_gate) + mm_t(up_lin_grad, w_up)

    convoy.launch(mid, cot)
    hidden, mid_part = convoy.work(middle, scaled_mid)
    convoy.land(cot)
    mid_sum = sum_head(mid_part)

    def share_work(hidden, *slots):
        mlp_part = mm(hidden, w_down)
        return mlp_part, *cot_work(*after(slots, mlp_part))

    mlp_part, cot_b, hidden_grad_b = convoy.work(
        share_work, hidden, *ready(cot, cot_slots, late)
    )
    mlp = Chain(line_steps(mlp_part, 2))
    convoy.land(mid)
    mid_early = ready(mid, mid_slots, early)
    convoy.launch(mid)
    mid_a, gate_a = convoy.work(gate_work, *mid_early)
    hidden_a, gate_grad_a, up_grad_a = convoy.work(
        up_work, after(mid_a, convoy.done), gate_a, hidden_grad_a
    )
    down_a = convoy.work(t_mm, after(hidden_a, convoy.done), cot_a)
    mid_grad = after(mid_sum, down_a)

    resid_grad = cot_wide + norm_back(mid_grad, resid_mid, inv_mid, gain_two)
    out_lin_grad = resid_grad.astype(bf16)
    attended_grad = mm_t(out_lin_grad, w_out)
    numer_grad = attended_grad * inverse
    denom_grad = -jnp.sum((numer_grad * mean).reshape(rows, heads, DV), axis=-1)
    denom_lines = denom_grad.T.reshape(rows // DV, vw)
    denom_lines = jnp.pad(denom_lines, ((0, -denom_lines.shape[0] % 8), (0, 0)))
    sent = jnp.concatenate([numer_grad, denom_lines])
    convoy.done = sent
    convoy.land(mid)
    grad_slots = {}
    grads = Chain(gather_steps(sent, grad_slots))

    def query_work(numer_grad, denom_grad):
        (query_lin_grad,) = whole_call(
            functools.partial(query_kernel, heads, shape),
            (jax.ShapeDtypeStruct((rows, qk), bf16),),
            columns,
            lines,
            numer_grad,
            jnp.repeat(denom_grad, DV, axis=1),
            *qkv_parts,
            flops=cost,
        )
        return query_lin_grad

    convoy.launch(grads, mlp)
    query_lin_grad = convoy.work(query_work, numer_grad, denom_grad)
    convoy.land(grads)
    out_part = convoy.wave([grads], t_mm, attended, out_lin_grad)
    convoy.launch(grads)
    convoy.land(grads, mlp)
    convoy.finish(grads)
    grad_slots = [grad_slots[slot] for slot in range(blk_count)]
    grad_shape = tuple(len(slot) for slot in grad_slots)

    def key_work(query_lin_grad, grad_parts):
        key_lin_grad, value_grad = whole_call(
            functools.partial(key_kernel, heads, shape, grad_shape),
            (jax.ShapeDtypeStruct((rows, qk), bf16), jax.ShapeDtypeStruct((rows, vw), bf16)),
            columns,
            lines,
            *qkv_parts,
            *grad_parts,
            flops=2 * cost,
        )
        lin_grads = (query_lin_grad, key_lin_grad, value_grad)
        parts = [t_mm(normed_in, grad) for grad in lin_grads]
        query_lin_grad, key_lin_grad, value_grad = after(lin_grads, parts)
        in_part = mm_t(query_lin_grad, w_query) + mm_t(key_lin_grad, w_key)
        return in_part + mm_t(value_grad, w_value), parts

    grad_parts = [part for slot in grad_slots for part in slot]
    convoy.launch(mid, mlp)
    in_part, parts = convoy.work(key_work, query_lin_grad, grad_parts)
    *qkv_w_grads, out_w_grad = lax.psum((*parts, out_part), "blk")
    convoy.land(mid)
    mid_late = ready(mid, mid_slots, late)

    in_sum = Chain(line_steps(in_part, 2))
    convoy.launch(in_sum)

    gain_parts = jnp.stack(
        [
            jnp.sum(after(in_part, convoy.sent) * token_wide * inv_in, axis=0),
            jnp.sum(mid_part * scaled_mid, axis=0),
        ]
    )
    convoy.done = gain_parts
    convoy.land(mlp)
    gains = Chain(small_steps(gain_parts))
    convoy.launch(mlp, gains)
    chains = [in_sum, gains, mlp]
    mid_b, gate_b = convoy.work(gate_work, *mid_late)
    convoy.land(*chains)

    def second_work(mid_b, gate_b, hidden_grad_b):
        parts = up_work(mid_b, gate_b, hidden_grad_b)
        return (*parts, t_mm(mid_a, after(up_grad_a, parts)))

    hidden_b, gate_grad_b, up_grad_b, up_part = convoy.wave(
        chains, second_work, mid_b, gate_b, hidden_grad_b
    )

    def third_work(hidden_b, gate_grad_a):
        down_w_grad = down_a + t_mm(hidden_b, cot_b)
        return down_w_grad, t_mm(mid_a, after(gate_grad_a, down_w_grad))

    down_w_grad, gate_part = convoy.wave(chains, third_work, hidden_b, gate_grad_a)
    convoy.finish(mlp)

    def gate_last(gate_grad_b, mlp_sum):
        output = (resid_mid + mlp_sum).astype(bf16)
        return gate_part + t_mm(mid_b, after(gate_grad_b, output)), output

    chains = [in_sum, gains]
    convoy.launch(*chains)
    gate_w_grad, output = convoy.work(gate_last, gate_grad_b, mlp.result)
    up_w_grad = convoy.work(
        lambda x: up_part + t_mm(mid_b, x), after(up_grad_b, gate_w_grad)
    )
    convoy.land(*chains)
    while any(chain.due for chain in chains):
        convoy.wave(chains)
    in_grad, gain_grads = (chain.result for chain in chains)
    gain_grads = after(gain_grads, qkv_w_grads, out_w_grad)
    input_grad = resid_grad + norm_back(in_grad, token_wide, inv_in, gain_one)
    return (
        output,
        input_grad,
        gain_grads[0],
        *qkv_w_grads,
        out_w_grad,
        gain_grads[1],
        gate_w_grad,
        up_w_grad,
        down_w_grad,
    )


def solution(mesh):
    in_specs = (
        P("blk", None),
        P(),
        P(None, "head"),
        P(None, "head"),
        P(None, "head"),
        P("head", None),
        P(),
        P(None, "head"),
        P(None, "head"),
        P("head", None),
        P(),
        P("blk", None),
    )
    out_specs = (
        P("blk", None),
        P("blk", None),
        P(),
        P(None, "head"),
        P(None, "head"),
        P(None, "head"),
        P("head", None),
        P(),
        P(None, "head"),
        P(None, "head"),
        P("head", None),
    )
    return jax.shard_map(
        per_device, mesh=mesh, in_specs=in_specs, out_specs=out_specs, check_vma=False
    )
```

```python
import functools

import jax
import jax.numpy as jnp
from jax import lax
from jax.experimental import pallas as pl
from jax.experimental.pallas import tpu as pltpu
from jax.sharding import PartitionSpec as P

FEAT = 16
DV = 128

epsilon = 1e-05
f32, bf16 = jnp.float32, jnp.bfloat16
VMEM_LIMIT = 56 * 1024 * 1024


def hop(value, axis, way):
    if isinstance(way, int):
        way = [(i, i ^ way) for i in range(lax.axis_size(axis))]
    return lax.ppermute(value, axis, way)


def after(value, *others):
    return lax.optimization_barrier((value, others))[0]


class Chain:
    def __init__(self, steps):
        self.steps, self.result, self.flying = steps, None, None
        self.advance(None)

    def advance(self, values):
        try:
            self.due = self.steps.send(values)
        except StopIteration as end:
            self.due, self.result = [], end.value


class Convoy:
    def __init__(self):
        self.landed, self.sent, self.done = (), (), ()

    def launch(self, *chains):
        for chain in chains:
            if chain.due:
                values = after([value for value, _, _ in chain.due], self.landed, self.sent)
                chain.flying = [
                    hop(value, axis, way) for value, (_, axis, way) in zip(values, chain.due)
                ]
                self.sent = (self.sent, values)

    def work(self, work, *operands):
        self.done = work(*after(operands, self.sent, self.landed))
        return self.done

    def land(self, *chains):
        chains = [chain for chain in chains if chain.flying is not None]
        came = after([chain.flying for chain in chains], self.done)
        self.landed, self.sent = (came, self.done), ()
        for chain, values in zip(chains, came):
            chain.flying = None
            chain.advance(values)

    def wave(self, chains, work=None, *operands):
        self.launch(*chains)
        result = None if work is None else self.work(work, *operands)
        self.land(*chains)
        return result

    def finish(self, chain):
        while chain.due:
            self.wave([chain])


def gather_steps(value, slots):
    count = lax.axis_size("blk")
    slots[0] = [value]
    if count != 8:
        bit = 1
        while bit < count:
            got = yield [(slots[slot][0], "blk", bit) for slot in range(bit)]
            slots.update({bit + slot: [part] for slot, part in enumerate(got)})
            bit *= 2
        return
    half = value.shape[0] // 16 * 8
    x_all, y_all, own_pair = yield [(value, "blk", way) for way in (2, 4, 1)]
    slots[1], slots[2], slots[4] = [own_pair], [x_all], [y_all]
    *slots[6], x_pair, y_pair = yield [
        (x_all[:half], "blk", 4),
        (y_all[half:], "blk", 2),
        (x_all, "blk", 1),
        (y_all, "blk", 1),
    ]
    slots[3], slots[5] = [x_pair], [y_pair]
    slots[7] = yield [(part, "blk", 1) for part in slots[6]]


def small_steps(value):
    for axis in ("head", "blk"):
        bit = 1
        while bit < lax.axis_size(axis):
            ways = [bit]
            if axis == "blk" and bit == 2 and lax.axis_size(axis) == 8:
                ways = [2, 4, 6]
            for got in (yield [(value, axis, way) for way in ways]):
                value = value + got
            bit *= 2 * len(ways)
    return value


def head_share(value, step=0):
    rows = value.shape[0] // lax.axis_size("head")
    return lax.dynamic_slice_in_dim(value, (lax.axis_index("head") ^ step) * rows, rows)


def head_steps(value, finish=None):
    count, mine = lax.axis_size("head"), lax.axis_index("head")
    got = yield [(head_share(value, step), "head", step) for step in range(1, count)]
    total = head_share(value)
    for part in got:
        total = total + part
    total = total if finish is None else finish(total)
    got = yield [(total, "head", step) for step in range(1, count)]
    whole = jnp.zeros_like(value)
    for step, part in enumerate([total, *got]):
        whole = lax.dynamic_update_slice_in_dim(whole, part, (mine ^ step) * part.shape[0], 0)
    return whole


def line_steps(value, pieces):
    if lax.axis_size("head") != 4:
        return (yield from head_steps(value))
    mine = lax.axis_index("head")
    inner = (mine == 1) | (mine == 2)
    parts = jnp.split(value, pieces)
    pairs, whole, done = {}, {}, {}
    for wave in range(pieces + 2):
        sends, takes = [], []
        if wave < pieces:
            sends.append((parts[wave], "head", [(0, 1), (3, 2)]))
            takes.append((pairs, wave, parts))
        if 0 <= wave - 1 < pieces:
            sends.append((pairs[wave - 1], "head", [(1, 2), (2, 1)]))
            takes.append((whole, wave - 1, pairs))
        if 0 <= wave - 2:
            sends.append((whole[wave - 2], "head", [(1, 0), (2, 3)]))
            takes.append((done, wave - 2, whole))
        got = yield sends
        for part, (into, piece, own) in zip(got, takes):
            if into is done:
                into[piece] = jnp.where(inner, own[piece], part)
            else:
                into[piece] = own[piece] + part
    return jnp.concatenate([done[piece] for piece in range(pieces)])


def sum_head(value):
    return lax.psum(value, "head")


def dot_t(left, right):
    return lax.dot_general(left, right, (((1,), (1,)), ((), ())), preferred_element_type=f32)


def dot_n(left, right):
    return lax.dot_general(left, right, (((1,), (0,)), ((), ())), preferred_element_type=f32)


def head_lanes(rows, width, first):
    lanes = lax.broadcasted_iota(jnp.int32, (rows, width), 1)
    return (lanes >= first) & (lanes < first + FEAT)


def read(slot, lines, lanes):
    parts = [ref[:, lanes] for ref in slot]
    whole = parts[0] if len(parts) == 1 else jnp.concatenate(parts)
    return whole if lines is None else whole[lines]


def split_refs(refs, shape):
    slots, at = [], 0
    for pieces in shape:
        slots.append(refs[at : at + pieces])
        at += pieces
    return slots, refs[at:]


def turned(tile, heads, use_key):
    rows, width = tile.shape
    moved = jnp.concatenate([tile[:, width // 2 :], tile[:, : width // 2]], axis=1)
    base = 0 if use_key else width // 2
    scaled = moved * 0.25
    return [
        jnp.where(head_lanes(rows, width, base + head * FEAT), scaled, 0.0).astype(bf16)
        for head in range(heads)
    ]


def attend_kernel(heads, shape, col_ref, row_ref, *refs):
    slots, (att_ref, mean_ref, inverse_ref) = split_refs(refs, shape)
    count = len(slots)
    rows = col_ref.shape[0]
    qk = heads * FEAT
    own_pos, own_doc = col_ref[:, 0:1], col_ref[:, 1:2]
    valid = col_ref[:, 2:3].astype(f32)
    numer = [jnp.zeros((rows, DV), f32) for _ in range(heads)]
    denom = [jnp.zeros((rows, 1), f32) for _ in range(heads)]
    queries = turned(read(slots[0], None, slice(0, 2 * qk)), heads, False)
    for slot in range(count):
        allowed = (row_ref[slot : slot + 1, :] <= own_pos) & (
            row_ref[count + slot : count + slot + 1, :] == own_doc
        )
        keys = read(slots[slot], None, slice(0, 2 * qk)).astype(bf16)
        for head in range(heads):
            near = 1.0 + dot_t(queries[head], keys)
            score = jnp.where(allowed, 0.5 * near * near + 0.5, 0.0)
            first = 2 * qk + head * DV
            value = read(slots[slot], None, slice(first, first + DV)).astype(bf16)
            numer[head] = numer[head] + dot_n(score.astype(bf16), value)
            denom[head] = denom[head] + jnp.sum(score, axis=1, keepdims=True)
    for head in range(heads):
        span = slice(head * DV, (head + 1) * DV)
        mean = numer[head] / denom[head]
        att_ref[:, span] = (valid * mean).astype(bf16)
        mean_ref[:, span] = mean
        inverse_ref[:, span] = jnp.broadcast_to(valid / denom[head], (rows, DV))


def share_kernel(heads, grad_ref, inverse_ref, mean_ref, sent_ref, denom_ref):
    rows = grad_ref.shape[0]
    vw = heads * DV
    sent_ref[rows:, :] = jnp.zeros((sent_ref.shape[0] - rows, vw), f32)
    for head in range(heads):
        span = slice(head * DV, (head + 1) * DV)
        numer = grad_ref[:, span] * inverse_ref[:, span]
        sent_ref[:rows, span] = numer
        product = numer * mean_ref[:, span]
        denom_ref[:, span] = jnp.broadcast_to(
            -jnp.sum(product, axis=1, keepdims=True), (rows, DV)
        )
        line, lane = rows + (head * rows) // vw, (head * rows) % vw
        sent_ref[line : line + 1, lane : lane + rows] = -jnp.sum(product.T, axis=0, keepdims=True)


def query_kernel(heads, shape, col_ref, row_ref, numer_ref, denom_ref, *refs):
    slots, (out_ref,) = split_refs(refs, shape)
    count = len(slots)
    rows = col_ref.shape[0]
    qk = heads * FEAT
    own_pos, own_doc = col_ref[:, 0:1], col_ref[:, 1:2]
    queries = turned(read(slots[0], None, slice(0, 2 * qk)), heads, False)
    sums = [jnp.zeros((rows, 2 * qk), f32) for _ in range(heads)]
    for slot in range(count):
        allowed = (row_ref[slot : slot + 1, :] <= own_pos) & (
            row_ref[count + slot : count + slot + 1, :] == own_doc
        )
        keys = read(slots[slot], None, slice(0, 2 * qk)).astype(bf16)
        for head in range(heads):
            near = 1.0 + dot_t(queries[head], keys)
            first = 2 * qk + head * DV
            value = read(slots[slot], None, slice(first, first + DV)).astype(bf16)
            grad = dot_t(numer_ref[:rows, head * DV : (head + 1) * DV].astype(bf16), value)
            grad = grad + denom_ref[:, head * DV : head * DV + 1]
            grad = jnp.where(allowed, grad * near, 0.0).astype(bf16)
            sums[head] = sums[head] + dot_n(grad, keys)
    total = jnp.zeros((rows, 2 * qk), f32)
    for head in range(heads):
        total = jnp.where(head_lanes(rows, 2 * qk, qk + head * FEAT), 0.25 * sums[head], total)
    out_ref[...] = total[:, qk:].astype(bf16)


def key_kernel(heads, shape, grad_shape, col_ref, row_ref, *refs):
    slots, rest = split_refs(refs, shape)
    grads, (key_ref, value_ref) = split_refs(rest, grad_shape)
    count = len(slots)
    rows = col_ref.shape[0]
    qk, vw = heads * FEAT, heads * DV
    own_pos, own_doc = col_ref[:, 0:1], col_ref[:, 3:4]
    keys = turned(read(slots[0], None, slice(0, 2 * qk)), heads, True)
    values = [
        read(slots[0], None, slice(2 * qk + head * DV, 2 * qk + (head + 1) * DV)).astype(bf16)
        for head in range(heads)
    ]
    key_sums = [jnp.zeros((rows, 2 * qk), f32) for _ in range(heads)]
    value_sums = [jnp.zeros((rows, DV), f32) for _ in range(heads)]
    for slot in range(count):
        allowed = (row_ref[slot : slot + 1, :] >= own_pos) & (
            row_ref[2 * count + slot : 2 * count + slot + 1, :] == own_doc
        )
        queries = read(slots[slot], None, slice(0, 2 * qk)).astype(bf16)
        last = grads[slot][-1]
        extra = last.shape[0] - (rows - sum(ref.shape[0] for ref in grads[slot][:-1]))
        base = last.shape[0] - extra
        for head in range(heads):
            near = 1.0 + dot_t(keys[head], queries)
            span = slice(head * DV, (head + 1) * DV)
            numer = read(grads[slot], slice(0, rows), span).astype(bf16)
            line, lane = base + (head * rows) // vw, (head * rows) % vw
            grad = dot_t(values[head], numer) + last[line : line + 1, lane : lane + rows]
            grad = jnp.where(allowed, grad * near, 0.0).astype(bf16)
            key_sums[head] = key_sums[head] + dot_n(grad, queries)
            score = jnp.where(allowed, 0.5 * near * near + 0.5, 0.0).astype(bf16)
            value_sums[head] = value_sums[head] + dot_n(score, numer)
    total = jnp.zeros((rows, 2 * qk), f32)
    for head in range(heads):
        total = jnp.where(head_lanes(rows, 2 * qk, head * FEAT), 0.25 * key_sums[head], total)
        value_ref[:, head * DV : (head + 1) * DV] = value_sums[head].astype(bf16)
    key_ref[...] = total[:, :qk].astype(bf16)


def whole_call(body, outs, *operands, flops=0):
    moved = sum(x.size * x.dtype.itemsize for x in (*operands, *outs))
    return pl.pallas_call(
        body,
        out_shape=outs,
        in_specs=[pl.BlockSpec(memory_space=pltpu.VMEM)] * len(operands),
        out_specs=jax.tree.map(lambda _: pl.BlockSpec(memory_space=pltpu.VMEM), outs),
        compiler_params=pltpu.CompilerParams(vmem_limit_bytes=VMEM_LIMIT),
        cost_estimate=pl.CostEstimate(flops=flops, bytes_accessed=moved, transcendentals=0),
    )(*operands)


def join_kernel(shape, scale_ref, *refs):
    slots, (out_ref,) = split_refs(refs, shape)
    step = pl.program_id(0)
    for slot in range(len(slots)):

        @pl.when(step == slot)
        def _():
            at = 0
            for ref in slots[slot]:
                out_ref[at : at + ref.shape[0], :] = (ref[...] * scale_ref[...]).astype(bf16)
                at += ref.shape[0]


def join_rounded(slots, scale):
    parts = [part for slot in slots for part in slot]
    rows, width = sum(part.shape[0] for part in slots[0]), parts[0].shape[1]
    count = len(slots)
    return pl.pallas_call(
        functools.partial(join_kernel, tuple(len(slot) for slot in slots)),
        grid=(count,),
        out_shape=jax.ShapeDtypeStruct((count * rows, width), bf16),
        in_specs=[pl.BlockSpec((1, width), lambda i: (0, 0))]
        + [
            pl.BlockSpec(part.shape, lambda i: (0, 0), pipeline_mode=pl.Buffered(1))
            for part in parts
        ],
        out_specs=pl.BlockSpec((rows, width), lambda i: (i, 0)),
        compiler_params=pltpu.CompilerParams(vmem_limit_bytes=VMEM_LIMIT),
        cost_estimate=pl.CostEstimate(
            flops=0, bytes_accessed=6 * count * rows * width, transcendentals=0
        ),
    )(scale[None, :], *parts)


def norm_back(grad_out, values, inverse, gain):
    scaled = grad_out * gain
    return inverse * (
        scaled - values * inverse * inverse * jnp.mean(scaled * values, axis=-1, keepdims=True)
    )


def mm(left, right):
    return jnp.dot(left, right, preferred_element_type=f32)


def mm_t(left, right):
    return jnp.einsum("ac,bc->ab", left, right, preferred_element_type=f32)


def t_mm(left, right):
    return jnp.einsum("ca,cb->ab", left, right, preferred_element_type=f32)


def gated(gate, up_lin, hidden_grad):
    sigmoid = 0.5 + 0.5 * jnp.tanh(0.5 * gate)
    silu = gate * sigmoid
    return (
        (silu * up_lin).astype(bf16),
        (hidden_grad * up_lin * sigmoid * (1.0 + gate * (1.0 - sigmoid))).astype(bf16),
        (hidden_grad * silu).astype(bf16),
    )


def per_device(
    tokens,
    gain_attn,
    w_query,
    w_key,
    w_value,
    w_out,
    gain_mlp,
    w_gate,
    w_up,
    w_down,
    doc_lengths,
    cotangent,
):
    rows, width = tokens.shape
    heads = w_query.shape[1] // FEAT
    qk, vw = heads * FEAT, heads * DV
    blk_index, blk_count = lax.axis_index("blk"), lax.axis_size("blk")

    def layout(doc_lengths, cotangent):
        ends = [doc_lengths[0]]
        for doc in range(1, doc_lengths.shape[0]):
            ends.append(ends[-1] + doc_lengths[doc])

        def documents(positions):
            docs = sum((positions >= end).astype(jnp.int32) for end in ends[:-1])
            valid = positions < ends[-1]
            return docs, valid, jnp.where(valid, docs, -1)

        own_pos = blk_index * rows + jnp.arange(rows, dtype=jnp.int32)
        own_docs, own_valid, own_key_docs = documents(own_pos)
        columns = [own_pos, own_docs, own_valid.astype(jnp.int32), own_key_docs]
        slot_blocks = blk_index ^ jnp.arange(blk_count, dtype=jnp.int32)
        slot_pos = slot_blocks[:, None] * rows + jnp.arange(rows, dtype=jnp.int32)[None, :]
        slot_docs, _, slot_key_docs = documents(slot_pos)
        lines = jnp.concatenate([slot_pos, slot_key_docs, slot_docs])
        return jnp.stack(columns, axis=1), lines, cotangent.astype(f32)

    gain_one, gain_two = gain_attn.astype(f32), gain_mlp.astype(f32)
    token_wide = tokens.astype(f32)
    inv_in = lax.rsqrt(jnp.mean(token_wide * token_wide, axis=-1, keepdims=True) + epsilon)
    normed_in = (token_wide * inv_in * gain_one).astype(bf16)
    qkv_own = jnp.concatenate(
        [mm(normed_in, w_query), mm(normed_in, w_key), mm(normed_in, w_value)], axis=1
    )
    convoy = Convoy()
    qkv_slots = {}
    qkv_chain = Chain(gather_steps(qkv_own, qkv_slots))
    columns, lines, cot_wide = convoy.wave([qkv_chain], layout, doc_lengths, cotangent)
    convoy.finish(qkv_chain)
    qkv = [qkv_slots[slot] for slot in range(blk_count)]
    shape = tuple(len(slot) for slot in qkv)
    qkv_parts = [part for slot in qkv for part in slot]

    cost = 8 * rows * rows * blk_count * vw
    attended, mean, inverse = whole_call(
        functools.partial(attend_kernel, heads, shape),
        (
            jax.ShapeDtypeStruct((rows, vw), bf16),
            jax.ShapeDtypeStruct((rows, vw), f32),
            jax.ShapeDtypeStruct((rows, vw), f32),
        ),
        columns,
        lines,
        *qkv_parts,
        flops=cost,
    )
    attn_part = mm(attended, w_out)
    attn_sum = sum_head(attn_part)
    order = [0, 1, 2, 4, 3, 5, 6, 7] if blk_count == 8 else list(range(blk_count))
    early, late = order[: blk_count // 2], order[blk_count // 2 :]
    ones = jnp.ones_like(gain_two)

    def ready(chain, slots, wanted):
        while not all(slot in slots for slot in wanted):
            convoy.wave([chain])
        return [slots[slot] for slot in wanted]

    def cot_work(*slots):
        rows_of = join_rounded(slots, ones)
        return rows_of, mm_t(rows_of, w_down)

    def gate_work(*slots):
        rows_of = join_rounded(slots, gain_two)
        return rows_of, mm(rows_of, w_gate)

    def up_work(rows_of, gate, hidden_grad):
        return gated(gate, mm(rows_of, w_up), hidden_grad)

    cot_slots = {}
    cot = Chain(gather_steps(cot_wide, cot_slots))
    own_hidden_grad = convoy.wave(
        [cot], lambda left, _: mm_t(left, w_down), cotangent, attn_part
    )
    cot_early = ready(cot, cot_slots, early)
    convoy.launch(cot)
    cot_a, hidden_grad_a = convoy.work(cot_work, *cot_early)
    token_wide = after(tokens, attn_part).astype(f32)
    resid_mid = after(token_wide, convoy.done) + attn_sum
    inv_mid = lax.rsqrt(jnp.mean(resid_mid * resid_mid, axis=-1, keepdims=True) + epsilon)
    scaled_mid = resid_mid * inv_mid
    convoy.done = scaled_mid
    convoy.land(cot)
    mid_slots = {}
    mid = Chain(gather_steps(scaled_mid, mid_slots))

    def middle(scaled_mid):
        normed_mid = (scaled_mid * gain_two).astype(bf16)
        hidden, gate_lin_grad, up_lin_grad = gated(
            mm(normed_mid, w_gate), mm(normed_mid, w_up), own_hidden_grad
        )
        return hidden, mm_t(gate_lin_grad, w_gate) + mm_t(up_lin_grad, w_up)

    convoy.launch(mid, cot)
    hidden, mid_part = convoy.work(middle, scaled_mid)
    convoy.land(cot)
    mid_sum = sum_head(mid_part)

    def share_work(hidden, *slots):
        mlp_part = mm(hidden, w_down)
        return mlp_part, *cot_work(*after(slots, mlp_part))

    mlp_part, cot_b, hidden_grad_b = convoy.work(
        share_work, hidden, *ready(cot, cot_slots, late)
    )
    mlp = Chain(line_steps(mlp_part, 2))
    convoy.land(mid)
    mid_early = ready(mid, mid_slots, early)
    convoy.launch(mid)
    mid_a, gate_a = convoy.work(gate_work, *mid_early)
    hidden_a, gate_grad_a, up_grad_a = convoy.work(
        up_work, after(mid_a, convoy.done), gate_a, hidden_grad_a
    )
    down_a = convoy.work(t_mm, after(hidden_a, convoy.done), cot_a)
    mid_grad = after(mid_sum, down_a)

    resid_grad = cot_wide + norm_back(mid_grad, resid_mid, inv_mid, gain_two)
    out_lin_grad = resid_grad.astype(bf16)
    attended_grad = mm_t(out_lin_grad, w_out)
    extra = -(-rows // DV // 8) * 8
    sent, denom_grad = whole_call(
        functools.partial(share_kernel, heads),
        (
            jax.ShapeDtypeStruct((rows + extra, vw), f32),
            jax.ShapeDtypeStruct((rows, vw), f32),
        ),
        attended_grad,
        inverse,
        mean,
    )
    convoy.done = sent
    convoy.land(mid)
    grad_slots = {}
    grads = Chain(gather_steps(sent, grad_slots))

    def query_work(sent, denom_grad):
        (query_lin_grad,) = whole_call(
            functools.partial(query_kernel, heads, shape),
            (jax.ShapeDtypeStruct((rows, qk), bf16),),
            columns,
            lines,
            sent,
            denom_grad,
            *qkv_parts,
            flops=cost,
        )
        return query_lin_grad

    convoy.launch(grads, mlp)
    query_lin_grad = convoy.work(query_work, sent, denom_grad)
    convoy.land(grads)
    out_part = convoy.wave([grads], t_mm, attended, out_lin_grad)
    convoy.launch(grads)
    convoy.land(grads, mlp)
    convoy.finish(grads)
    grad_slots = [grad_slots[slot] for slot in range(blk_count)]
    grad_shape = tuple(len(slot) for slot in grad_slots)

    def key_work(query_lin_grad, grad_parts):
        key_lin_grad, value_grad = whole_call(
            functools.partial(key_kernel, heads, shape, grad_shape),
            (jax.ShapeDtypeStruct((rows, qk), bf16), jax.ShapeDtypeStruct((rows, vw), bf16)),
            columns,
            lines,
            *qkv_parts,
            *grad_parts,
            flops=2 * cost,
        )
        lin_grads = (query_lin_grad, key_lin_grad, value_grad)
        parts = [t_mm(normed_in, grad) for grad in lin_grads]
        query_lin_grad, key_lin_grad, value_grad = after(lin_grads, parts)
        in_part = mm_t(query_lin_grad, w_query) + mm_t(key_lin_grad, w_key)
        return in_part + mm_t(value_grad, w_value), parts

    grad_parts = [part for slot in grad_slots for part in slot]
    convoy.launch(mid, mlp)
    in_part, parts = convoy.work(key_work, query_lin_grad, grad_parts)
    *qkv_w_grads, out_w_grad = lax.psum((*parts, out_part), "blk")
    convoy.land(mid)
    mid_late = ready(mid, mid_slots, late)

    in_sum = Chain(line_steps(in_part, 2))
    convoy.launch(in_sum)

    gain_parts = jnp.stack(
        [
            jnp.sum(after(in_part, convoy.sent) * token_wide * inv_in, axis=0),
            jnp.sum(mid_part * scaled_mid, axis=0),
        ]
    )
    convoy.done = gain_parts
    convoy.land(mlp)
    gains = Chain(small_steps(gain_parts))
    convoy.launch(mlp, gains)
    chains = [in_sum, gains, mlp]
    mid_b, gate_b = convoy.work(gate_work, *mid_late)
    convoy.land(*chains)

    def second_work(mid_b, gate_b, hidden_grad_b):
        parts = up_work(mid_b, gate_b, hidden_grad_b)
        return (*parts, t_mm(mid_a, after(up_grad_a, parts)))

    hidden_b, gate_grad_b, up_grad_b, up_part = convoy.wave(
        chains, second_work, mid_b, gate_b, hidden_grad_b
    )

    def third_work(hidden_b, gate_grad_a):
        down_w_grad = down_a + t_mm(hidden_b, cot_b)
        return down_w_grad, t_mm(mid_a, after(gate_grad_a, down_w_grad))

    down_w_grad, gate_part = convoy.wave(chains, third_work, hidden_b, gate_grad_a)
    convoy.finish(mlp)

    def gate_last(gate_grad_b, mlp_sum):
        output = (resid_mid + mlp_sum).astype(bf16)
        return gate_part + t_mm(mid_b, after(gate_grad_b, output)), output

    chains = [in_sum, gains]
    convoy.launch(*chains)
    gate_w_grad, output = convoy.work(gate_last, gate_grad_b, mlp.result)
    up_w_grad = convoy.work(
        lambda x: up_part + t_mm(mid_b, x), after(up_grad_b, gate_w_grad)
    )
    convoy.land(*chains)
    while any(chain.due for chain in chains):
        convoy.wave(chains)
    in_grad, gain_grads = (chain.result for chain in chains)
    gain_grads = after(gain_grads, qkv_w_grads, out_w_grad)
    input_grad = resid_grad + norm_back(in_grad, token_wide, inv_in, gain_one)
    return (
        output,
        input_grad,
        gain_grads[0],
        *qkv_w_grads,
        out_w_grad,
        gain_grads[1],
        gate_w_grad,
        up_w_grad,
        down_w_grad,
    )


def solution(mesh):
    in_specs = (
        P("blk", None),
        P(),
        P(None, "head"),
        P(None, "head"),
        P(None, "head"),
        P("head", None),
        P(),
        P(None, "head"),
        P(None, "head"),
        P("head", None),
        P(),
        P("blk", None),
    )
    out_specs = (
        P("blk", None),
        P("blk", None),
        P(),
        P(None, "head"),
        P(None, "head"),
        P(None, "head"),
        P("head", None),
        P(),
        P(None, "head"),
        P(None, "head"),
        P("head", None),
    )
    return jax.shard_map(
        per_device, mesh=mesh, in_specs=in_specs, out_specs=out_specs, check_vma=False
    )
```
